32 devices in a mesh: dp: 8 (over z, x), fsdp: 4 (over y, core).
Axes of the slice: x: 2, y: 2, z: 4, core: 2. Of those that a mesh axis runs over, the one named last changes fastest.
Arguments:
- tokens: bfloat16 [8, 2048, 960], P('dp', 'fsdp'), may hold values from -6 to 6
- seq_cuts: int32 [8, 3], P('dp'), may hold values from 0 to 2048, as said below
- w_query: bfloat16 [960, 960], P('fsdp'), may hold values from -0.1875 to 0.1875
- w_key: bfloat16 [960, 320], P('fsdp'), may hold values from -0.1875 to 0.1875
- w_value: bfloat16 [960, 320], P('fsdp'), may hold values from -0.1875 to 0.1875
- w_output: bfloat16 [960, 960], P('fsdp'), may hold values from -1.5 to 1.5
- w_gate: bfloat16 [960, 2560], P('fsdp'), may hold values from -0.1875 to 0.1875
- w_up: bfloat16 [960, 2560], P('fsdp'), may hold values from -0.1875 to 0.1875
- w_down: bfloat16 [2560, 960], P('fsdp'), may hold values from -0.15625 to 0.15625
- gain_attn: float32 [960], replicated, may hold values from 0.5 to 1.5
- gain_ffn: float32 [960], replicated, may hold values from 0.5 to 1.5
- cotangent: bfloat16 [8, 2048, 960], P('dp', 'fsdp'), may hold values from -6 to 6
Outputs:
- output: bfloat16 [8, 2048, 960], P('dp', 'fsdp')
- grad_tokens: bfloat16 [8, 2048, 960], P('dp', 'fsdp')
- grad_query: float32 [960, 960], P('fsdp')
- grad_key: float32 [960, 320], P('fsdp')
- grad_value: float32 [960, 320], P('fsdp')
- grad_output: float32 [960, 960], P('fsdp')
- grad_gate: float32 [960, 2560], P('fsdp')
- grad_up: float32 [960, 2560], P('fsdp')
- grad_down: float32 [2560, 960], P('fsdp')
- grad_gain_attn: float32 [960], P('fsdp')
- grad_gain_ffn: float32 [960], P('fsdp')
The draws below stay inside these ranges and needn't reach their ends.
Inputs may be any that keep to these rules, and one draw needn't show every extreme that they name: For every group g: seq_cuts[g, 0] < 512, 1536 < seq_cuts[g, 1] <= seq_cuts[g, 2] <= 2048. The group's sequences are the nonempty ranges between 0, the cuts and 2048. In every draw some group holds a single sequence.
All inputs are finite; a program needn't handle non-finite values.
Results may differ from the reference program's by a relative error of at most 0.025.
Values may be sent and summed in bfloat16 or wider, within the bound.
No kernel may reach another device: no remote copies, remote signals or barrier semaphores. Data moves between devices by JAX's collectives and lax.ppermute only.
A program may use at most 192 MiB of HBM per device.

```python
import jax
import jax.numpy as jnp
from jax import lax

D = 960
HEADS = 15
KV_HEADS = 5
HEAD = 64
FF = 2560
TOK_DEV = 512
GROUP_TOK = 2048
GROUPS = 8


def draw_seq_cuts(key, part):
    key = jax.random.fold_in(key, 11)
    key_list = jax.random.split(key, 4)
    lower_cut = jax.random.randint(key_list[0], (GROUPS,), 0, TOK_DEV)
    middle_cut = jax.random.randint(key_list[1], (GROUPS,), 3 * TOK_DEV + 1, GROUP_TOK + 1)
    upper_cut = jax.random.randint(key_list[2], (GROUPS,), 0, GROUP_TOK + 1)
    upper_cut = jnp.maximum(upper_cut, middle_cut)
    ranking = jax.random.permutation(key_list[3], GROUPS)
    single = ranking == 0
    lower_cut = jnp.where(single, 0, lower_cut)
    middle_cut = jnp.where(single, GROUP_TOK, middle_cut)
    upper_cut = jnp.where(single, GROUP_TOK, upper_cut)
    return jnp.stack([lower_cut, middle_cut, upper_cut], axis=1).astype(jnp.int32)


def block_scale(rng, dims, cuts, least, high):
    level = 1.0
    for position, shards_of in cuts:
        draws = jax.random.uniform(jax.random.fold_in(jax.random.fold_in(rng, 6), position), (shards_of,), jnp.float32, least / len(cuts), high / len(cuts))
        level = level * jnp.repeat(jnp.exp(draws), dims[position] // shards_of).reshape((-1,) + (1,) * (len(dims) - 1 - position))
    return level


def scatter_about(key, extent, deviation, reach, pieces=(), held_as=jnp.bfloat16):
    drawn = jax.random.normal(key, extent, jnp.float32) * deviation
    if len(pieces) > 0:
        drawn = block_scale(key, extent, pieces, -0.22, 0.18) * drawn
    return jnp.clip(drawn, min=-reach, max=reach).astype(held_as)


def setup_inputs(seed: int = 0) -> dict:
    keys = jax.random.split(jax.random.key(seed), 13)
    tokens = scatter_about(keys[0], (GROUPS, GROUP_TOK, D), 1.0, 6.0, ((0, 8), (1, 4)))
    seq_cuts = draw_seq_cuts(jax.random.fold_in(keys[12], 71), 0)
    w_query = scatter_about(keys[2], (D, HEADS * HEAD), D ** -0.5, 0.1875, ((0, 4),))
    w_key = scatter_about(keys[3], (D, KV_HEADS * HEAD), D ** -0.5, 0.1875, ((0, 4),))
    w_value = scatter_about(keys[4], (D, KV_HEADS * HEAD), D ** -0.5, 0.1875, ((0, 4),))
    w_output = scatter_about(keys[5], (HEADS * HEAD, D), (max(D // 60, 1)) ** -0.5, 1.5, ((0, 4),))
    w_gate = scatter_about(keys[6], (D, FF), D ** -0.5, 0.1875, ((0, 4),))
    w_up = scatter_about(keys[7], (D, FF), D ** -0.5, 0.1875, ((0, 4),))
    w_down = scatter_about(keys[8], (FF, D), (FF // 2) ** -0.5, 0.15625, ((0, 4),))
    gain_attn = jnp.clip(1.0 + 0.1 * jax.random.normal(keys[9], (D,), jnp.float32), 0.5, 1.5)
    gain_ffn = jnp.clip(1.0 + 0.1 * jax.random.normal(keys[10], (D,), jnp.float32), 0.5, 1.5)
    cotangent = scatter_about(keys[11], (GROUPS, GROUP_TOK, D), 1.0, 6.0, ((0, 8), (1, 4)))
    return {"tokens": tokens, "seq_cuts": seq_cuts, "w_query": w_query, "w_key": w_key, "w_value": w_value, "w_output": w_output, "w_gate": w_gate, "w_up": w_up, "w_down": w_down, "gain_attn": gain_attn, "gain_ffn": gain_ffn, "cotangent": cotangent}


@jax.custom_vjp
def low(v):
    return lax.optimization_barrier(v.astype(jnp.bfloat16)).astype(jnp.float32)

@jax.custom_vjp
def low_back(v):
    return v

def low_keep(v):
    return (low(v), None)

def low_pass(kept, grad):
    return (grad,)

def back_keep(v):
    return (v, None)

def back_low(kept, grad):
    return (low(grad),)
low.defvjp(low_keep, low_pass)
low_back.defvjp(back_keep, back_low)
EPS = 1e-05
NEGATIVE = -1e+30

def dense(left, right):
    return jnp.dot(left, right, precision=lax.Precision.HIGHEST)

def rms_scale(hidden, gain):
    return hidden * lax.rsqrt(lax.optimization_barrier(jnp.mean(hidden * hidden, axis=-1, keepdims=True)) + EPS) * gain

def rotate(values, cosine, sine_table):
    half_width = values.shape[-1] // 2
    lower_half = values[..., :half_width]
    upper_half = values[..., half_width:]
    return jnp.concatenate([lower_half * cosine - upper_half * sine_table, upper_half * cosine + lower_half * sine_table], axis=-1)

def tables(positions):
    half_width = HEAD // 2
    frequency = jnp.power(10000.0, -2.0 * jnp.arange(half_width, dtype=jnp.float32) / HEAD)
    angle_table = positions.astype(jnp.float32)[:, None] * frequency[None, :]
    return (jnp.cos(angle_table)[:, None, :], jnp.sin(angle_table)[:, None, :])

def layer(hidden, params, cosine, sine_table, doc_ids):
    w_query, w_key, w_value, w_output, w_gate, w_up, w_down, gain_attn, gain_ffn = params
    length = hidden.shape[0]
    group_size = HEADS // KV_HEADS
    normed = low(rms_scale(hidden, gain_attn))
    queries = low(rotate(low_back(dense(normed, w_query)).reshape(length, HEADS, HEAD), cosine, sine_table))
    key_rows = low(rotate(low_back(dense(normed, w_key)).reshape(length, KV_HEADS, HEAD), cosine, sine_table))
    value_rows = low(low_back(dense(normed, w_value))).reshape(length, KV_HEADS, HEAD)
    queries = queries.reshape(length, KV_HEADS, group_size, HEAD)
    query_rows = min(512, length)
    key_index = jnp.arange(length, dtype=jnp.int32)

    def attend(start):
        query_block = lax.dynamic_slice_in_dim(queries, start, query_rows, 0)
        query_index = start + jnp.arange(query_rows, dtype=jnp.int32)
        query_docs = lax.dynamic_slice_in_dim(doc_ids, start, query_rows, 0)
        allowed = (query_docs[:, None] == doc_ids[None, :]) & (key_index[None, :] <= query_index[:, None])
        raw_scores = jnp.einsum('qkgd,skd->kgqs', query_block, key_rows, precision=lax.Precision.HIGHEST)
        scores = jnp.where(allowed[None, None], low_back(raw_scores * HEAD ** (-0.5)), NEGATIVE)
        probabilities = low(jax.nn.softmax(scores, axis=-1))
        return jnp.einsum('kgqs,skd->qkgd', probabilities, value_rows, precision=lax.Precision.HIGHEST)
    starts = jnp.arange(length // query_rows, dtype=jnp.int32) * query_rows
    mixed_heads = lax.map(jax.checkpoint(attend), starts).reshape(length, HEADS * HEAD)
    attended = low(low_back(mixed_heads))
    after_attn = hidden + low_back(dense(attended, w_output))
    normed_ffn = low(rms_scale(after_attn, gain_ffn))
    gate_act = low_back(dense(normed_ffn, w_gate))
    up_act = low_back(dense(normed_ffn, w_up))
    hidden_act = low(jax.nn.silu(gate_act) * up_act)
    return after_attn + low_back(dense(hidden_act, w_down))

def reference(tokens, seq_cuts, w_query, w_key, w_value, w_output, w_gate, w_up, w_down, gain_attn, gain_ffn, cotangent):
    token_index = jnp.arange(GROUP_TOK, dtype=jnp.int32)
    passed = token_index[None, :, None] >= seq_cuts[:, None, :]
    doc_ids = lax.optimization_barrier(jnp.sum(passed.astype(jnp.int32), axis=-1)).astype(jnp.int32)
    positions = token_index[None, :] - lax.optimization_barrier(jnp.max(jnp.where(passed, seq_cuts[:, None, :], 0), axis=-1))
    params = tuple((weight.astype(jnp.float32) for weight in (w_query, w_key, w_value, w_output, w_gate, w_up, w_down, gain_attn, gain_ffn)))

    def forward(inputs, *weights):

        def per_group(operands):
            hidden, group_positions, group_docs = operands
            cosine, sine_table = tables(group_positions)
            hidden = layer(hidden, weights, cosine, sine_table, group_docs)
            return layer(hidden, weights, cosine, sine_table, group_docs)
        return lax.map(jax.checkpoint(per_group), (inputs, positions, doc_ids))
    result, pullback = jax.vjp(forward, tokens.astype(jnp.float32), *params)
    grad_set = pullback(cotangent.astype(jnp.float32))
    return (result.astype(jnp.bfloat16), grad_set[0].astype(jnp.bfloat16), grad_set[1], grad_set[2], grad_set[3], grad_set[4], grad_set[5], grad_set[6], grad_set[7], grad_set[8], grad_set[9])
```

```python
import functools
import jax
import jax.numpy as jnp
from jax import lax
from jax.experimental import pallas as pl
from jax.experimental.pallas import tpu as pltpu
from jax.sharding import PartitionSpec as P

HEADS = 15
KV_HEADS = 5
HEAD = 64
GROUP = HEADS // KV_HEADS
LANES = 128
NEGATIVE = -1e30
LOG2E = 1.4426950408889634
LN2 = 0.6931471805599453
MIB = 1 << 20
f32 = jnp.float32
bf16 = jnp.bfloat16


def nn(left, right):
    return lax.dot_general(left, right, (((1,), (0,)), ((), ())), preferred_element_type=f32)


def nt(left, right):
    return lax.dot_general(left, right, (((1,), (1,)), ((), ())), preferred_element_type=f32)


def lane_index(shape):
    return lax.broadcasted_iota(jnp.int32, shape, len(shape) - 1)


def block_of(device, half):
    return 2 * device if half == 0 else 7 - 2 * device


def swap_halves(tile):
    low = lane_index(tile.shape) % HEAD < HEAD // 2
    return jnp.where(low, pltpu.roll(tile, LANES - HEAD // 2, 1), pltpu.roll(tile, HEAD // 2, 1))


def three_terms(column, lane):
    high = column.astype(bf16).astype(f32)
    rest = column - high
    middle = rest.astype(bf16).astype(f32)
    low = rest - middle
    return jnp.where(lane == 8, high, jnp.where(lane == 9, middle, jnp.where(lane == 10, low, 0.0)))


def gather_keys(f, g, pieces, key_marks, kvf):
    block = kvf.shape[1]
    for m, piece in enumerate(pieces):
        device = f ^ m
        for half in (0, 1):
            kvf[block_of(device, half), :, :LANES] = piece[0, half * block : (half + 1) * block, :]

    @pl.when(g == 0)
    def _():
        for j in range(kvf.shape[0]):
            kvf[j, :, LANES:] = key_marks[j * block : (j + 1) * block, :]


def attend_kernel(f_ref, q, q_marks, key_marks, own, near, far, last, attended, marks_out, kvf, scores, peak, acc):
    g, b = pl.program_id(0), pl.program_id(1)
    f = f_ref[0]
    block = kvf.shape[1]
    rows = GROUP * block

    @pl.when(b == 0)
    def _():
        gather_keys(f, g, (own, near, far, last), key_marks, kvf)

    count = jnp.where(b == 0, 2 * f, 7 - 2 * f)
    marks = q_marks[...]
    qf = jnp.concatenate(
        [q[...].reshape(rows, LANES), jnp.concatenate([marks] * GROUP, axis=0)], axis=1
    )
    peak[...] = jnp.full(peak.shape, NEGATIVE, f32)

    def score(j, diagonal):
        s = nt(qf, kvf[j])
        if diagonal:
            row = lax.broadcasted_iota(jnp.int32, (block, block), 0)
            column = lax.broadcasted_iota(jnp.int32, (block, block), 1)
            shift = jnp.where(column <= row, 0.0, NEGATIVE)
            s = (s.reshape(GROUP, block, block) + shift[None]).reshape(rows, block)
        scores[j] = s
        best = s[:, :LANES]
        for t in range(1, block // LANES):
            best = jnp.maximum(best, s[:, t * LANES : (t + 1) * LANES])
        peak[...] = jnp.maximum(peak[...], best)

    lax.fori_loop(0, count, lambda j, c: (score(j, False), c)[1], 0)
    score(count, True)
    top = jnp.max(peak[...], axis=1, keepdims=True)
    acc[...] = jnp.zeros(acc.shape, f32)

    def mix(j, c):
        p = jnp.exp2(scores[j] - top).astype(bf16)
        acc[...] += nn(p, kvf[j])
        return c

    lax.fori_loop(0, count + 1, mix, 0)
    total = acc[:, LANES + 8 : LANES + 9]
    out = acc[:, :LANES] / total
    log_total = top + jnp.log2(total)
    lane = lane_index((rows, LANES))
    new_marks = jnp.concatenate([marks] * GROUP, axis=0).astype(f32) + three_terms(-log_total, lane)
    marks_out[...] = new_marks.astype(bf16).reshape(GROUP, block, LANES)
    row0 = pl.multiple_of(b * block, block)
    lane = lane_index((block, LANES))
    for i in range(GROUP):
        h = GROUP * g + i
        pair = pl.multiple_of((h // 2) * LANES, LANES)
        odd = h % 2 == 1
        tile = out[i * block : (i + 1) * block, :]
        turned = pltpu.roll(tile, HEAD, 1)
        old = attended[pl.ds(row0, block), pl.ds(pair, LANES)].astype(f32)
        new = jnp.where(
            odd, jnp.where(lane >= HEAD, tile, old), jnp.where(lane < HEAD, turned, 0.0)
        )
        attended[pl.ds(row0, block), pl.ds(pair, LANES)] = new.astype(bf16)


def attend(f, q, q_marks, key_marks, pieces):
    tokens = q.shape[1]
    block = tokens // 2
    blocks = key_marks.shape[0] // block
    piece = pl.BlockSpec((1, tokens, LANES), lambda g, b, f: (g, 0, 0))
    heads = pl.BlockSpec((GROUP, block, LANES), lambda g, b, f: (g, b, 0))
    width = (HEADS + 1) * HEAD
    return pl.pallas_call(
        attend_kernel,
        grid_spec=pltpu.PrefetchScalarGridSpec(
            num_scalar_prefetch=1,
            grid=(KV_HEADS, 2),
            in_specs=[
                heads,
                pl.BlockSpec((block, LANES), lambda g, b, f: (b, 0)),
                pl.BlockSpec(key_marks.shape, lambda g, b, f: (0, 0)),
                piece,
                piece,
                piece,
                piece,
            ],
            out_specs=[
                pl.BlockSpec((tokens, width), lambda g, b, f: (0, 0)),
                heads,
            ],
            scratch_shapes=[
                pltpu.VMEM((blocks, block, 2 * LANES), bf16),
                pltpu.VMEM((blocks, GROUP * block, block), f32),
                pltpu.VMEM((GROUP * block, LANES), f32),
                pltpu.VMEM((GROUP * block, 2 * LANES), f32),
            ],
        ),
        out_shape=[
            jax.ShapeDtypeStruct((tokens, width), bf16),
            jax.ShapeDtypeStruct((HEADS, tokens, LANES), bf16),
        ],
        compiler_params=pltpu.CompilerParams(vmem_limit_bytes=48 * MIB),
        cost_estimate=pl.CostEstimate(flops=12_000_000_000, bytes_accessed=8_000_000, transcendentals=9_000_000),
        name="attend",
    )(f, q, q_marks, key_marks, *pieces)


def attend_back_kernel(
    f_ref, q, marks, key_marks, own, near, far, last, grad, attended, cos_ref, sin_ref,
    grad_q, keep, send, kvf, kv_sum, both, turned, acc,
):
    g, b = pl.program_id(0), pl.program_id(1)
    f = f_ref[0]
    block = kvf.shape[1]
    rows = GROUP * block

    @pl.when(b == 0)
    def _():
        gather_keys(f, g, (own, near, far, last), key_marks, kvf)
        kv_sum[...] = jnp.zeros(kv_sum.shape, f32)

    count = jnp.where(b == 0, 2 * f, 7 - 2 * f)
    row0 = pl.multiple_of(b * block, block)
    lane = lane_index((block, LANES))
    both[:rows, :LANES] = q[...].reshape(rows, LANES)
    both[:rows, LANES:] = marks[...].reshape(rows, LANES)
    for i in range(GROUP):
        h = GROUP * g + i
        pair = pl.multiple_of((h // 2) * LANES, LANES)
        odd = h % 2 == 1
        d_tile = grad[pl.ds(row0, block), pl.ds(pair, LANES)].astype(f32)
        o_tile = attended[pl.ds(row0, block), pl.ds(pair, LANES)].astype(f32)
        mine = (lane >= HEAD) == odd
        inner = jnp.sum(jnp.where(mine, d_tile * o_tile, 0.0), axis=1, keepdims=True)
        moved = jnp.where(odd, d_tile, pltpu.roll(d_tile, HEAD, 1))
        moved = jnp.where(lane >= HEAD, moved, 0.0)
        first = rows + i * block
        both[first : first + block, :LANES] = moved.astype(bf16)
        both[first : first + block, LANES:] = three_terms(-inner, lane).astype(bf16)
        joined = moved + q[i].astype(f32)
        turned[:, i * block : (i + 1) * block] = joined.T.astype(bf16)
    acc[...] = jnp.zeros(acc.shape, f32)

    def step(j, diagonal):
        keys = kvf[j]
        s = nt(both[...], keys)
        p = jnp.exp2(s[:rows])
        if diagonal:
            row = lax.broadcasted_iota(jnp.int32, (block, block), 0)
            column = lax.broadcasted_iota(jnp.int32, (block, block), 1)
            p = jnp.where((column <= row)[None], p.reshape(GROUP, block, block), 0.0).reshape(rows, block)
        ds = (p * s[rows:]).astype(bf16)
        p = p.astype(bf16)
        acc[...] += nn(ds, keys[:, :LANES])
        kv_sum[j, :HEAD] += nn(turned[:HEAD], ds)
        kv_sum[j, HEAD:] += nn(turned[HEAD:], p)

    lax.fori_loop(0, count, lambda j, c: (step(j, False), c)[1], 0)
    step(count, True)
    scale = HEAD ** (-0.5)
    for i in range(GROUP):
        h = GROUP * g + i
        pair = pl.multiple_of((h // 2) * LANES, LANES)
        odd = h % 2 == 1
        tile = acc[i * block : (i + 1) * block, :] * scale
        tile = tile * cos_ref[...] - swap_halves(tile) * sin_ref[...]
        other = pltpu.roll(tile, HEAD, 1)
        old = grad_q[pl.ds(row0, block), pl.ds(pair, LANES)].astype(f32)
        new = jnp.where(odd, jnp.where(lane >= HEAD, other, old), jnp.where(lane < HEAD, tile, 0.0))
        grad_q[pl.ds(row0, block), pl.ds(pair, LANES)] = new.astype(bf16)

    @pl.when(b == 1)
    def _():
        factor = jnp.where(lane < HEAD, LN2, 1.0)
        for m in range(4):
            device = f ^ m
            for half in (0, 1):
                total = kv_sum[block_of(device, half)].T * factor
                ref = send if m % 2 else keep
                ref[m // 2, 0, half * block : (half + 1) * block, :] = total.astype(ref.dtype)


def attend_back(f, q, marks, key_marks, pieces, grad, attended, cos, sin):
    tokens = q.shape[1]
    block = tokens // 2
    blocks = key_marks.shape[0] // block
    piece = pl.BlockSpec((1, tokens, LANES), lambda g, b, f: (g, 0, 0))
    heads = pl.BlockSpec((GROUP, block, LANES), lambda g, b, f: (g, b, 0))
    width = (HEADS + 1) * HEAD
    whole = pl.BlockSpec((tokens, width), lambda g, b, f: (0, 0))
    table = pl.BlockSpec((block, LANES), lambda g, b, f: (b, 0))
    pair = pl.BlockSpec((2, 1, tokens, LANES), lambda g, b, f: (0, g, 0, 0))
    rows = GROUP * block
    return pl.pallas_call(
        attend_back_kernel,
        grid_spec=pltpu.PrefetchScalarGridSpec(
            num_scalar_prefetch=1,
            grid=(KV_HEADS, 2),
            in_specs=[
                heads,
                heads,
                pl.BlockSpec(key_marks.shape, lambda g, b, f: (0, 0)),
                piece,
                piece,
                piece,
                piece,
                whole,
                whole,
                table,
                table,
            ],
            out_specs=[whole, pair, pair],
            scratch_shapes=[
                pltpu.VMEM((blocks, block, 2 * LANES), bf16),
                pltpu.VMEM((blocks, LANES, block), f32),
                pltpu.VMEM((2 * rows, 2 * LANES), bf16),
                pltpu.VMEM((LANES, rows), bf16),
                pltpu.VMEM((rows, LANES), f32),
            ],
        ),
        out_shape=[
            jax.ShapeDtypeStruct((tokens, width), bf16),
            jax.ShapeDtypeStruct((2, KV_HEADS, tokens, LANES), bf16),
            jax.ShapeDtypeStruct((2, KV_HEADS, tokens, LANES), bf16),
        ],
        compiler_params=pltpu.CompilerParams(vmem_limit_bytes=48 * MIB),
        cost_estimate=pl.CostEstimate(flops=30_000_000_000, bytes_accessed=12_000_000, transcendentals=9_000_000),
        name="attend_back",
    )(f, q, marks, key_marks, *pieces, grad, attended, cos, sin)


EPS = 1e-05
ANY = pl.BlockSpec(memory_space=pl.ANY)


def params(mib):
    return pltpu.CompilerParams(vmem_limit_bytes=mib * MIB)


def cost(flops, moved):
    return pl.CostEstimate(flops=int(flops), bytes_accessed=int(moved), transcendentals=0)


def row_copies(f, pieces, target, sems):
    rows = pieces[0].shape[0]
    return [
        pltpu.make_async_copy(
            piece, target.at[pl.ds(pl.multiple_of((f ^ m) * rows, 16), rows), :], sems.at[m]
        )
        for m, piece in enumerate(pieces)
    ]


def tile_copies(f, t, pieces, target, sems):
    rows, width = pieces[0].shape[0], target.shape[2]
    return [
        pltpu.make_async_copy(
            piece.at[:, pl.ds(pl.multiple_of(t * width, width), width)],
            target.at[t, pl.ds(pl.multiple_of((f ^ m) * rows, 16), rows), :],
            sems.at[t, m],
        )
        for m, piece in enumerate(pieces)
    ]


def start(copies):
    for copy in copies:
        copy.start()


def wait(copies):
    for copy in copies:
        copy.wait()


def inverse_of(values):
    return lax.rsqrt(jnp.mean(values * values, axis=-1, keepdims=True) + EPS)


def norm_back(upstream, values, gain):
    inverse = inverse_of(values)
    scaled = upstream * gain
    gain_grad = jnp.sum(upstream * (values * inverse), axis=0, keepdims=True)
    middle = jnp.mean(scaled * values, axis=-1, keepdims=True)
    return inverse * scaled - (inverse * inverse * inverse * middle) * values, gain_grad


def project_kernel(f_ref, h, gain, cos_ref, sin_ref, own, near, far, last, normed_t, q_out, kv_out, w, sems):
    copies = row_copies(f_ref[0], (own, near, far, last), w, sems)
    start(copies)
    hidden = h[...].astype(f32)
    normed = (hidden * inverse_of(hidden) * gain[...]).astype(bf16)
    normed_t[...] = normed.T
    cos, sin = cos_ref[...], sin_ref[...]
    lane = lane_index(cos.shape)
    kv_cos, kv_sin = jnp.where(lane < HEAD, cos, 1.0), jnp.where(lane < HEAD, sin, 0.0)
    wait(copies)
    for g in range(KV_HEADS):
        tile = nn(normed, w[:, g * LANES : (g + 1) * LANES])
        kv_out[g] = (tile * kv_cos + swap_halves(tile) * kv_sin).astype(bf16)
    first = KV_HEADS * LANES
    for p in range((HEADS + 1) // 2):
        tile = nn(normed, w[:, first + p * LANES : first + (p + 1) * LANES])
        tile = (tile * cos + swap_halves(tile) * sin) * (HEAD ** (-0.5) * LOG2E)
        q_out[2 * p] = jnp.where(lane < HEAD, tile, 0.0).astype(bf16)
        if 2 * p + 1 < HEADS:
            q_out[2 * p + 1] = jnp.where(lane < HEAD, pltpu.roll(tile, HEAD, 1), 0.0).astype(bf16)


def project(f, hidden, gain, cos, sin, pieces):
    tokens, width = hidden.shape
    rows, columns = pieces[0].shape
    full = lambda *shape: pl.BlockSpec(shape, lambda i, f: (0,) * len(shape))
    return pl.pallas_call(
        project_kernel,
        grid_spec=pltpu.PrefetchScalarGridSpec(
            num_scalar_prefetch=1,
            grid=(1,),
            in_specs=[full(tokens, width), full(1, width), full(*cos.shape), full(*sin.shape)] + [ANY] * 4,
            out_specs=[
                full(width, tokens),
                full(HEADS, tokens, LANES),
                full(KV_HEADS, tokens, LANES),
            ],
            scratch_shapes=[pltpu.VMEM((4 * rows, columns), bf16), pltpu.SemaphoreType.DMA((4,))],
        ),
        out_shape=[
            jax.ShapeDtypeStruct((width, tokens), bf16),
            jax.ShapeDtypeStruct((HEADS, tokens, LANES), bf16),
            jax.ShapeDtypeStruct((KV_HEADS, tokens, LANES), bf16),
        ],
        compiler_params=params(40),
        cost_estimate=cost(4e9, 8e6),
        name="project",
    )(f, hidden, gain, cos, sin, *pieces)


def feed_kernel(
    f_ref, h, attended, gain, *refs,
):
    o, gate, up, down = (refs[4 * i : 4 * i + 4] for i in range(4))
    after, attended_t, normed_t, gate_out, up_out, hidden_t, result = refs[16:23]
    w_o, w_gate, w_up, w_down, n16, acc, o_sem, gate_sem, up_sem, down_sem = refs[23:]
    f, t = f_ref[0], pl.program_id(0)
    tiles = w_gate.shape[0]
    depth = 4 * o[0].shape[0]

    @pl.when(t == 0)
    def _():
        o_copies = row_copies(f, o, w_o, o_sem)
        start(o_copies)
        for tile in range(tiles):
            start(tile_copies(f, tile, gate, w_gate, gate_sem))
            start(tile_copies(f, tile, up, w_up, up_sem))
            if tile == 0:
                start(row_copies(f, down, w_down, down_sem))
        att = attended[...]
        attended_t[...] = att.T
        w_o[depth:, :] = jnp.zeros((w_o.shape[0] - depth, w_o.shape[1]), bf16)
        wait(o_copies)
        value = h[...].astype(f32) + nn(att, w_o[...])
        after[...] = value
        normed = (value * inverse_of(value) * gain[...]).astype(bf16)
        n16[...] = normed
        normed_t[...] = normed.T
        acc[...] = value
        wait(row_copies(f, down, w_down, down_sem))

    wait(tile_copies(f, t, gate, w_gate, gate_sem))
    wait(tile_copies(f, t, up, w_up, up_sem))
    gate_act = nn(n16[...], w_gate[t])
    up_act = nn(n16[...], w_up[t])
    hidden = (gate_act * jax.nn.sigmoid(gate_act) * up_act).astype(bf16)
    gate_out[0] = gate_act.astype(bf16)
    up_out[0] = up_act.astype(bf16)
    hidden_t[0] = hidden.T
    wide = hidden.shape[1]
    acc[...] += nn(hidden, w_down[pl.ds(pl.multiple_of(t * wide, wide), wide), :])

    @pl.when(t == tiles - 1)
    def _():
        result[...] = acc[...].astype(result.dtype)


TILE = 512


def weight_scratch(o, gate, down):
    rows, width = o.shape
    tiles = gate.shape[1] // TILE
    return [
        pltpu.VMEM((4 * rows + HEAD, width), bf16),
        pltpu.VMEM((tiles, 4 * rows, TILE), bf16),
        pltpu.VMEM((tiles, 4 * rows, TILE), bf16),
        pltpu.VMEM((4 * down.shape[0], width), bf16),
    ]


def weight_sems(gate):
    tiles = gate.shape[1] // TILE
    dma = pltpu.SemaphoreType.DMA
    return [dma((4,)), dma((tiles, 4)), dma((tiles, 4)), dma((4,))]


def feed(f, hidden, attended, gain, o, gate, up, down, result_type):
    tokens, width = hidden.shape
    tiles = gate[0].shape[1] // TILE
    full = lambda *shape: pl.BlockSpec(shape, lambda i, f: (0,) * len(shape))
    tile = lambda *shape: pl.BlockSpec((1,) + shape, lambda i, f: (i, 0, 0))
    like = jax.ShapeDtypeStruct
    return pl.pallas_call(
        feed_kernel,
        grid_spec=pltpu.PrefetchScalarGridSpec(
            num_scalar_prefetch=1,
            grid=(tiles,),
            in_specs=[full(tokens, width), full(*attended.shape), full(1, width)] + [ANY] * 16,
            out_specs=[
                full(tokens, width),
                full(attended.shape[1], tokens),
                full(width, tokens),
                tile(tokens, TILE),
                tile(tokens, TILE),
                tile(TILE, tokens),
                full(tokens, width),
            ],
            scratch_shapes=weight_scratch(o[0], gate[0], down[0])
            + [pltpu.VMEM((tokens, width), bf16), pltpu.VMEM((tokens, width), f32)]
            + weight_sems(gate[0]),
        ),
        out_shape=[
            like((tokens, width), f32),
            like((attended.shape[1], tokens), bf16),
            like((width, tokens), bf16),
            like((tiles, tokens, TILE), bf16),
            like((tiles, tokens, TILE), bf16),
            like((tiles, TILE, tokens), bf16),
            like((tokens, width), result_type),
        ],
        compiler_params=params(56),
        cost_estimate=cost(10e9, 30e6),
        name="feed",
    )(f, hidden, attended, gain, *o, *gate, *up, *down)


def feed_back_kernel(f_ref, g, after, gain, gate_act, up_act, *refs):
    o, gate, up, down = (refs[4 * i : 4 * i + 4] for i in range(4))
    grad_gate, grad_up, g_out, grad_after, branch_out, grad_attended, gain_grad = refs[16:23]
    w_o, w_gate, w_up, w_down, acc, o_sem, gate_sem, up_sem, down_sem = refs[23:]
    f, t = f_ref[0], pl.program_id(0)
    tiles = w_gate.shape[0]
    depth = 4 * o[0].shape[0]

    @pl.when(t == 0)
    def _():
        down_copies = row_copies(f, down, w_down, down_sem)
        start(down_copies)
        for tile in range(tiles):
            start(tile_copies(f, tile, gate, w_gate, gate_sem))
            start(tile_copies(f, tile, up, w_up, up_sem))
        start(row_copies(f, o, w_o, o_sem))
        g_out[...] = g[...].astype(bf16)
        acc[...] = jnp.zeros(acc.shape, f32)
        w_o[depth:, :] = jnp.zeros((w_o.shape[0] - depth, w_o.shape[1]), bf16)
        wait(down_copies)

    wait(tile_copies(f, t, gate, w_gate, gate_sem))
    wait(tile_copies(f, t, up, w_up, up_sem))
    wide = w_gate.shape[2]
    grad_hidden = nt(g_out[...], w_down[pl.ds(pl.multiple_of(t * wide, wide), wide), :])
    value = gate_act[0].astype(f32)
    logistic = jax.nn.sigmoid(value)
    d_gate = grad_hidden * up_act[0].astype(f32) * (logistic * (1.0 + value * (1.0 - logistic)))
    d_gate = d_gate.astype(bf16)
    d_up = (grad_hidden * (value * logistic)).astype(bf16)
    grad_gate[0] = d_gate
    grad_up[0] = d_up
    acc[...] += nt(d_gate, w_gate[t]) + nt(d_up, w_up[t])

    @pl.when(t == tiles - 1)
    def _():
        back, gain_part = norm_back(acc[...], after[...], gain[...])
        back = back + g[...].astype(f32)
        gain_grad[...] = gain_part
        grad_after[...] = back
        branch = back.astype(bf16)
        branch_out[...] = branch
        wait(row_copies(f, o, w_o, o_sem))
        grad_attended[...] = nt(branch, w_o[...]).astype(bf16)


def feed_back(f, g, after, gain, gate_act, up_act, o, gate, up, down):
    tokens, width = after.shape
    tiles = gate[0].shape[1] // TILE
    full = lambda *shape: pl.BlockSpec(shape, lambda i, f: (0,) * len(shape))
    tile = lambda *shape: pl.BlockSpec((1,) + shape, lambda i, f: (i, 0, 0))
    like = jax.ShapeDtypeStruct
    depth = 4 * o[0].shape[0] + HEAD
    return pl.pallas_call(
        feed_back_kernel,
        grid_spec=pltpu.PrefetchScalarGridSpec(
            num_scalar_prefetch=1,
            grid=(tiles,),
            in_specs=[full(tokens, width), full(tokens, width), full(1, width)]
            + [tile(tokens, TILE), tile(tokens, TILE)]
            + [ANY] * 16,
            out_specs=[
                tile(tokens, TILE),
                tile(tokens, TILE),
                full(tokens, width),
                full(tokens, width),
                full(tokens, width),
                full(tokens, depth),
                full(1, width),
            ],
            scratch_shapes=weight_scratch(o[0], gate[0], down[0])
            + [pltpu.VMEM((tokens, width), f32)]
            + weight_sems(gate[0]),
        ),
        out_shape=[
            like((tiles, tokens, TILE), bf16),
            like((tiles, tokens, TILE), bf16),
            like((tokens, width), bf16),
            like((tokens, width), f32),
            like((tokens, width), bf16),
            like((tokens, depth), bf16),
            like((1, width), f32),
        ],
        compiler_params=params(56),
        cost_estimate=cost(10e9, 30e6),
        name="feed_back",
    )(f, g, after, gain, gate_act, up_act, *o, *gate, *up, *down)


def project_back_kernel(
    f_ref, grad_q, kept, came, cos_ref, sin_ref, h, gain, grad_after, own, near, far, last,
    grads, grad_in, gain_grad, w, sems,
):
    copies = row_copies(f_ref[0], (own, near, far, last), w, sems)
    start(copies)
    cos, sin = cos_ref[...], sin_ref[...]
    lane = lane_index(cos.shape)
    cos, sin = jnp.where(lane < HEAD, cos, 1.0), jnp.where(lane < HEAD, sin, 0.0)
    for g in range(KV_HEADS):
        tile = kept[g].astype(f32) + came[g].astype(f32)
        tile = tile * cos - swap_halves(tile) * sin
        grads[:, g * LANES : (g + 1) * LANES] = tile.astype(bf16)
    grads[:, KV_HEADS * LANES :] = grad_q[...]
    wait(copies)
    grad_normed = nt(grads[...], w[...])
    back, gain_part = norm_back(grad_normed, h[...].astype(f32), gain[...])
    gain_grad[...] = gain_part
    grad_in[...] = (back + grad_after[...]).astype(grad_in.dtype)


def project_back(f, grad_q, kept, came, cos, sin, hidden, gain, grad_after, pieces, result_type):
    tokens, width = hidden.shape
    rows, columns = pieces[0].shape
    full = lambda *shape: pl.BlockSpec(shape, lambda i, f: (0,) * len(shape))
    like = jax.ShapeDtypeStruct
    return pl.pallas_call(
        project_back_kernel,
        grid_spec=pltpu.PrefetchScalarGridSpec(
            num_scalar_prefetch=1,
            grid=(1,),
            in_specs=[
                full(*grad_q.shape),
                full(*kept.shape),
                full(*came.shape),
                full(*cos.shape),
                full(*sin.shape),
                full(tokens, width),
                full(1, width),
                full(tokens, width),
            ]
            + [ANY] * 4,
            out_specs=[full(tokens, columns), full(tokens, width), full(1, width)],
            scratch_shapes=[pltpu.VMEM((4 * rows, columns), bf16), pltpu.SemaphoreType.DMA((4,))],
        ),
        out_shape=[
            like((tokens, columns), bf16),
            like((tokens, width), result_type),
            like((1, width), f32),
        ],
        compiler_params=params(40),
        cost_estimate=cost(4e9, 12e6),
        name="project_back",
    )(f, grad_q, kept, came, cos, sin, hidden, gain, grad_after, *pieces)


def outer_kernel(f_ref, *refs, pairs, rows):
    lefts, rights = refs[:2], refs[2 : 2 + 2 * pairs]
    outs = refs[2 + 2 * pairs : 2 + 4 * pairs]
    acc = refs[-1]
    f = f_ref[0]
    for k in range(pairs):
        first, second = rights[2 * k], rights[2 * k + 1]
        value = lambda ref: ref[0] if len(ref.shape) == 3 else ref[...]
        acc[...] = nn(lefts[0][...], value(first)) + nn(lefts[1][...], value(second))
        for m in range(4):
            out = outs[2 * k + m % 2]
            out[m // 2] = acc[pl.ds(pl.multiple_of((f ^ m) * rows, 16), rows), :].astype(bf16)


def outer(f, lefts, rights, rows, name):
    width, tokens = lefts[0].shape
    tiled = rights[0][0].ndim == 3
    tiles = rights[0][0].shape[0] if tiled else 1
    columns = rights[0][0].shape[-1]
    pairs = len(rights)
    right_spec = (
        pl.BlockSpec((1, tokens, columns), lambda i, f: (i, 0, 0))
        if tiled
        else pl.BlockSpec((tokens, columns), lambda i, f: (0, 0))
    )
    left_spec = pl.BlockSpec((width, tokens), lambda i, f: (0, 0))
    out_spec = pl.BlockSpec((2, rows, columns), lambda i, f: (0, 0, i))
    shape = jax.ShapeDtypeStruct((2, rows, tiles * columns), bf16)
    return pl.pallas_call(
        functools.partial(outer_kernel, pairs=pairs, rows=rows),
        grid_spec=pltpu.PrefetchScalarGridSpec(
            num_scalar_prefetch=1,
            grid=(tiles,),
            in_specs=[left_spec] * 2 + [right_spec] * (2 * pairs),
            out_specs=[out_spec] * (2 * pairs),
            scratch_shapes=[pltpu.VMEM((width, columns), f32)],
        ),
        out_shape=[shape] * (2 * pairs),
        compiler_params=params(48),
        cost_estimate=cost(4 * width * tokens * tiles * columns * pairs, 20e6),
        name=name,
    )(f, *lefts, *[r for pair in rights for r in pair])


def outer_rows_kernel(f_ref, left_first, left_second, right_first, right_second, keep, send):
    value = nn(left_first[...], right_first[...]) + nn(left_second[...], right_second[...])
    s = pl.program_id(0)

    @pl.when(s < 2)
    def _():
        send[0] = value.astype(bf16)

    @pl.when(s >= 2)
    def _():
        keep[0] = value.astype(bf16)


def outer_rows(f, lefts, rights, name):
    width, tokens = lefts[0].shape
    rows, columns = width // 4, rights[0].shape[1]

    def quarter(s, f):
        slot = jnp.where(s < 2, 2 * s + 1, 2 * s - 4)
        return (f[0] ^ slot, 0)

    left_spec = pl.BlockSpec((rows, tokens), quarter)
    right_spec = pl.BlockSpec((tokens, columns), lambda s, f: (0, 0))
    shape = jax.ShapeDtypeStruct((2, rows, columns), bf16)
    return pl.pallas_call(
        outer_rows_kernel,
        grid_spec=pltpu.PrefetchScalarGridSpec(
            num_scalar_prefetch=1,
            grid=(4,),
            in_specs=[left_spec, left_spec, right_spec, right_spec],
            out_specs=[
                pl.BlockSpec((1, rows, columns), lambda s, f: (jnp.maximum(s - 2, 0), 0, 0)),
                pl.BlockSpec((1, rows, columns), lambda s, f: (jnp.minimum(s, 1), 0, 0)),
            ],
        ),
        out_shape=[shape] * 2,
        compiler_params=params(48),
        cost_estimate=cost(4 * width * tokens * columns, 12e6),
        name=name,
    )(f, *lefts, *rights)


def flip(array, axis, bit):
    size = lax.axis_size(axis)
    return lax.ppermute(array, axis, [(i, i ^ bit) for i in range(size)])


def pieces_of(shard):
    far = flip(shard, "fsdp", 2)
    return (shard, flip(shard, "fsdp", 1), far, flip(far, "fsdp", 1))


def exchange_halves(array):
    half = array.shape[0] // 2
    return jnp.concatenate([array[:half], flip(array[half:], "fsdp", 3)], axis=0)


def scatter_kept(keep, send):
    came = flip(send, "fsdp", 1)
    half = keep.astype(f32) + came.astype(f32)
    return half[0], flip(half[1].astype(bf16), "fsdp", 2)


def total_over_dp(array):
    size = lax.axis_size("dp")
    index = lax.axis_index("dp")
    bits = [1 << b for b in range(size.bit_length() - 1)]
    part = array
    dims = []
    for bit in bits:
        dim = next((d for d, t in ((1, 128), (0, 8)) if part.shape[d] % (2 * t) == 0), 1)
        dims.append(dim)
        width = part.shape[dim] // 2
        mine = (index // bit) % 2
        send = lax.dynamic_slice_in_dim(part, (1 - mine) * width, width, dim).astype(bf16)
        keep = lax.dynamic_slice_in_dim(part, mine * width, width, dim).astype(f32)
        part = keep + flip(send, "dp", bit).astype(f32)
    part = part.astype(bf16)
    for bit, dim in zip(reversed(bits), reversed(dims)):
        other = flip(part, "dp", bit)
        mine = (index // bit) % 2
        part = jnp.where(
            mine == 0, jnp.concatenate([part, other], dim), jnp.concatenate([other, part], dim)
        )
    return part.astype(f32)


def total_small(array):
    for bit in (1, 2):
        array = array + flip(array, "fsdp", bit)
    for b in range(lax.axis_size("dp").bit_length() - 1):
        array = array + flip(array, "dp", 1 << b)
    return array


def reduce_unit(keep, send):
    kept, came = scatter_kept(keep, send)
    return total_over_dp(kept + came.astype(f32))


def per_device(
    tokens, seq_cuts, w_query, w_key, w_value, w_output, w_gate, w_up, w_down, gain_attn, gain_ffn, cotangent
):
    rows, width = tokens.shape[1], tokens.shape[2]
    half = rows // 2
    index = lax.axis_index("fsdp")
    f = index.astype(jnp.int32).reshape(1)
    count = rows * lax.axis_size("fsdp")
    shard_rows = w_key.shape[0]

    key_value = jnp.stack(
        [w_key.reshape(shard_rows, KV_HEADS, HEAD), w_value.reshape(shard_rows, KV_HEADS, HEAD)], axis=2
    ).reshape(shard_rows, 2 * KV_HEADS * HEAD)
    w_in = pieces_of(jnp.concatenate([key_value, w_query, jnp.zeros((shard_rows, HEAD), bf16)], axis=1))
    h0 = exchange_halves(tokens[0])
    o, gate, up, down = pieces_of(w_output), pieces_of(w_gate), pieces_of(w_up), pieces_of(w_down)

    bounds = seq_cuts[0]
    within = jnp.arange(half, dtype=jnp.int32)
    local = jnp.concatenate([2 * index * half + within, (7 - 2 * index) * half + within]).astype(jnp.int32)
    every = jnp.arange(count, dtype=jnp.int32)
    passed = local[:, None] >= bounds[None, :]
    docs = jnp.sum(passed.astype(jnp.int32), axis=1)
    positions = local - jnp.max(jnp.where(passed, bounds[None, :], 0), axis=1)
    key_docs = jnp.sum((every[:, None] >= bounds[None, :]).astype(jnp.int32), axis=1)
    lane = jnp.arange(LANES, dtype=jnp.int32)[None, :]
    one = ((lane == key_docs[:, None]) & (lane < 4)) | ((lane >= 8) & (lane < 11))
    key_marks = one.astype(bf16)
    q_marks = jnp.where((lane < 4) & (lane != docs[:, None]), NEGATIVE, 0.0).astype(bf16)
    frequency = jnp.power(10000.0, -2.0 * jnp.arange(HEAD // 2, dtype=f32) / HEAD)
    angle = positions.astype(f32)[:, None] * frequency[None, :]
    cosine, sine = jnp.cos(angle), jnp.sin(angle)
    cos = jnp.concatenate([cosine] * 4, axis=1)
    sin = jnp.concatenate([-sine, sine] * 2, axis=1)
    gain_a, gain_f = gain_attn[None, :], gain_ffn[None, :]

    def forward(hidden, result_type):
        normed_t, q, kv = project(f, hidden, gain_a, cos, sin, w_in)
        far = flip(kv, "fsdp", 2)
        pieces = (kv, flip(kv, "fsdp", 1), far, flip(far, "fsdp", 1))
        attended, marks = attend(f, q, q_marks, key_marks, pieces)
        after, attended_t, normed_ffn_t, gate_act, up_act, hidden_t, result = feed(
            f, hidden, attended, gain_f, o, gate, up, down, result_type
        )
        return result, (
            hidden, normed_t, q, pieces, attended, marks, after, attended_t, normed_ffn_t, gate_act, up_act,
            hidden_t,
        )

    def backward(g, stored, result_type):
        hidden, _, q, pieces, attended, marks, after, _, _, gate_act, up_act, _ = stored
        grad_gate, grad_up, g16, grad_after, branch, grad_attended, gain_f_part = feed_back(
            f, g, after, gain_f, gate_act, up_act, o, gate, up, down
        )
        grad_q, keep, send = attend_back(f, q, marks, key_marks, pieces, grad_attended, attended, cos, sin)
        kept, came = scatter_kept(keep, send)
        grads, grad_in, gain_a_part = project_back(
            f, grad_q, kept, came, cos, sin, hidden, gain_a, grad_after, w_in, result_type
        )
        return grad_in, (grad_gate, grad_up, g16, branch, grads, gain_a_part, gain_f_part)

    h1, first = forward(h0, f32)
    h2, second = forward(h1, bf16)
    output = exchange_halves(h2)
    middle, back2 = backward(exchange_halves(cotangent[0]), second, f32)
    grad_tokens, back1 = backward(middle, first, bf16)
    grad_tokens = exchange_halves(grad_tokens)

    flat = lambda a: a.reshape(-1, a.shape[-1])
    down_k, down_s = outer_rows(f, (flat(first[11]), flat(second[11])), (back1[2], back2[2]), "outer_down")
    gate_k, gate_s, up_k, up_s = outer(
        f, (first[8], second[8]), [(back1[0], back2[0]), (back1[1], back2[1])], shard_rows, "outer_ffn"
    )
    o_k, o_s = outer(f, (first[7], second[7]), [(back1[3], back2[3])], shard_rows, "outer_o")
    in_k, in_s = outer(f, (first[1], second[1]), [(back1[4], back2[4])], shard_rows, "outer_in")
    grad_down = reduce_unit(down_k, down_s)
    grad_gate = reduce_unit(gate_k, gate_s)
    grad_up = reduce_unit(up_k, up_s)
    grad_o = reduce_unit(o_k, o_s)
    grad_in = reduce_unit(in_k, in_s)
    kv_width = 2 * KV_HEADS * HEAD
    pairs = grad_in[:, :kv_width].reshape(shard_rows, KV_HEADS, 2, HEAD)
    grad_key = pairs[:, :, 0].reshape(shard_rows, KV_HEADS * HEAD)
    grad_value = pairs[:, :, 1].reshape(shard_rows, KV_HEADS * HEAD)
    grad_query = grad_in[:, kv_width : kv_width + HEADS * HEAD]
    gains = total_small(jnp.concatenate([back1[5] + back2[5], back1[6] + back2[6]], axis=0))
    share = width // 4
    gains = lax.dynamic_slice_in_dim(gains, index * share, share, 1)
    return (
        output[None], grad_tokens[None], grad_query, grad_key, grad_value, grad_o, grad_gate, grad_up,
        grad_down, gains[0], gains[1],
    )


def solution(mesh):
    split, whole = P("fsdp", None), P("dp", "fsdp", None)
    return jax.shard_map(
        per_device,
        mesh=mesh,
        in_specs=(whole, P("dp", None)) + (split,) * 7 + (P(), P(), whole),
        out_specs=(whole, whole) + (split,) * 7 + (P("fsdp"), P("fsdp")),
        check_vma=False,
    )
```

```python
import functools
import jax
import jax.numpy as jnp
from jax import lax
from jax.experimental import pallas as pl
from jax.experimental.pallas import tpu as pltpu
from jax.sharding import PartitionSpec as P

HEADS = 15
KV_HEADS = 5
HEAD = 64
GROUP = HEADS // KV_HEADS
LANES = 128
NEGATIVE = -1e30
LOG2E = 1.4426950408889634
LN2 = 0.6931471805599453
MIB = 1 << 20
f32 = jnp.float32
bf16 = jnp.bfloat16


def nn(left, right):
    return lax.dot_general(left, right, (((1,), (0,)), ((), ())), preferred_element_type=f32)


def nt(left, right):
    return lax.dot_general(left, right, (((1,), (1,)), ((), ())), preferred_element_type=f32)


def lane_index(shape):
    return lax.broadcasted_iota(jnp.int32, shape, len(shape) - 1)


def swap_halves(tile):
    low = lane_index(tile.shape) % HEAD < HEAD // 2
    return jnp.where(low, pltpu.roll(tile, LANES - HEAD // 2, 1), pltpu.roll(tile, HEAD // 2, 1))


def three_terms(column, lane):
    high = column.astype(bf16).astype(f32)
    rest = column - high
    middle = rest.astype(bf16).astype(f32)
    low = rest - middle
    return jnp.where(lane == 8, high, jnp.where(lane == 9, middle, jnp.where(lane == 10, low, 0.0)))


def gather_keys(f, fresh, pieces, key_marks, kvf):
    block = kvf.shape[1]
    half = block // 2
    for m, piece in enumerate(pieces):
        device = f ^ m
        kvf[device, :half, :LANES] = piece[0, :half, :]
        kvf[3 - device, half:, :LANES] = piece[0, half:, :]

    @pl.when(fresh)
    def _():
        for j in range(kvf.shape[0]):
            kvf[j, :, LANES:] = key_marks[j * block : (j + 1) * block, :]


def causal(shape):
    row = lax.broadcasted_iota(jnp.int32, shape, 0)
    return lane_index(shape) <= row + (shape[1] - shape[0])


def score_parts(f):
    parts = [(0, f, 1, True), (1, 3 - f, 2, True)]
    for i in range(3):
        second = i >= f
        parts.append((second.astype(jnp.int32), jnp.where(second, i - f, i), 2, False))
    return parts


def attend_kernel(f_ref, q, q_marks, key_marks, own, near, far, last, attended, marks_out, kvf, qf, scores, best, top, acc):
    g = pl.program_id(0)
    f = f_ref[0]
    half = kvf.shape[1] // 2
    gather_keys(f, g == 0, (own, near, far, last), key_marks, kvf)
    parts = score_parts(f)

    @pl.when(g == 0)
    def _():
        for b in (0, 1):
            for i in range(GROUP):
                qf[b, i * half : (i + 1) * half, LANES:] = q_marks[b * half : (b + 1) * half, :]

    for b in (0, 1):
        for i in range(GROUP):
            qf[b, i * half : (i + 1) * half, :LANES] = q[i, b * half : (b + 1) * half, :]

    for n, (b, k, size, diagonal) in enumerate(parts):
        keys = kvf[k, : size * half, :]
        for i in range(GROUP):
            rows = slice(i * half, (i + 1) * half)
            s = nt(qf[b, rows, :], keys)
            if diagonal:
                s = jnp.where(causal(s.shape), s, NEGATIVE)
            scores[n, rows, : size * half] = s
            peak = s[:, :LANES]
            for t in range(1, size * half // LANES):
                peak = jnp.maximum(peak, s[:, t * LANES : (t + 1) * LANES])
            best[n, rows, :] = peak

    for b in (0, 1):
        for i in range(GROUP):
            rows = slice(i * half, (i + 1) * half)
            peak = best[b, rows, :]
            for n in (2, 3, 4):
                peak = jnp.maximum(peak, jnp.where(parts[n][0] == b, best[n, rows, :], NEGATIVE))
            top[b, rows, :] = jnp.broadcast_to(jnp.max(peak, axis=1, keepdims=True), peak.shape)

    for n, (b, k, size, _) in enumerate(parts):
        keys = kvf[k, : size * half, :]
        for i in range(GROUP):
            rows = slice(i * half, (i + 1) * half)
            high = jnp.concatenate([top[b, rows, :]] * (size * half // LANES), axis=1)
            p = jnp.exp2(scores[n, rows, : size * half] - high).astype(bf16)
            mixed = nn(p, keys)
            if n < 2:
                acc[b, rows, :] = mixed
            else:
                acc[b, rows, :] += mixed

    lane = lane_index((half, LANES))
    for b in (0, 1):
        outer = slice(b * half, (b + 1) * half)
        for i in range(GROUP):
            rows = slice(i * half, (i + 1) * half)
            total = acc[b, rows, LANES + 8 : LANES + 9]
            out = acc[b, rows, :LANES] * (1.0 / total)
            log_total = top[b, rows, :] + jnp.log2(total)
            new_marks = q_marks[outer, :].astype(f32) + three_terms(-log_total, lane)
            marks_out[i, outer, :] = new_marks.astype(bf16)
            h = GROUP * g + i
            pair = pl.multiple_of((h // 2) * LANES, LANES)
            odd = h % 2 == 1
            turned = pltpu.roll(out, HEAD, 1)
            old = attended[outer, pl.ds(pair, LANES)].astype(f32)
            new = jnp.where(odd, jnp.where(lane >= HEAD, out, old), jnp.where(lane < HEAD, turned, 0.0))
            attended[outer, pl.ds(pair, LANES)] = new.astype(bf16)


def pair_lanes(heads_here):
    return -(-GROUP * heads_here // 2) * LANES


def attend(f, q, q_marks, key_marks, pieces, group):
    first, heads_here = group
    tokens = q.shape[1]
    blocks = key_marks.shape[0] // tokens
    rows = GROUP * tokens // 2
    piece = pl.BlockSpec((1, tokens, LANES), lambda g, f: (g, 0, 0))
    width = pair_lanes(heads_here)
    return pl.pallas_call(
        attend_kernel,
        grid_spec=pltpu.PrefetchScalarGridSpec(
            num_scalar_prefetch=1,
            grid=(heads_here,),
            in_specs=[
                pl.BlockSpec((GROUP, tokens, LANES), lambda g, f: (first + g, 0, 0)),
                pl.BlockSpec((tokens, LANES), lambda g, f: (0, 0)),
                pl.BlockSpec(key_marks.shape, lambda g, f: (0, 0)),
                piece,
                piece,
                piece,
                piece,
            ],
            out_specs=[
                pl.BlockSpec((tokens, width), lambda g, f: (0, 0)),
                pl.BlockSpec((GROUP, tokens, LANES), lambda g, f: (g, 0, 0)),
            ],
            scratch_shapes=[
                pltpu.VMEM((blocks, tokens, 2 * LANES), bf16),
                pltpu.VMEM((2, rows, 2 * LANES), bf16),
                pltpu.VMEM((5, rows, tokens), f32),
                pltpu.VMEM((5, rows, LANES), f32),
                pltpu.VMEM((2, rows, LANES), f32),
                pltpu.VMEM((2, rows, 2 * LANES), f32),
            ],
        ),
        out_shape=[
            jax.ShapeDtypeStruct((tokens, width), bf16),
            jax.ShapeDtypeStruct((GROUP * heads_here, tokens, LANES), bf16),
        ],
        compiler_params=params(48),
        cost_estimate=cost(4e10, 1e6),
        name="attend",
    )(f, q, q_marks, key_marks, *pieces)


def attend_back_kernel(
    f_ref, q, marks, key_marks, own, near, far, last, grad, attended, cos_ref, sin_ref,
    grad_q, keep, send, kvf, kv_sum, qf, df, turned, acc, ds_all, p_all,
):
    g = pl.program_id(0)
    f = f_ref[0]
    half = kvf.shape[1] // 2
    gather_keys(f, g == 0, (own, near, far, last), key_marks, kvf)
    kv_sum[...] = jnp.zeros(kv_sum.shape, f32)
    lane = lane_index((half, LANES))
    for b in (0, 1):
        outer = slice(b * half, (b + 1) * half)
        for i in range(GROUP):
            rows = slice(i * half, (i + 1) * half)
            qf[b, rows, :LANES] = q[i, outer, :]
            qf[b, rows, LANES:] = marks[i, outer, :]
            h = GROUP * g + i
            pair = pl.multiple_of((h // 2) * LANES, LANES)
            odd = h % 2 == 1
            d_tile = grad[outer, pl.ds(pair, LANES)].astype(f32)
            o_tile = attended[outer, pl.ds(pair, LANES)].astype(f32)
            mine = (lane >= HEAD) == odd
            inner = jnp.sum(jnp.where(mine, d_tile * o_tile, 0.0), axis=1, keepdims=True)
            moved = jnp.where(odd, d_tile, pltpu.roll(d_tile, HEAD, 1))
            moved = jnp.where(lane >= HEAD, moved, 0.0)
            df[b, rows, :LANES] = moved.astype(bf16)
            df[b, rows, LANES:] = three_terms(-inner, lane).astype(bf16)
            joined = moved + q[i, outer, :].astype(f32)
            turned[b, :, rows] = joined.T.astype(bf16)

    for n, (b, k, size, diagonal) in enumerate(score_parts(f)):
        wide = size * half
        keys = kvf[k, :wide, :]
        for i in range(GROUP):
            rows = slice(i * half, (i + 1) * half)
            p = jnp.exp2(nt(qf[b, rows, :], keys))
            if diagonal:
                p = jnp.where(causal(p.shape), p, 0.0)
            ds_all[rows, :wide] = (p * nt(df[b, rows, :], keys)).astype(bf16)
            p_all[rows, :wide] = p.astype(bf16)
        part = nn(ds_all[:, :wide], keys[:, :LANES])
        if n < 2:
            acc[b] = part
        else:
            acc[b] += part
        kv_sum[k, :HEAD, :wide] += nn(turned[b, :HEAD, :], ds_all[:, :wide])
        kv_sum[k, HEAD:, :wide] += nn(turned[b, HEAD:, :], p_all[:, :wide])

    scale = HEAD ** (-0.5)
    for b in (0, 1):
        outer = slice(b * half, (b + 1) * half)
        for i in range(GROUP):
            rows = slice(i * half, (i + 1) * half)
            h = GROUP * g + i
            pair = pl.multiple_of((h // 2) * LANES, LANES)
            odd = h % 2 == 1
            tile = acc[b, rows, :] * scale
            tile = tile * cos_ref[outer, :] - swap_halves(tile) * sin_ref[outer, :]
            other = pltpu.roll(tile, HEAD, 1)
            old = grad_q[outer, pl.ds(pair, LANES)].astype(f32)
            new = jnp.where(odd, jnp.where(lane >= HEAD, other, old), jnp.where(lane < HEAD, tile, 0.0))
            grad_q[outer, pl.ds(pair, LANES)] = new.astype(bf16)

    factor = jnp.where(lane < HEAD, LN2, 1.0)
    for m in range(4):
        device = f ^ m
        ref = send if m % 2 else keep
        ref[m // 2, 0, :half, :] = (kv_sum[device, :, :half].T * factor).astype(bf16)
        ref[m // 2, 0, half:, :] = (kv_sum[3 - device, :, half:].T * factor).astype(bf16)


def attend_back(f, q, marks, key_marks, pieces, grad, attended, cos, sin, group):
    first, heads_here = group
    tokens = q.shape[1]
    blocks = key_marks.shape[0] // tokens
    rows = GROUP * tokens // 2
    piece = pl.BlockSpec((1, tokens, LANES), lambda g, f: (g, 0, 0))
    width = pair_lanes(heads_here)
    whole = pl.BlockSpec((tokens, width), lambda g, f: (0, 0))
    table = pl.BlockSpec((tokens, LANES), lambda g, f: (0, 0))
    pair = pl.BlockSpec((2, 1, tokens, LANES), lambda g, f: (0, g, 0, 0))
    return pl.pallas_call(
        attend_back_kernel,
        grid_spec=pltpu.PrefetchScalarGridSpec(
            num_scalar_prefetch=1,
            grid=(heads_here,),
            in_specs=[
                pl.BlockSpec((GROUP, tokens, LANES), lambda g, f: (first + g, 0, 0)),
                pl.BlockSpec((GROUP, tokens, LANES), lambda g, f: (g, 0, 0)),
                pl.BlockSpec(key_marks.shape, lambda g, f: (0, 0)),
                piece,
                piece,
                piece,
                piece,
                whole,
                whole,
                table,
                table,
            ],
            out_specs=[whole, pair, pair],
            scratch_shapes=[
                pltpu.VMEM((blocks, tokens, 2 * LANES), bf16),
                pltpu.VMEM((blocks, LANES, tokens), f32),
                pltpu.VMEM((2, rows, 2 * LANES), bf16),
                pltpu.VMEM((2, rows, 2 * LANES), bf16),
                pltpu.VMEM((2, LANES, rows), bf16),
                pltpu.VMEM((2, rows, LANES), f32),
                pltpu.VMEM((rows, tokens), bf16),
                pltpu.VMEM((rows, tokens), bf16),
            ],
        ),
        out_shape=[
            jax.ShapeDtypeStruct((tokens, width), bf16),
            jax.ShapeDtypeStruct((2, heads_here, tokens, LANES), bf16),
            jax.ShapeDtypeStruct((2, heads_here, tokens, LANES), bf16),
        ],
        compiler_params=params(48),
        cost_estimate=cost(4e10, 1e6),
        name="attend_back",
    )(f, q, marks, key_marks, *pieces, grad, attended, cos, sin)


EPS = 1e-05
ANY = pl.BlockSpec(memory_space=pl.ANY)


def params(mib):
    return pltpu.CompilerParams(vmem_limit_bytes=mib * MIB)


def cost(flops, moved):
    return pl.CostEstimate(flops=int(flops), bytes_accessed=int(moved), transcendentals=0)


def row_copies(f, pieces, target, sems):
    rows = pieces[0].shape[0]
    return [
        pltpu.make_async_copy(
            piece, target.at[pl.ds(pl.multiple_of((f ^ m) * rows, 16), rows), :], sems.at[m]
        )
        for m, piece in enumerate(pieces)
    ]


def tile_copies(info, bit, t, pieces, target, sems):
    own, near, far_mine, far_other, last_mine, last_other = pieces
    f = info[0]
    rows, width = own.shape[0], target.shape[2]
    chip = (f >> 1) ^ t

    def copy(source, m):
        at = pl.ds(pl.multiple_of((f ^ m) * rows, 16), rows)
        return lambda: pltpu.make_async_copy(source, target.at[t, at, :], sems.at[t, m])

    columns = pl.ds(pl.multiple_of(chip * width, width), width)
    mine = chip == info[bit]
    return [
        (None, copy(own.at[:, columns], 0)),
        (None, copy(near.at[:, columns], 1)),
        (mine, copy(far_mine, 2)),
        (~mine, copy(far_other, 2)),
        (mine, copy(last_mine, 3)),
        (~mine, copy(last_other, 3)),
    ]


def start_tile(copies):
    for condition, copy in copies:
        if condition is None:
            copy().start()
        else:
            pl.when(condition)(lambda copy=copy: copy().start())


def wait_tile(copies):
    for k in (0, 1, 2, 4):
        copies[k][1]().wait()


def down_copies(info, bit, t, pieces, target, sems):
    f = info[0]
    width = pieces[0].shape[1]
    copies = []
    for m in (2 * t, 2 * t + 1):
        columns = pl.ds(pl.multiple_of(((f ^ m) & 1) * width, width), width)
        if t == 0:
            copies.append(pltpu.make_async_copy(pieces[m], target.at[t, :, columns], sems.at[m, 0]))
            continue
        for k in (0, 1):
            source = pieces[2 + 2 * (m - 2) + k]
            rows = source.shape[0]
            at = pl.ds(pl.multiple_of((info[bit] ^ k) * rows, 16), rows)
            copies.append(pltpu.make_async_copy(source, target.at[t, at, columns], sems.at[m, k]))
    return copies


def start(copies):
    for copy in copies:
        copy.start()


def wait(copies):
    for copy in copies:
        copy.wait()


def inverse_of(values):
    return lax.rsqrt(jnp.mean(values * values, axis=-1, keepdims=True) + EPS)


def norm_back(upstream, values, gain):
    inverse = inverse_of(values)
    scaled = upstream * gain
    gain_grad = jnp.sum(upstream * (values * inverse), axis=0, keepdims=True)
    middle = jnp.mean(scaled * values, axis=-1, keepdims=True)
    return inverse * scaled - (inverse * inverse * inverse * middle) * values, gain_grad


def join_kernel(first, second, out, turned):
    half = out.shape[0] // 2
    turned[:, :half] = first[...]
    turned[:, half:] = second[...]
    out[:half, :] = first[...].T
    out[half:, :] = second[...].T


def join(turned, came):
    width, half = came.shape
    spec = pl.BlockSpec((width, half), lambda i: (0, 0))
    return pl.pallas_call(
        join_kernel,
        grid=(1,),
        in_specs=[spec, spec],
        out_specs=[
            pl.BlockSpec((2 * half, width), lambda i: (0, 0)),
            pl.BlockSpec((width, 2 * half), lambda i: (0, 0)),
        ],
        out_shape=[
            jax.ShapeDtypeStruct((2 * half, width), bf16),
            jax.ShapeDtypeStruct((width, 2 * half), bf16),
        ],
        compiler_params=params(16),
        cost_estimate=cost(4e10, 1e6),
        name="join",
    )(turned, came)


def part_kernel(rows, first, second):
    half = rows.shape[0] // 2
    first[...] = rows[:half, :].T
    second[...] = rows[half:, :].T


def part(rows):
    tokens, width = rows.shape
    half = tokens // 2
    spec = pl.BlockSpec((width, half), lambda i: (0, 0))
    return pl.pallas_call(
        part_kernel,
        grid=(1,),
        in_specs=[pl.BlockSpec((tokens, width), lambda i: (0, 0))],
        out_specs=[spec, spec],
        out_shape=[jax.ShapeDtypeStruct((width, half), bf16)] * 2,
        compiler_params=params(16),
        cost_estimate=cost(4e10, 1e6),
        name="part",
    )(rows)


def pack_kernel(key_t, value_t, query, out):
    rows = []
    for g in range(KV_HEADS):
        rows += [key_t[g * HEAD : (g + 1) * HEAD, :], value_t[g * HEAD : (g + 1) * HEAD, :]]
    width = 2 * KV_HEADS * HEAD
    out[:, :width] = jnp.concatenate(rows, axis=0).T
    out[:, width : width + HEADS * HEAD] = query[...]
    out[:, width + HEADS * HEAD :] = jnp.zeros((out.shape[0], HEAD), bf16)


def pack(key, value, query):
    rows = key.shape[0]
    width = (2 * KV_HEADS + HEADS + 1) * HEAD
    full = lambda *shape: pl.BlockSpec(shape, lambda i: (0, 0))
    return pl.pallas_call(
        pack_kernel,
        grid=(1,),
        in_specs=[full(KV_HEADS * HEAD, rows)] * 2 + [full(*query.shape)],
        out_specs=full(rows, width),
        out_shape=jax.ShapeDtypeStruct((rows, width), bf16),
        compiler_params=params(16),
        cost_estimate=cost(4e10, 1e6),
        name="pack",
    )(key.T, value.T, query)


GROUPS = ((4, 1), (0, 2), (2, 2))
ORDER = (1, 2, 0)


def project_kernel(f_ref, h, gain, cos_ref, sin_ref, own, near, far, last, normed_t, q_out, *refs):
    kv_out, (w, sems) = refs[: len(GROUPS)], refs[len(GROUPS) :]
    copies = row_copies(f_ref[0], (own, near, far, last), w, sems)
    start(copies)
    hidden = h[...].astype(f32)
    normed = (hidden * inverse_of(hidden) * gain[...]).astype(bf16)
    normed_t[...] = normed.T
    cos, sin = cos_ref[...], sin_ref[...]
    lane = lane_index(cos.shape)
    kv_cos, kv_sin = jnp.where(lane < HEAD, cos, 1.0), jnp.where(lane < HEAD, sin, 0.0)
    wait(copies)
    first = KV_HEADS * LANES
    both = nn(normed, w[:, :first])
    for (start_head, heads_here), out in zip(GROUPS, kv_out):
        for i in range(heads_here):
            g = start_head + i
            tile = both[:, g * LANES : (g + 1) * LANES]
            out[i] = (tile * kv_cos + swap_halves(tile) * kv_sin).astype(bf16)
    query = nn(normed, w[:, first:])
    for p in range((HEADS + 1) // 2):
        tile = query[:, p * LANES : (p + 1) * LANES]
        tile = (tile * cos + swap_halves(tile) * sin) * (HEAD ** (-0.5) * LOG2E)
        q_out[2 * p] = jnp.where(lane < HEAD, tile, 0.0).astype(bf16)
        if 2 * p + 1 < HEADS:
            q_out[2 * p + 1] = jnp.where(lane < HEAD, pltpu.roll(tile, HEAD, 1), 0.0).astype(bf16)


def project(f, hidden, gain, cos, sin, pieces):
    tokens, width = hidden.shape
    rows, columns = pieces[0].shape
    full = lambda *shape: pl.BlockSpec(shape, lambda i, f: (0,) * len(shape))
    like = jax.ShapeDtypeStruct
    return pl.pallas_call(
        project_kernel,
        grid_spec=pltpu.PrefetchScalarGridSpec(
            num_scalar_prefetch=1,
            grid=(1,),
            in_specs=[full(tokens, width), full(1, width), full(*cos.shape), full(*sin.shape)] + [ANY] * 4,
            out_specs=[full(width, tokens), full(HEADS, tokens, LANES)]
            + [full(heads_here, tokens, LANES) for _, heads_here in GROUPS],
            scratch_shapes=[pltpu.VMEM((4 * rows, columns), bf16), pltpu.SemaphoreType.DMA((4,))],
        ),
        out_shape=[like((width, tokens), bf16), like((HEADS, tokens, LANES), bf16)]
        + [like((heads_here, tokens, LANES), bf16) for _, heads_here in GROUPS],
        compiler_params=params(40),
        cost_estimate=cost(4e10, 1e6),
        name="project",
    )(f, hidden, gain, cos, sin, *pieces)


PARTS = len(GROUPS)


def split_pieces(refs):
    return refs[:4], refs[4:10], refs[10:16], refs[16:22], refs[22:]


CHUNK = 256


def feed_kernel(f_ref, h, *refs):
    attended, gain = refs[:PARTS], refs[PARTS]
    o, gate, up, down, refs = split_pieces(refs[PARTS + 1 :])
    outs, result = refs[:6], refs[6]
    w_o, w_gate, w_up, w_down, n16, acc, *refs = refs[7:]
    after, attended_t, normed_t, gate_out, up_out, hidden_out = refs[:6]
    o_sem, gate_sem, up_sem, down_sem, out_sem = refs[6:]
    f = f_ref[0]
    tiles, depth, wide = w_gate.shape[0], 4 * o[0].shape[0], w_gate.shape[2]

    def leave(k, tile=0):
        source, target = refs[k], outs[k]
        if len(source.shape) == 3:
            source, target = source.at[tile], target.at[tile]
        return pltpu.make_async_copy(source, target, out_sem.at[k, tile])

    bring = [
        lambda: start_tile(tile_copies(f_ref, 2, 0, up, w_up, up_sem)),
        lambda: start(down_copies(f_ref, 1, 0, down, w_down, down_sem)),
        lambda: start_tile(tile_copies(f_ref, 1, 1, gate, w_gate, gate_sem)),
        lambda: start_tile(tile_copies(f_ref, 2, 1, up, w_up, up_sem)),
        lambda: start(down_copies(f_ref, 1, 1, down, w_down, down_sem)),
    ]
    start(row_copies(f, o, w_o, o_sem))
    start_tile(tile_copies(f_ref, 1, 0, gate, w_gate, gate_sem))
    att = jnp.concatenate([attended[i][...] for i in ORDER], axis=1)
    attended_t[...] = att.T
    leave(1).start()
    w_o[depth:, :] = jnp.zeros((w_o.shape[0] - depth, w_o.shape[1]), bf16)
    wait(row_copies(f, o, w_o, o_sem))
    bring.pop(0)()
    value = h[...].astype(f32) + nn(att, w_o[...])
    after[...] = value
    normed = (value * inverse_of(value) * gain[...]).astype(bf16)
    n16[...] = normed
    normed_t[...] = normed.T
    for t in range(tiles):
        wait_tile(tile_copies(f_ref, 1, t, gate, w_gate, gate_sem))
        if t == 0:
            bring.pop(0)()
        wait_tile(tile_copies(f_ref, 2, t, up, w_up, up_sem))
        for at in range(0, wide, CHUNK):
            columns = slice(at, at + CHUNK)
            gate_act = nn(n16[...], w_gate[t, :, columns])
            up_act = nn(n16[...], w_up[t, :, columns])
            hidden = gate_act * jax.nn.sigmoid(gate_act) * up_act
            gate_out[t, :, columns] = gate_act.astype(bf16)
            up_out[t, :, columns] = up_act.astype(bf16)
            hidden_out[t, :, columns] = hidden.astype(bf16)
            if bring and at < 2 * CHUNK:
                bring.pop(0)()
        if t == 0:
            leave(0).start()
            leave(2).start()
        for k in (3, 4, 5):
            leave(k, t).start()
        wait(down_copies(f_ref, 1, t, down, w_down, down_sem))
        if bring:
            bring.pop(0)()
        part = nt(hidden_out[t], w_down[t])
        acc[...] = part if t == 0 else acc[...] + part
    result[...] = (after[...] + acc[...]).astype(result.dtype)
    for k in (0, 1, 2):
        leave(k).wait()
    for t in range(tiles):
        for k in (3, 4, 5):
            leave(k, t).wait()


def weight_scratch(o, gate):
    rows, width = o.shape
    columns = gate.shape[1]
    return [
        pltpu.VMEM((4 * rows + HEAD, width), bf16),
        pltpu.VMEM((2, 4 * rows, columns // 2), bf16),
        pltpu.VMEM((2, 4 * rows, columns // 2), bf16),
        pltpu.VMEM((2, width, columns // 2), bf16),
    ]


def weight_sems():
    dma = pltpu.SemaphoreType.DMA
    return [dma((4,)), dma((2, 4)), dma((2, 4)), dma((4, 2))]


def feed(f, hidden, attended, gain, o, gate, up, down, result_type):
    tokens, width = hidden.shape
    wide = gate[0].shape[1] // 2
    lanes = (HEADS + 1) * HEAD
    full = lambda *shape: pl.BlockSpec(shape, lambda i, f: (0,) * len(shape))
    like = jax.ShapeDtypeStruct
    kept = [((tokens, width), f32), ((lanes, tokens), bf16), ((width, tokens), bf16)] + [((2, tokens, wide), bf16)] * 3
    return pl.pallas_call(
        feed_kernel,
        grid_spec=pltpu.PrefetchScalarGridSpec(
            num_scalar_prefetch=1,
            grid=(1,),
            in_specs=[full(tokens, width)] + [full(*a.shape) for a in attended] + [full(1, width)] + [ANY] * 22,
            out_specs=[ANY] * 6 + [full(tokens, width)],
            scratch_shapes=weight_scratch(o[0], gate[0])
            + [pltpu.VMEM((tokens, width), bf16), pltpu.VMEM((tokens, width), f32)]
            + [pltpu.VMEM(*k) for k in kept]
            + weight_sems()
            + [pltpu.SemaphoreType.DMA((6, 2))],
        ),
        out_shape=[like(*k) for k in kept] + [like((tokens, width), result_type)],
        compiler_params=params(56),
        cost_estimate=cost(4e10, 1e6),
        name="feed",
    )(f, hidden, *attended, gain, *o, *gate, *up, *down)


def feed_back_kernel(f_ref, g, gain, *refs):
    held = refs[:3]
    o, gate, up, down, refs = split_pieces(refs[3:])
    outs, grad_after, branch_out = refs[:2], refs[2], refs[3]
    grad_attended, gain_grad = refs[4 : 4 + PARTS], refs[4 + PARTS]
    w_o, w_gate, w_up, w_down, g16, acc, *refs = refs[5 + PARTS :]
    after, gate_act, up_act, grad_gate, grad_up, o_sem, gate_sem, up_sem, down_sem, in_sem, out_sem = refs
    f = f_ref[0]
    tiles, depth, wide = w_gate.shape[0], 4 * o[0].shape[0], w_gate.shape[2]

    def arrive(k, tile=0):
        source, target = held[k], refs[k]
        if k:
            source, target = source.at[tile], target.at[tile]
        return pltpu.make_async_copy(source, target, in_sem.at[k, tile])

    def leave(k, tile):
        return pltpu.make_async_copy(refs[3 + k].at[tile], outs[k].at[tile], out_sem.at[k, tile])

    def bring_first(t):
        start(down_copies(f_ref, 1, t, down, w_down, down_sem))
        arrive(1, t).start()
        arrive(2, t).start()

    bring_first(0)
    g16[...] = g[...].astype(bf16)
    w_o[depth:, :] = jnp.zeros((w_o.shape[0] - depth, w_o.shape[1]), bf16)
    for t in range(tiles):
        wait(down_copies(f_ref, 1, t, down, w_down, down_sem))
        arrive(1, t).wait()
        arrive(2, t).wait()
        start_tile(tile_copies(f_ref, 1, t, gate, w_gate, gate_sem))
        for at in range(0, wide, CHUNK):
            columns = slice(at, at + CHUNK)
            grad_hidden = nn(g16[...], w_down[t, :, columns])
            value = gate_act[t, :, columns].astype(f32)
            logistic = jax.nn.sigmoid(value)
            steep = logistic * (1.0 + value * (1.0 - logistic))
            grad_gate[t, :, columns] = (grad_hidden * up_act[t, :, columns].astype(f32) * steep).astype(bf16)
            grad_up[t, :, columns] = (grad_hidden * (value * logistic)).astype(bf16)
            if at == CHUNK:
                start_tile(tile_copies(f_ref, 2, t, up, w_up, up_sem))
        leave(0, t).start()
        leave(1, t).start()
        wait_tile(tile_copies(f_ref, 1, t, gate, w_gate, gate_sem))
        part = nt(grad_gate[t], w_gate[t])
        acc[...] = part if t == 0 else acc[...] + part
        wait_tile(tile_copies(f_ref, 2, t, up, w_up, up_sem))
        if t + 1 < tiles:
            bring_first(t + 1)
        else:
            arrive(0).start()
            start(row_copies(f, o, w_o, o_sem))
        part = nt(grad_up[t], w_up[t])
        acc[...] += part
    arrive(0).wait()
    wait(row_copies(f, o, w_o, o_sem))
    back, gain_part = norm_back(acc[...], after[...], gain[...])
    back = back + g[...].astype(f32)
    gain_grad[...] = gain_part
    grad_after[...] = back
    branch = back.astype(bf16)
    branch_out[...] = branch
    whole = nt(branch, w_o[...]).astype(bf16)
    at = 0
    for i in ORDER:
        lanes = grad_attended[i].shape[1]
        grad_attended[i][...] = whole[:, at : at + lanes]
        at += lanes
    for t in range(tiles):
        leave(0, t).wait()
        leave(1, t).wait()


def feed_back(f, g, after, gain, gate_act, up_act, o, gate, up, down):
    tokens, width = after.shape
    wide = gate[0].shape[1] // 2
    full = lambda *shape: pl.BlockSpec(shape, lambda i, f: (0,) * len(shape))
    like = jax.ShapeDtypeStruct
    lanes = [pair_lanes(heads_here) for _, heads_here in GROUPS]
    tile = (2, tokens, wide)
    dma = pltpu.SemaphoreType.DMA
    return pl.pallas_call(
        feed_back_kernel,
        grid_spec=pltpu.PrefetchScalarGridSpec(
            num_scalar_prefetch=1,
            grid=(1,),
            in_specs=[full(tokens, width), full(1, width)] + [ANY] * 25,
            out_specs=[ANY, ANY, full(tokens, width), full(tokens, width)]
            + [full(tokens, n) for n in lanes]
            + [full(1, width)],
            scratch_shapes=weight_scratch(o[0], gate[0])
            + [pltpu.VMEM((tokens, width), bf16), pltpu.VMEM((tokens, width), f32)]
            + [pltpu.VMEM((tokens, width), f32)]
            + [pltpu.VMEM(tile, bf16)] * 4
            + weight_sems()
            + [dma((3, 2)), dma((2, 2))],
        ),
        out_shape=[like(tile, bf16), like(tile, bf16), like((tokens, width), f32), like((tokens, width), bf16)]
        + [like((tokens, n), bf16) for n in lanes]
        + [like((1, width), f32)],
        compiler_params=params(56),
        cost_estimate=cost(4e10, 1e6),
        name="feed_back",
    )(f, g, gain, after, gate_act, up_act, *o, *gate, *up, *down)


def project_back_kernel(f_ref, *refs):
    grad_q, kept, came = refs[:PARTS], refs[PARTS : 2 * PARTS], refs[2 * PARTS : 3 * PARTS]
    cos_ref, sin_ref, h, gain, grad_after, own, near, far, last = refs[3 * PARTS : 3 * PARTS + 9]
    grads, grad_in, turned, gain_grad, w, sems = refs[3 * PARTS + 9 :]
    copies = row_copies(f_ref[0], (own, near, far, last), w, sems)
    start(copies)
    cos, sin = cos_ref[...], sin_ref[...]
    lane = lane_index(cos.shape)
    cos, sin = jnp.where(lane < HEAD, cos, 1.0), jnp.where(lane < HEAD, sin, 0.0)
    at = KV_HEADS * LANES
    for k in ORDER:
        first, heads_here = GROUPS[k]
        for i in range(heads_here):
            g = first + i
            tile = kept[k][i].astype(f32) + came[k][i].astype(f32)
            tile = tile * cos - swap_halves(tile) * sin
            grads[:, g * LANES : (g + 1) * LANES] = tile.astype(bf16)
        lanes = grad_q[k].shape[1]
        grads[:, at : at + lanes] = grad_q[k][...]
        at += lanes
    wait(copies)
    grad_normed = nt(grads[...], w[...])
    back, gain_part = norm_back(grad_normed, h[...].astype(f32), gain[...])
    gain_grad[...] = gain_part
    back = back + grad_after[...]
    grad_in[...] = back.astype(grad_in.dtype)
    turned[...] = back.astype(bf16).T


def project_back(f, grad_q, kept, came, cos, sin, hidden, gain, grad_after, pieces, result_type):
    tokens, width = hidden.shape
    rows, columns = pieces[0].shape
    full = lambda *shape: pl.BlockSpec(shape, lambda i, f: (0,) * len(shape))
    like = jax.ShapeDtypeStruct
    arrays = (*grad_q, *kept, *came, cos, sin, hidden, gain, grad_after)
    return pl.pallas_call(
        project_back_kernel,
        grid_spec=pltpu.PrefetchScalarGridSpec(
            num_scalar_prefetch=1,
            grid=(1,),
            in_specs=[full(*a.shape) for a in arrays] + [ANY] * 4,
            out_specs=[full(tokens, columns), full(tokens, width), full(width, tokens), full(1, width)],
            scratch_shapes=[pltpu.VMEM((4 * rows, columns), bf16), pltpu.SemaphoreType.DMA((4,))],
        ),
        out_shape=[
            like((tokens, columns), bf16),
            like((tokens, width), result_type),
            like((width, tokens), bf16),
            like((1, width), f32),
        ],
        compiler_params=params(40),
        cost_estimate=cost(4e10, 1e6),
        name="project_back",
    )(f, *arrays, *pieces)


def outer_tiles_kernel(f_ref, *refs, rows):
    left_first, left_second, right_first, right_second, keep, send, acc = refs
    left = jnp.concatenate([left_first[...], left_second[...]], axis=1)
    acc[...] = nn(left, jnp.concatenate([right_first[0], right_second[0]], axis=0))
    half = acc.shape[1] // 2
    for m in range(4):
        out = send if m % 2 else keep
        from_row = pl.multiple_of((f_ref[0] ^ m) * rows, 16)
        for c in (0, 1):
            out[m // 2, c] = acc[pl.ds(from_row, rows), c * half : (c + 1) * half].astype(bf16)


def outer_tiles(f, lefts, rights, rows, name):
    width, tokens = lefts[0].shape
    wide = rights[0].shape[2]
    left = pl.BlockSpec((width, tokens), lambda i, f: (0, 0))
    right = pl.BlockSpec((1, tokens, wide), lambda i, f: (i, 0, 0))
    out = pl.BlockSpec((2, 2, rows, wide // 2), lambda i, f: (0, (f[0] >> 1) ^ i, 0, 0))
    return pl.pallas_call(
        functools.partial(outer_tiles_kernel, rows=rows),
        grid_spec=pltpu.PrefetchScalarGridSpec(
            num_scalar_prefetch=1,
            grid=(2,),
            in_specs=[left, left, right, right],
            out_specs=[out, out],
            scratch_shapes=[pltpu.VMEM((width, wide), f32)],
        ),
        out_shape=[jax.ShapeDtypeStruct((2, 4, rows, wide // 2), bf16)] * 2,
        compiler_params=params(48),
        cost_estimate=cost(4e10, 1e6),
        name=name,
    )(f, *lefts, *rights)


def outer_down_kernel(f_ref, left_first, left_second, right_first, right_second, keep, send):
    left = jnp.concatenate([left_first[...], left_second[...]], axis=1)
    value = nn(left, jnp.concatenate([right_first[0], right_second[0]], axis=0))
    half = value.shape[1] // 2
    own = (f_ref[0] & 1) == 0
    lower, upper = value[:, :half], value[:, half:]
    keep[0, 0] = jnp.where(own, lower, upper).astype(bf16)
    send[0, 0] = jnp.where(own, upper, lower).astype(bf16)


def outer_down(f, lefts, rights, name):
    width, tokens = lefts[0].shape
    wide = rights[0].shape[2]
    left = pl.BlockSpec((width, tokens), lambda i, f: (0, 0))
    right = pl.BlockSpec((1, tokens, wide), lambda i, f: (i, 0, 0))
    out = pl.BlockSpec((1, 1, width, wide // 2), lambda i, f: (i, 0, 0, 0))
    return pl.pallas_call(
        outer_down_kernel,
        grid_spec=pltpu.PrefetchScalarGridSpec(
            num_scalar_prefetch=1,
            grid=(2,),
            in_specs=[left, left, right, right],
            out_specs=[out, out],
        ),
        out_shape=[jax.ShapeDtypeStruct((2, 1, width, wide // 2), bf16)] * 2,
        compiler_params=params(48),
        cost_estimate=cost(4e10, 1e6),
        name=name,
    )(f, *lefts, *rights)


def outer_kernel(f_ref, left_first, left_second, right_first, right_second, extra, keep, send, acc, *, rows):
    left = jnp.concatenate([left_first[...], left_second[...]], axis=1)
    acc[...] = nn(left, jnp.concatenate([right_first[...], right_second[...]], axis=0))
    spare = keep.shape[2] - rows
    for m in range(4):
        out = send if m % 2 else keep
        device = f_ref[0] ^ m
        out[m // 2, 0, :rows] = acc[pl.ds(pl.multiple_of(device * rows, 16), rows), :].astype(bf16)
        out[m // 2, 0, rows:] = jnp.zeros((spare, acc.shape[1]), bf16)
        out[m // 2, 0, rows:, : extra.shape[2]] = extra[device]


def outer(f, lefts, rights, extra, rows, name):
    width, tokens = lefts[0].shape
    columns = rights[0].shape[1]
    padded = rows + extra.shape[1]
    full = lambda *shape: pl.BlockSpec(shape, lambda i, f: (0,) * len(shape))
    height = width if width % (4 * rows) == 0 else width
    return pl.pallas_call(
        functools.partial(outer_kernel, rows=rows),
        grid_spec=pltpu.PrefetchScalarGridSpec(
            num_scalar_prefetch=1,
            grid=(1,),
            in_specs=[full(width, tokens)] * 2 + [full(tokens, columns)] * 2 + [full(*extra.shape)],
            out_specs=[full(2, 1, padded, columns)] * 2,
            scratch_shapes=[pltpu.VMEM((height, columns), f32)],
        ),
        out_shape=[jax.ShapeDtypeStruct((2, 1, padded, columns), bf16)] * 2,
        compiler_params=params(48),
        cost_estimate=cost(4e10, 1e6),
        name=name,
    )(f, *lefts, *rights, extra)


def unpack_kernel(total, key_t, value_t, query):
    rows = query.shape[0]
    width = 2 * KV_HEADS * HEAD
    turned = total[:rows, :width].astype(f32).T
    for g in range(KV_HEADS):
        key_t[g * HEAD : (g + 1) * HEAD, :] = turned[2 * g * HEAD : (2 * g + 1) * HEAD, :]
        value_t[g * HEAD : (g + 1) * HEAD, :] = turned[(2 * g + 1) * HEAD : (2 * g + 2) * HEAD, :]
    query[...] = total[:rows, width : width + HEADS * HEAD].astype(f32)


def unpack(total, rows):
    full = lambda *shape: pl.BlockSpec(shape, lambda i: (0, 0))
    like = jax.ShapeDtypeStruct
    side = (KV_HEADS * HEAD, rows)
    key_t, value_t, query = pl.pallas_call(
        unpack_kernel,
        grid=(1,),
        in_specs=[full(*total.shape)],
        out_specs=[full(*side), full(*side), full(rows, HEADS * HEAD)],
        out_shape=[like(side, f32), like(side, f32), like((rows, HEADS * HEAD), f32)],
        compiler_params=params(16),
        cost_estimate=cost(4e10, 1e6),
        name="unpack",
    )(total)
    return key_t.T, value_t.T, query


def flip(array, axis, bit):
    size = lax.axis_size(axis)
    return lax.ppermute(array, axis, [(i, i ^ bit) for i in range(size)])


def add(left, right):
    return left.astype(f32) + right.astype(f32)


def levels_of(size):
    bits = size.bit_length() - 1
    levels = [(0, 2)] if bits else []
    at = 1
    while at < bits:
        step = min(2, bits - at)
        levels.append((at, 1 << step))
        at += step
    return levels


def cut(array, count):
    blocks, rows, columns = array.shape
    outer = next(n for n in (4, 2, 1) if n <= count and blocks % n == 0)
    inner = count // outer
    array = array.reshape(outer, blocks // outer, inner, rows // inner, columns)
    return [array[i // inner, :, i % inner] for i in range(count)]


def glue(parts, shape):
    count = len(parts)
    outer = next(n for n in (4, 2, 1) if n <= count and shape[0] % n == 0)
    inner = count // outer
    rows = [jnp.concatenate(parts[i * inner : (i + 1) * inner], axis=1) for i in range(outer)]
    return jnp.concatenate(rows, axis=0).reshape(shape)


def pick(parts, index):
    while len(parts) > 1:
        odd = index % 2 == 1
        parts = [jnp.where(odd, parts[i + 1], parts[i]) for i in range(0, len(parts), 2)]
        index = index // 2
    return parts[0]


def reduction(keep, send, halves):
    shape = keep.shape[1:]
    (near,) = yield [(send, "fsdp", 1)]
    far = [add(k, n).astype(bf16) for k, n in zip(cut(keep[1], halves), cut(near[1], halves))]
    came = []
    for piece in far:
        came += yield [(piece, "fsdp", 2)]
    came = glue(came, shape) if halves > 1 else came[0]
    part = add(keep[0], near[0]) + came.astype(f32)
    index = lax.axis_index("dp")
    shapes = []
    for bit, count in levels_of(lax.axis_size("dp")):
        shapes.append(part.shape)
        parts = cut(part, count)
        mine = (index >> bit) % count
        came = yield [(pick(parts, mine ^ j).astype(bf16), "dp", j << bit) for j in range(1, count)]
        part = pick(parts, mine).astype(f32)
        for other in came:
            part = part + other.astype(f32)
    part = part.astype(bf16)
    for (bit, count), wide in zip(reversed(levels_of(lax.axis_size("dp"))), reversed(shapes)):
        came = yield [(part, "dp", j << bit) for j in range(1, count)]
        mine = (index >> bit) % count
        held = [part] + came
        part = glue([pick(held, mine ^ p) for p in range(count)], wide)
    return part


class Unit:
    def __init__(self, keep, send, halves=1):
        self.steps = reduction(keep, send, halves)
        self.asks = next(self.steps)
        self.total = None

    def take(self, came):
        try:
            self.asks = self.steps.send(came)
        except StopIteration as end:
            self.asks, self.total = [], end.value


class Clock:
    def __init__(self, f):
        self.f = f
        self.before = []

    def phase(self, moves=(), work=None, units=(), extra=()):
        asks = list(moves)
        for unit in units:
            asks += unit.asks
        gated = lax.optimization_barrier((self.f, *(a[0] for a in asks), *extra, *self.before))
        came = [flip(g, axis, bit) for g, (_, axis, bit) in zip(gated[1:], asks)]
        done = None if work is None else work(gated[0])
        self.before = list(came) + ([] if done is None else [jax.tree.leaves(done)[0]])
        at = len(moves)
        for unit in units:
            count = len(unit.asks)
            unit.take(came[at : at + count])
            at += count
        return came[: len(moves)], done


def half_for(shard, low_first, dim):
    width = shard.shape[dim] // 2
    low = lax.slice_in_dim(shard, 0, width, axis=dim)
    high = lax.slice_in_dim(shard, width, 2 * width, axis=dim)
    return jnp.where(low_first, low, high)


def per_device(
    tokens, seq_cuts, w_query, w_key, w_value, w_output, w_gate, w_up, w_down, gain_attn, gain_ffn, cotangent
):
    rows, width = tokens.shape[1], tokens.shape[2]
    half = rows // 2
    index = lax.axis_index("fsdp")
    replica = lax.axis_index("dp")
    f = jnp.stack([index, replica % 2, replica // 2 % 2]).astype(jnp.int32)
    count = rows * lax.axis_size("fsdp")
    shard_rows = w_key.shape[0]
    core, y = ("fsdp", 1), ("fsdp", 2)
    side = (("dp", 1), ("dp", 2))

    bounds = seq_cuts[0]
    within = jnp.arange(half, dtype=jnp.int32)
    local = jnp.concatenate([2 * index * half + within, (7 - 2 * index) * half + within]).astype(jnp.int32)
    every = jnp.arange(count, dtype=jnp.int32)
    passed = local[:, None] >= bounds[None, :]
    docs = jnp.sum(passed.astype(jnp.int32), axis=1)
    positions = local - jnp.max(jnp.where(passed, bounds[None, :], 0), axis=1)
    key_docs = jnp.sum((every[:, None] >= bounds[None, :]).astype(jnp.int32), axis=1)
    lane = jnp.arange(LANES, dtype=jnp.int32)[None, :]
    one = ((lane == key_docs[:, None]) & (lane < 4)) | ((lane >= 8) & (lane < 11))
    key_marks = one.astype(bf16)
    q_marks = jnp.where((lane < 4) & (lane != docs[:, None]), NEGATIVE, 0.0).astype(bf16)
    frequency = jnp.power(10000.0, -2.0 * jnp.arange(HEAD // 2, dtype=f32) / HEAD)
    angle = positions.astype(f32)[:, None] * frequency[None, :]
    cosine, sine = jnp.cos(angle), jnp.sin(angle)
    cos = jnp.concatenate([cosine] * 4, axis=1)
    sin = jnp.concatenate([-sine, sine] * 2, axis=1)
    gain_a, gain_f = gain_attn[None, :], gain_ffn[None, :]

    clock = Clock(f)
    tokens_t, cotangent_t, down_t = tokens[0].T, cotangent[0].T, w_down.T
    shards = {"gate": w_gate, "up": w_up, "down": down_t}
    bit_of, dim_of = {"gate": 0, "up": 1, "down": 0}, {"gate": 1, "up": 1, "down": 0}
    across = lambda name: (half_for(shards[name], f[1 + bit_of[name]] == 0, dim_of[name]), *y)

    w_own = pack(w_key, w_value, w_query)
    (w_far, w_near, other_tokens), _ = clock.phase([(w_own, *y), (w_own, *core), (tokens_t[:, half:], "fsdp", 3)])
    (w_last, w_o_far), (h0, _) = clock.phase(
        [(w_far, *core), (w_output, *y)], lambda turn: join(tokens_t, other_tokens), extra=(key_marks, q_marks, cos, sin)
    )
    w_in = (w_own, w_near, w_far, w_last)

    def attend_phases(hidden, first, moves):
        came = []
        got, (normed_t, q, *parts) = clock.phase(first, lambda turn: project(turn, hidden, gain_a, cos, sin, w_in))
        came.append(got)
        a, b, c = parts
        got, _ = clock.phase([(a, *y), (a, *core), (b, *core)] + moves[0](came))
        a_far, a_near, b_near = got[:3]
        came.append(got[3:])
        got, _ = clock.phase([(a_far, *core), (b, *y), (c, *core)] + moves[1](came))
        a_last, b_far, c_near = got[:3]
        came.append(got[3:])
        gathered = [(a, a_near, a_far, a_last)]
        attended, marks = [], []

        def call(k):
            return lambda turn: attend(turn, q, q_marks, key_marks, gathered[k], GROUPS[k])

        got, (x, m) = clock.phase([(b_far, *core), (c, *y)] + moves[2](came), call(0))
        attended.append(x), marks.append(m)
        b_last, c_far = got[:2]
        came.append(got[2:])
        gathered.append((b, b_near, b_far, b_last))
        got, (x, m) = clock.phase([(c_far, *core)] + moves[3](came), call(1))
        attended.append(x), marks.append(m)
        came.append(got[1:])
        gathered.append((c, c_near, c_far, got[0]))
        got, (x, m) = clock.phase(moves[4](came), call(2))
        attended.append(x), marks.append(m)
        came.append(got)
        return (normed_t, q, gathered, attended, marks), came

    def feed_phase(hidden, weights, run, result_type):
        normed_t, q, gathered, attended, marks = run
        _, (after, attended_t, normed_ffn_t, gate_act, up_act, hidden_act, result) = clock.phase(
            (), lambda turn: feed(turn, hidden, attended, gain_f, *weights, result_type)
        )
        return result, (
            hidden, normed_t, q, gathered, attended, marks, after, attended_t, normed_ffn_t, gate_act, up_act, hidden_act,
        )

    none = lambda came: []
    run, came = attend_phases(
        h0,
        [across("gate")],
        (
            lambda came: [(w_o_far, *core)],
            lambda came: [(came[0][0], *side[0])],
            lambda came: [across("up")],
            lambda came: [across("down"), (came[3][0], *side[1])],
            lambda came: [(came[4][0], *side[0])] + [(shards[n], *core) for n in shards] + [(w_output, *core)],
        ),
    )
    fars = {"gate": (came[0][0], came[2][0]), "up": (came[3][0], came[4][1]), "down": (came[4][0], came[5][0])}
    nears = dict(zip(shards, came[5][1:4]))
    lasts, _ = clock.phase([(x, *core) for n in shards for x in fars[n]])
    lasts = {n: tuple(lasts[2 * i : 2 * i + 2]) for i, n in enumerate(shards)}
    o = (w_output, came[5][4], w_o_far, came[1][0])
    weights = (o,) + tuple((shards[n], nears[n], *fars[n], *lasts[n]) for n in ("gate", "up", "down"))
    h1, first = feed_phase(h0, weights, run, f32)

    run, came = attend_phases(h1, [], (none, none, none, lambda came: [(cotangent_t[:, half:], "fsdp", 3)], none))
    other_cotangent = came[4][0]
    h2, second = feed_phase(h1, weights, run, bf16)
    _, (cot, cot_turned) = clock.phase((), lambda turn: join(cotangent_t, other_cotangent))

    def feed_back_work(g, stored):
        return lambda turn: feed_back(turn, g, stored[6], gain_f, stored[9], stored[10], *weights)

    BACK = (1, 2, 0)

    def back_phases(grad_attended, stored, beside):
        q, gathered, attended, marks = stored[2], stored[3], stored[4], stored[5]
        grad_q, kept, far = [None] * PARTS, [None] * PARTS, [None] * PARTS
        extra = []

        def call(k):
            return lambda turn: attend_back(
                turn, q, marks[k], key_marks, gathered[k], grad_attended[k], attended[k], cos, sin, GROUPS[k]
            )

        def sums(k, keep, near):
            kept[k] = add(keep[0], near[0]).astype(bf16)
            return add(keep[1], near[1]).astype(bf16)

        b, c, a = BACK
        moves, units = beside(0)
        got, (grad_q[b], b_keep, b_send) = clock.phase(moves, call(b), units)
        extra += got
        moves, units = beside(1)
        got, (grad_q[c], c_keep, c_send) = clock.phase([(b_send, *core)] + moves, call(c), units)
        extra += got[1:]
        b_sum = sums(b, b_keep, got[0])
        moves, units = beside(2)
        got, (grad_q[a], a_keep, a_send) = clock.phase([(b_sum, *y), (c_send, *core)] + moves, call(a), units)
        far[b] = got[0]
        extra += got[2:]
        c_sum = sums(c, c_keep, got[1])
        moves, units = beside(3)
        got, _ = clock.phase([(c_sum, *y), (a_send, *core)] + moves, None, units)
        far[c] = got[0]
        extra += got[2:]
        a_sum = sums(a, a_keep, got[1])
        moves, units = beside(4)
        got, _ = clock.phase([(a_sum, *y)] + moves, None, units)
        far[a] = got[0]
        extra += got[1:]
        return (grad_q, kept, far), extra

    def project_back_work(parts, stored, grad_after, result_type):
        return lambda turn: project_back(
            turn, *parts, cos, sin, stored[0], gain_a, grad_after, w_in, result_type
        )

    _, fed2 = clock.phase((), feed_back_work(cot, second))
    out_first, out_second = part(h2)
    parts, extra = back_phases(
        fed2[4 : 4 + PARTS], second, lambda k: ([(out_second, "fsdp", 3)] if k == 0 else [], ())
    )
    output = jnp.concatenate([out_first, extra[0]], axis=1).T
    _, (grads2, middle, middle_turned, gain_a2) = clock.phase((), project_back_work(parts, second, fed2[2], f32))

    _, down_pair = clock.phase(
        (), lambda turn: outer_down(turn, (middle_turned, cot_turned), (first[11], second[11]), "outer_down")
    )
    down = Unit(*down_pair, 2)
    _, fed1 = clock.phase((), feed_back_work(middle, first), (down,))

    def outer_work(i, name):
        return lambda turn: outer_tiles(turn, (first[8], second[8]), (fed1[i], fed2[i]), shard_rows, name)

    nothing = jnp.zeros((4, 16, LANES), bf16)
    _, gate_pair = clock.phase((), outer_work(0, "outer_gate"), (down,))
    gate = Unit(*gate_pair, 2)
    _, up_pair = clock.phase((), outer_work(1, "outer_up"), (down, gate))
    up = Unit(*up_pair, 2)
    _, o_pair = clock.phase(
        (),
        lambda turn: outer(turn, (first[7], second[7]), (fed1[3], fed2[3]), nothing, shard_rows, "outer_o"),
        (down, up),
    )
    out = Unit(*o_pair)
    plan = ((gate, down, out), (gate, down), (down,), (), (gate,))
    parts, _ = back_phases(fed1[4 : 4 + PARTS], first, lambda k: ([], plan[k]))
    _, (grads1, grad_tokens, _, gain_a1) = clock.phase(
        (), project_back_work(parts, first, fed1[2], bf16), (up, gate)
    )
    gains = jnp.concatenate([gain_a1 + gain_a2, fed1[4 + PARTS] + fed2[4 + PARTS]], axis=0)
    gains = gains.reshape(2, 4, width // 4).transpose(1, 0, 2).astype(bf16)
    gains = jnp.pad(gains, ((0, 0), (0, 14), (0, 256 - width // 4)))
    _, in_pair = clock.phase(
        (),
        lambda turn: outer(turn, (first[1], second[1]), (grads1, grads2), gains, shard_rows, "outer_in"),
        (up, gate),
    )
    into = Unit(*in_pair)
    back_half, back_send = part(grad_tokens)
    clock.phase((), None, (into, gate, up))
    clock.phase((), None, (into, up))
    clock.phase((), None, (out, into, up))
    clock.phase((), None, (out, into, up))
    (other_tokens,), _ = clock.phase([(back_send, "fsdp", 3)], None, (out, into))
    grad_tokens = jnp.concatenate([back_half, other_tokens], axis=1).T
    units = (down, gate, up, out, into)
    while any(unit.asks for unit in units):
        clock.phase((), None, [unit for unit in units if unit.asks])

    grad_down = down.total[0].T.astype(f32)
    wide = lambda unit: jnp.concatenate([unit.total[i] for i in range(4)], axis=1).astype(f32)
    grad_gate, grad_up = wide(gate), wide(up)
    grad_o = out.total[0, :shard_rows].astype(f32)
    total = into.total[0]
    grad_key, grad_value, grad_query = unpack(total, shard_rows)
    gains = total[shard_rows : shard_rows + 2, : width // 4].astype(f32)
    return (
        output[None], grad_tokens[None], grad_query, grad_key, grad_value, grad_o, grad_gate, grad_up,
        grad_down, gains[0], gains[1],
    )


def solution(mesh):
    split, whole = P("fsdp", None), P("dp", "fsdp", None)
    return jax.shard_map(
        per_device,
        mesh=mesh,
        in_specs=(whole, P("dp", None)) + (split,) * 7 + (P(), P(), whole),
        out_specs=(whole, whole) + (split,) * 7 + (P("fsdp"), P("fsdp")),
        check_vma=False,
    )
```

```python
import functools
import jax
import jax.numpy as jnp
from jax import lax
from jax.experimental import pallas as pl
from jax.experimental.pallas import tpu as pltpu
from jax.sharding import PartitionSpec as P

HEADS = 15
KV_HEADS = 5
HEAD = 64
GROUP = HEADS // KV_HEADS
LANES = 128
NEGATIVE = -1e30
LOG2E = 1.4426950408889634
LN2 = 0.6931471805599453
MIB = 1 << 20
f32 = jnp.float32
bf16 = jnp.bfloat16


def nn(left, right):
    return lax.dot_general(left, right, (((1,), (0,)), ((), ())), preferred_element_type=f32)


def nt(left, right):
    return lax.dot_general(left, right, (((1,), (1,)), ((), ())), preferred_element_type=f32)


def lane_index(shape):
    return lax.broadcasted_iota(jnp.int32, shape, len(shape) - 1)


def swap_halves(tile):
    low = lane_index(tile.shape) % HEAD < HEAD // 2
    return jnp.where(low, pltpu.roll(tile, LANES - HEAD // 2, 1), pltpu.roll(tile, HEAD // 2, 1))


def three_terms(column, lane):
    high = column.astype(bf16).astype(f32)
    rest = column - high
    middle = rest.astype(bf16).astype(f32)
    low = rest - middle
    return jnp.where(lane == 8, high, jnp.where(lane == 9, middle, jnp.where(lane == 10, low, 0.0)))


def gather_keys(f, fresh, pieces, key_marks, kvf):
    block = kvf.shape[1]
    half = block // 2
    for m, piece in enumerate(pieces):
        device = f ^ m
        kvf[device, :half, :LANES] = piece[0, :half, :]
        kvf[3 - device, half:, :LANES] = piece[0, half:, :]

    @pl.when(fresh)
    def _():
        for j in range(kvf.shape[0]):
            kvf[j, :, LANES:] = key_marks[j * block : (j + 1) * block, :]


def causal(shape):
    row = lax.broadcasted_iota(jnp.int32, shape, 0)
    return lane_index(shape) <= row + (shape[1] - shape[0])


def score_parts(f):
    parts = [(0, f, 1, True), (1, 3 - f, 2, True)]
    for i in range(3):
        second = i >= f
        parts.append((second.astype(jnp.int32), jnp.where(second, i - f, i), 2, False))
    return parts


def attend_kernel(f_ref, q, q_marks, key_marks, own, near, far, last, attended, marks_out, kvf, qf, scores, best, top, acc):
    g = pl.program_id(0)
    f = f_ref[0]
    half = kvf.shape[1] // 2
    gather_keys(f, g == 0, (own, near, far, last), key_marks, kvf)
    parts = score_parts(f)

    @pl.when(g == 0)
    def _():
        for b in (0, 1):
            for i in range(GROUP):
                qf[b, i * half : (i + 1) * half, LANES:] = q_marks[b * half : (b + 1) * half, :]

    for b in (0, 1):
        for i in range(GROUP):
            qf[b, i * half : (i + 1) * half, :LANES] = q[i, b * half : (b + 1) * half, :]

    for n, (b, k, size, diagonal) in enumerate(parts):
        keys = kvf[k, : size * half, :]
        for i in range(GROUP):
            rows = slice(i * half, (i + 1) * half)
            s = nt(qf[b, rows, :], keys)
            if diagonal:
                s = jnp.where(causal(s.shape), s, NEGATIVE)
            scores[n, rows, : size * half] = s
            peak = s[:, :LANES]
            for t in range(1, size * half // LANES):
                peak = jnp.maximum(peak, s[:, t * LANES : (t + 1) * LANES])
            best[n, rows, :] = peak

    for b in (0, 1):
        for i in range(GROUP):
            rows = slice(i * half, (i + 1) * half)
            peak = best[b, rows, :]
            for n in (2, 3, 4):
                peak = jnp.maximum(peak, jnp.where(parts[n][0] == b, best[n, rows, :], NEGATIVE))
            top[b, rows, :] = jnp.broadcast_to(jnp.max(peak, axis=1, keepdims=True), peak.shape)

    for n, (b, k, size, _) in enumerate(parts):
        keys = kvf[k, : size * half, :]
        for i in range(GROUP):
            rows = slice(i * half, (i + 1) * half)
            high = jnp.concatenate([top[b, rows, :]] * (size * half // LANES), axis=1)
            p = jnp.exp2(scores[n, rows, : size * half] - high).astype(bf16)
            mixed = nn(p, keys)
            if n < 2:
                acc[b, rows, :] = mixed
            else:
                acc[b, rows, :] += mixed

    lane = lane_index((half, LANES))
    for b in (0, 1):
        outer = slice(b * half, (b + 1) * half)
        for i in range(GROUP):
            rows = slice(i * half, (i + 1) * half)
            total = acc[b, rows, LANES + 8 : LANES + 9]
            out = acc[b, rows, :LANES] * (1.0 / total)
            log_total = top[b, rows, :] + jnp.log2(total)
            new_marks = q_marks[outer, :].astype(f32) + three_terms(-log_total, lane)
            marks_out[i, outer, :] = new_marks.astype(bf16)
            h = GROUP * g + i
            pair = pl.multiple_of((h // 2) * LANES, LANES)
            odd = h % 2 == 1
            turned = pltpu.roll(out, HEAD, 1)
            old = attended[outer, pl.ds(pair, LANES)].astype(f32)
            new = jnp.where(odd, jnp.where(lane >= HEAD, out, old), jnp.where(lane < HEAD, turned, 0.0))
            attended[outer, pl.ds(pair, LANES)] = new.astype(bf16)


def pair_lanes(heads_here):
    return -(-GROUP * heads_here // 2) * LANES


def attend(f, q, q_marks, key_marks, pieces, group):
    first, heads_here = group
    tokens = q.shape[1]
    blocks = key_marks.shape[0] // tokens
    rows = GROUP * tokens // 2
    piece = pl.BlockSpec((1, tokens, LANES), lambda g, f: (g, 0, 0))
    width = pair_lanes(heads_here)
    return pl.pallas_call(
        attend_kernel,
        grid_spec=pltpu.PrefetchScalarGridSpec(
            num_scalar_prefetch=1,
            grid=(heads_here,),
            in_specs=[
                pl.BlockSpec((GROUP, tokens, LANES), lambda g, f: (first + g, 0, 0)),
                pl.BlockSpec((tokens, LANES), lambda g, f: (0, 0)),
                pl.BlockSpec(key_marks.shape, lambda g, f: (0, 0)),
                piece,
                piece,
                piece,
                piece,
            ],
            out_specs=[
                pl.BlockSpec((tokens, width), lambda g, f: (0, 0)),
                pl.BlockSpec((GROUP, tokens, LANES), lambda g, f: (g, 0, 0)),
            ],
            scratch_shapes=[
                pltpu.VMEM((blocks, tokens, 2 * LANES), bf16),
                pltpu.VMEM((2, rows, 2 * LANES), bf16),
                pltpu.VMEM((5, rows, tokens), f32),
                pltpu.VMEM((5, rows, LANES), f32),
                pltpu.VMEM((2, rows, LANES), f32),
                pltpu.VMEM((2, rows, 2 * LANES), f32),
            ],
        ),
        out_shape=[
            jax.ShapeDtypeStruct((tokens, width), bf16),
            jax.ShapeDtypeStruct((GROUP * heads_here, tokens, LANES), bf16),
        ],
        compiler_params=params(26),
        cost_estimate=cost(4e10, 1e6),
        name="attend",
    )(f, q, q_marks, key_marks, *pieces)


def attend_back_kernel(
    f_ref, q, marks, key_marks, own, near, far, last, grad, attended, cos_ref, sin_ref,
    grad_q, keep, send, kvf, kv_sum, qf, df, turned, acc, ds_all, p_all,
):
    g = pl.program_id(0)
    f = f_ref[0]
    half = kvf.shape[1] // 2
    gather_keys(f, g == 0, (own, near, far, last), key_marks, kvf)
    kv_sum[...] = jnp.zeros(kv_sum.shape, f32)
    lane = lane_index((half, LANES))
    for b in (0, 1):
        outer = slice(b * half, (b + 1) * half)
        for i in range(GROUP):
            rows = slice(i * half, (i + 1) * half)
            qf[b, rows, :LANES] = q[i, outer, :]
            qf[b, rows, LANES:] = marks[i, outer, :]
            h = GROUP * g + i
            pair = pl.multiple_of((h // 2) * LANES, LANES)
            odd = h % 2 == 1
            d_tile = grad[outer, pl.ds(pair, LANES)].astype(f32)
            o_tile = attended[outer, pl.ds(pair, LANES)].astype(f32)
            mine = (lane >= HEAD) == odd
            inner = jnp.sum(jnp.where(mine, d_tile * o_tile, 0.0), axis=1, keepdims=True)
            moved = jnp.where(odd, d_tile, pltpu.roll(d_tile, HEAD, 1))
            moved = jnp.where(lane >= HEAD, moved, 0.0)
            df[b, rows, :LANES] = moved.astype(bf16)
            df[b, rows, LANES:] = three_terms(-inner, lane).astype(bf16)
            joined = moved + q[i, outer, :].astype(f32)
            turned[b, :, rows] = joined.T.astype(bf16)

    for n, (b, k, size, diagonal) in enumerate(score_parts(f)):
        wide = size * half
        keys = kvf[k, :wide, :]
        for i in range(GROUP):
            rows = slice(i * half, (i + 1) * half)
            p = jnp.exp2(nt(qf[b, rows, :], keys))
            if diagonal:
                p = jnp.where(causal(p.shape), p, 0.0)
            ds_all[rows, :wide] = (p * nt(df[b, rows, :], keys)).astype(bf16)
            p_all[rows, :wide] = p.astype(bf16)
        part = nn(ds_all[:, :wide], keys[:, :LANES])
        if n < 2:
            acc[b] = part
        else:
            acc[b] += part
        kv_sum[k, :HEAD, :wide] += nn(turned[b, :HEAD, :], ds_all[:, :wide])
        kv_sum[k, HEAD:, :wide] += nn(turned[b, HEAD:, :], p_all[:, :wide])

    scale = HEAD ** (-0.5)
    for b in (0, 1):
        outer = slice(b * half, (b + 1) * half)
        for i in range(GROUP):
            rows = slice(i * half, (i + 1) * half)
            h = GROUP * g + i
            pair = pl.multiple_of((h // 2) * LANES, LANES)
            odd = h % 2 == 1
            tile = acc[b, rows, :] * scale
            tile = tile * cos_ref[outer, :] - swap_halves(tile) * sin_ref[outer, :]
            other = pltpu.roll(tile, HEAD, 1)
            old = grad_q[outer, pl.ds(pair, LANES)].astype(f32)
            new = jnp.where(odd, jnp.where(lane >= HEAD, other, old), jnp.where(lane < HEAD, tile, 0.0))
            grad_q[outer, pl.ds(pair, LANES)] = new.astype(bf16)

    factor = jnp.where(lane < HEAD, LN2, 1.0)
    for m in range(4):
        device = f ^ m
        ref = send if m % 2 else keep
        ref[m // 2, 0, :half, :] = (kv_sum[device, :, :half].T * factor).astype(bf16)
        ref[m // 2, 0, half:, :] = (kv_sum[3 - device, :, half:].T * factor).astype(bf16)


def attend_back(f, q, marks, key_marks, pieces, grad, attended, cos, sin, group):
    first, heads_here = group
    tokens = q.shape[1]
    blocks = key_marks.shape[0] // tokens
    rows = GROUP * tokens // 2
    piece = pl.BlockSpec((1, tokens, LANES), lambda g, f: (g, 0, 0))
    width = pair_lanes(heads_here)
    whole = pl.BlockSpec((tokens, width), lambda g, f: (0, 0))
    table = pl.BlockSpec((tokens, LANES), lambda g, f: (0, 0))
    pair = pl.BlockSpec((2, 1, tokens, LANES), lambda g, f: (0, g, 0, 0))
    return pl.pallas_call(
        attend_back_kernel,
        grid_spec=pltpu.PrefetchScalarGridSpec(
            num_scalar_prefetch=1,
            grid=(heads_here,),
            in_specs=[
                pl.BlockSpec((GROUP, tokens, LANES), lambda g, f: (first + g, 0, 0)),
                pl.BlockSpec((GROUP, tokens, LANES), lambda g, f: (g, 0, 0)),
                pl.BlockSpec(key_marks.shape, lambda g, f: (0, 0)),
                piece,
                piece,
                piece,
                piece,
                whole,
                whole,
                table,
                table,
            ],
            out_specs=[whole, pair, pair],
            scratch_shapes=[
                pltpu.VMEM((blocks, tokens, 2 * LANES), bf16),
                pltpu.VMEM((blocks, LANES, tokens), f32),
                pltpu.VMEM((2, rows, 2 * LANES), bf16),
                pltpu.VMEM((2, rows, 2 * LANES), bf16),
                pltpu.VMEM((2, LANES, rows), bf16),
                pltpu.VMEM((2, rows, LANES), f32),
                pltpu.VMEM((rows, tokens), bf16),
                pltpu.VMEM((rows, tokens), bf16),
            ],
        ),
        out_shape=[
            jax.ShapeDtypeStruct((tokens, width), bf16),
            jax.ShapeDtypeStruct((2, heads_here, tokens, LANES), bf16),
            jax.ShapeDtypeStruct((2, heads_here, tokens, LANES), bf16),
        ],
        compiler_params=params(22),
        cost_estimate=cost(4e10, 1e6),
        name="attend_back",
    )(f, q, marks, key_marks, *pieces, grad, attended, cos, sin)


EPS = 1e-05
ANY = pl.BlockSpec(memory_space=pl.ANY)


def params(mib):
    return pltpu.CompilerParams(vmem_limit_bytes=mib * MIB)


def cost(flops, moved):
    return pl.CostEstimate(flops=int(flops), bytes_accessed=int(moved), transcendentals=0)


def row_copies(f, pieces, target, sems):
    rows = pieces[0].shape[0]
    return [
        pltpu.make_async_copy(
            piece, target.at[pl.ds(pl.multiple_of((f ^ m) * rows, 16), rows), :], sems.at[m]
        )
        for m, piece in enumerate(pieces)
    ]


def side_copies(info, bit, pieces, target, sems):
    f = info[0]
    rows = pieces[0].shape[0]
    copies = []
    for k, (m, which) in enumerate(((0, None), (1, None), (2, 0), (2, 1), (3, 0), (3, 1))):
        at = pl.ds(pl.multiple_of((f ^ m) * rows, 16), rows)
        if which is None:
            place = target.at[at, :]
        else:
            width = pieces[k].shape[1]
            place = target.at[at, pl.ds(pl.multiple_of((info[bit] ^ which) * width, width), width)]
        copies.append(pltpu.make_async_copy(pieces[k], place, sems.at[k]))
    return copies


def down_copies(info, bit, pieces, target, sems):
    f = info[0]
    width = pieces[0].shape[1]
    copies = []
    for k, (m, which) in enumerate(((0, None), (1, None), (2, 0), (2, 1), (3, 0), (3, 1))):
        at = pl.ds(pl.multiple_of((f ^ m) * width, width), width)
        if which is None:
            place = target.at[:, at]
        else:
            rows = pieces[k].shape[0]
            place = target.at[pl.ds(pl.multiple_of((info[bit] ^ which) * rows, 16), rows), at]
        copies.append(pltpu.make_async_copy(pieces[k], place, sems.at[k]))
    return copies


def start(copies):
    for copy in copies:
        copy.start()


def wait(copies):
    for copy in copies:
        copy.wait()


def inverse_of(values):
    return lax.rsqrt(jnp.mean(values * values, axis=-1, keepdims=True) + EPS)


def norm_back(upstream, values, gain):
    inverse = inverse_of(values)
    scaled = upstream * gain
    gain_grad = jnp.sum(upstream * (values * inverse), axis=0, keepdims=True)
    middle = jnp.mean(scaled * values, axis=-1, keepdims=True)
    return inverse * scaled - (inverse * inverse * inverse * middle) * values, gain_grad


def join_kernel(first, second, out, turned):
    half = out.shape[0] // 2
    turned[:, :half] = first[...]
    turned[:, half:] = second[...]
    out[:half, :] = first[...].T
    out[half:, :] = second[...].T


def join(turned, came):
    width, half = came.shape
    spec = pl.BlockSpec((width, half), lambda i: (0, 0))
    return pl.pallas_call(
        join_kernel,
        grid=(1,),
        in_specs=[spec, spec],
        out_specs=[
            pl.BlockSpec((2 * half, width), lambda i: (0, 0)),
            pl.BlockSpec((width, 2 * half), lambda i: (0, 0)),
        ],
        out_shape=[
            jax.ShapeDtypeStruct((2 * half, width), bf16),
            jax.ShapeDtypeStruct((width, 2 * half), bf16),
        ],
        compiler_params=params(16),
        cost_estimate=cost(4e10, 1e6),
        name="join",
    )(turned, came)


def part_kernel(f_ref, rows, first, second):
    half = rows.shape[0] // 2
    first[...] = rows[:half, :].T
    second[...] = rows[half:, :].T


def part(f, rows):
    tokens, width = rows.shape
    half = tokens // 2
    spec = pl.BlockSpec((width, half), lambda i, f: (0, 0))
    return pl.pallas_call(
        part_kernel,
        grid_spec=pltpu.PrefetchScalarGridSpec(
            num_scalar_prefetch=1,
            grid=(1,),
            in_specs=[pl.BlockSpec((tokens, width), lambda i, f: (0, 0))],
            out_specs=[spec, spec],
        ),
        out_shape=[jax.ShapeDtypeStruct((width, half), bf16)] * 2,
        compiler_params=params(16),
        cost_estimate=cost(4e9, 1e6),
        name="part",
    )(f, rows)


def pack_kernel(key_t, value_t, query, out):
    rows = []
    for g in range(KV_HEADS):
        rows += [key_t[g * HEAD : (g + 1) * HEAD, :], value_t[g * HEAD : (g + 1) * HEAD, :]]
    width = 2 * KV_HEADS * HEAD
    out[:, :width] = jnp.concatenate(rows, axis=0).T
    out[:, width : width + HEADS * HEAD] = query[...]
    out[:, width + HEADS * HEAD :] = jnp.zeros((out.shape[0], HEAD), bf16)


def pack(key, value, query):
    rows = key.shape[0]
    width = (2 * KV_HEADS + HEADS + 1) * HEAD
    full = lambda *shape: pl.BlockSpec(shape, lambda i: (0, 0))
    return pl.pallas_call(
        pack_kernel,
        grid=(1,),
        in_specs=[full(KV_HEADS * HEAD, rows)] * 2 + [full(*query.shape)],
        out_specs=full(rows, width),
        out_shape=jax.ShapeDtypeStruct((rows, width), bf16),
        compiler_params=params(16),
        cost_estimate=cost(4e10, 1e6),
        name="pack",
    )(key.T, value.T, query)


GROUPS = ((4, 1), (0, 2), (2, 2))
ORDER = (1, 2, 0)


def project_kernel(f_ref, h, gain, cos_ref, sin_ref, own, near, far, last, normed_t, q_out, *refs):
    kv_out, (w, sems) = refs[: len(GROUPS)], refs[len(GROUPS) :]
    copies = row_copies(f_ref[0], (own, near, far, last), w, sems)
    start(copies)
    hidden = h[...].astype(f32)
    normed = (hidden * inverse_of(hidden) * gain[...]).astype(bf16)
    normed_t[...] = normed.T
    cos, sin = cos_ref[...], sin_ref[...]
    lane = lane_index(cos.shape)
    kv_cos, kv_sin = jnp.where(lane < HEAD, cos, 1.0), jnp.where(lane < HEAD, sin, 0.0)
    wait(copies)
    first = KV_HEADS * LANES
    both = nn(normed, w[:, :first])
    for (start_head, heads_here), out in zip(GROUPS, kv_out):
        for i in range(heads_here):
            g = start_head + i
            tile = both[:, g * LANES : (g + 1) * LANES]
            out[i] = (tile * kv_cos + swap_halves(tile) * kv_sin).astype(bf16)
    query = nn(normed, w[:, first:])
    for p in range((HEADS + 1) // 2):
        tile = query[:, p * LANES : (p + 1) * LANES]
        tile = (tile * cos + swap_halves(tile) * sin) * (HEAD ** (-0.5) * LOG2E)
        q_out[2 * p] = jnp.where(lane < HEAD, tile, 0.0).astype(bf16)
        if 2 * p + 1 < HEADS:
            q_out[2 * p + 1] = jnp.where(lane < HEAD, pltpu.roll(tile, HEAD, 1), 0.0).astype(bf16)


def project(f, hidden, gain, cos, sin, pieces):
    tokens, width = hidden.shape
    rows, columns = pieces[0].shape
    full = lambda *shape: pl.BlockSpec(shape, lambda i, f: (0,) * len(shape))
    like = jax.ShapeDtypeStruct
    return pl.pallas_call(
        project_kernel,
        grid_spec=pltpu.PrefetchScalarGridSpec(
            num_scalar_prefetch=1,
            grid=(1,),
            in_specs=[full(tokens, width), full(1, width), full(*cos.shape), full(*sin.shape)] + [ANY] * 4,
            out_specs=[full(width, tokens), full(HEADS, tokens, LANES)]
            + [full(heads_here, tokens, LANES) for _, heads_here in GROUPS],
            scratch_shapes=[pltpu.VMEM((4 * rows, columns), bf16), pltpu.SemaphoreType.DMA((4,))],
        ),
        out_shape=[like((width, tokens), bf16), like((HEADS, tokens, LANES), bf16)]
        + [like((heads_here, tokens, LANES), bf16) for _, heads_here in GROUPS],
        compiler_params=params(20),
        cost_estimate=cost(4e10, 1e6),
        name="project",
    )(f, hidden, gain, cos, sin, *pieces)


PARTS = len(GROUPS)


def split_pieces(refs):
    return refs[:4], refs[4:10], refs[10:16], refs[16:22], refs[22:]


CHUNK = 256


def feed_kernel(f_ref, h, *refs):
    attended, gain = refs[:PARTS], refs[PARTS]
    o, gate, up, down, refs = split_pieces(refs[PARTS + 1 :])
    outs, result = refs[:6], refs[6]
    w_o, w_gate, w_up, w_down, n16, *refs = refs[7:]
    after, attended_t, normed_t, gate_out, up_out, hidden_out = refs[:6]
    o_sem, gate_sem, up_sem, down_sem, out_sem = refs[6:]
    depth, wide = 4 * o[0].shape[0], w_gate.shape[1]
    o_copies = row_copies(f_ref[0], o, w_o, o_sem)
    gate_copies = side_copies(f_ref, 1, gate, w_gate, gate_sem)
    up_copies = side_copies(f_ref, 2, up, w_up, up_sem)
    d_copies = down_copies(f_ref, 1, down, w_down, down_sem)
    half = wide // 2

    def leave(k, part=None):
        if part is None:
            return pltpu.make_async_copy(refs[k], outs[k], out_sem.at[k, 0])
        columns = slice(part * half, (part + 1) * half)
        return pltpu.make_async_copy(refs[k].at[:, columns], outs[k].at[:, columns], out_sem.at[k, part])

    leaving = [leave(k) for k in range(3)] + [leave(k, part) for part in (0, 1) for k in (3, 4, 5)]
    for copies in (o_copies, gate_copies, up_copies, d_copies):
        start(copies)
    att = jnp.concatenate([attended[i][...] for i in ORDER], axis=1)
    attended_t[...] = att.T
    w_o[depth:, :] = jnp.zeros((w_o.shape[0] - depth, w_o.shape[1]), bf16)
    wait(o_copies)
    value = h[...].astype(f32) + nn(att, w_o[...])
    after[...] = value
    normed = (value * inverse_of(value) * gain[...]).astype(bf16)
    n16[...] = normed
    normed_t[...] = normed.T
    wait(gate_copies)
    wait(up_copies)
    for at in range(0, wide, CHUNK):
        columns = slice(at, at + CHUNK)
        gate_act = nn(n16[...], w_gate[:, columns])
        up_act = nn(n16[...], w_up[:, columns])
        hidden = gate_act * jax.nn.sigmoid(gate_act) * up_act
        gate_out[:, columns] = gate_act.astype(bf16)
        up_out[:, columns] = up_act.astype(bf16)
        hidden_out[:, columns] = hidden.astype(bf16)
        if at + CHUNK == half:
            start(leaving[:6])
    start(leaving[6:])
    wait(d_copies)
    result[...] = (after[...] + nt(hidden_out[...], w_down[...])).astype(result.dtype)
    wait(leaving)


def weight_scratch(o, gate):
    rows, width = o.shape
    columns = gate.shape[1]
    return [
        pltpu.VMEM((4 * rows + HEAD, width), bf16),
        pltpu.VMEM((4 * rows, columns), bf16),
        pltpu.VMEM((4 * rows, columns), bf16),
        pltpu.VMEM((width, columns), bf16),
    ]


def weight_sems():
    dma = pltpu.SemaphoreType.DMA
    return [dma((4,)), dma((6,)), dma((6,)), dma((6,))]


def feed(f, hidden, attended, gain, o, gate, up, down, result_type):
    tokens, width = hidden.shape
    wide = gate[0].shape[1]
    lanes = (HEADS + 1) * HEAD
    full = lambda *shape: pl.BlockSpec(shape, lambda i, f: (0,) * len(shape))
    like = jax.ShapeDtypeStruct
    kept = [((tokens, width), f32), ((lanes, tokens), bf16), ((width, tokens), bf16)] + [((tokens, wide), bf16)] * 3
    return pl.pallas_call(
        feed_kernel,
        grid_spec=pltpu.PrefetchScalarGridSpec(
            num_scalar_prefetch=1,
            grid=(1,),
            in_specs=[full(tokens, width)] + [full(*a.shape) for a in attended] + [full(1, width)] + [ANY] * 22,
            out_specs=[ANY] * 6 + [full(tokens, width)],
            scratch_shapes=weight_scratch(o[0], gate[0])
            + [pltpu.VMEM((tokens, width), bf16)]
            + [pltpu.VMEM(*k) for k in kept]
            + weight_sems()
            + [pltpu.SemaphoreType.DMA((6, 2))],
        ),
        out_shape=[like(*k) for k in kept] + [like((tokens, width), result_type)],
        compiler_params=params(48),
        cost_estimate=cost(4e10, 1e6),
        name="feed",
    )(f, hidden, *attended, gain, *o, *gate, *up, *down)


def feed_back_kernel(f_ref, g, gain, *refs):
    held = refs[:3]
    o, gate, up, down, refs = split_pieces(refs[3:])
    outs, grad_after, branch_out = refs[:2], refs[2], refs[3]
    grad_attended, gain_grad = refs[4 : 4 + PARTS], refs[4 + PARTS]
    w_o, w_gate, w_up, w_down, g16, *refs = refs[5 + PARTS :]
    after, gate_act, up_act, grad_gate, grad_up, o_sem, gate_sem, up_sem, down_sem, in_sem, out_sem = refs
    depth, wide = 4 * o[0].shape[0], w_gate.shape[1]
    half = wide // 2
    o_copies = row_copies(f_ref[0], o, w_o, o_sem)
    gate_copies = side_copies(f_ref, 1, gate, w_gate, gate_sem)
    up_copies = side_copies(f_ref, 2, up, w_up, up_sem)
    d_copies = down_copies(f_ref, 1, down, w_down, down_sem)

    def act_copies(part):
        columns = slice(part * half, (part + 1) * half)
        return [
            pltpu.make_async_copy(held[k].at[:, columns], refs[k].at[:, columns], in_sem.at[k, part]) for k in (1, 2)
        ]

    after_copy = pltpu.make_async_copy(held[0], after, in_sem.at[0, 0])
    leave = [pltpu.make_async_copy(refs[3 + k], outs[k], out_sem.at[k]) for k in (0, 1)]
    first, second = act_copies(0), act_copies(1)
    for copies in (d_copies, first, second, gate_copies, up_copies, [after_copy], o_copies):
        start(copies)
    g16[...] = g[...].astype(bf16)
    w_o[depth:, :] = jnp.zeros((w_o.shape[0] - depth, w_o.shape[1]), bf16)
    wait(d_copies)
    for part, copies in enumerate((first, second)):
        wait(copies)
        for at in range(part * half, (part + 1) * half, CHUNK):
            columns = slice(at, at + CHUNK)
            grad_hidden = nn(g16[...], w_down[:, columns])
            value = gate_act[:, columns].astype(f32)
            logistic = jax.nn.sigmoid(value)
            steep = logistic * (1.0 + value * (1.0 - logistic))
            grad_gate[:, columns] = (grad_hidden * up_act[:, columns].astype(f32) * steep).astype(bf16)
            grad_up[:, columns] = (grad_hidden * (value * logistic)).astype(bf16)
    wait(gate_copies)
    wait(up_copies)
    start(leave)
    grad_normed = nt(grad_gate[...], w_gate[...]) + nt(grad_up[...], w_up[...])
    wait([after_copy])
    wait(o_copies)
    back, gain_part = norm_back(grad_normed, after[...], gain[...])
    back = back + g[...].astype(f32)
    gain_grad[...] = gain_part
    grad_after[...] = back
    branch = back.astype(bf16)
    branch_out[...] = branch
    whole = nt(branch, w_o[...]).astype(bf16)
    at = 0
    for i in ORDER:
        lanes = grad_attended[i].shape[1]
        grad_attended[i][...] = whole[:, at : at + lanes]
        at += lanes
    wait(leave)


def feed_back(f, g, after, gain, gate_act, up_act, o, gate, up, down):
    tokens, width = after.shape
    wide = gate[0].shape[1]
    full = lambda *shape: pl.BlockSpec(shape, lambda i, f: (0,) * len(shape))
    like = jax.ShapeDtypeStruct
    lanes = [pair_lanes(heads_here) for _, heads_here in GROUPS]
    dma = pltpu.SemaphoreType.DMA
    return pl.pallas_call(
        feed_back_kernel,
        grid_spec=pltpu.PrefetchScalarGridSpec(
            num_scalar_prefetch=1,
            grid=(1,),
            in_specs=[full(tokens, width), full(1, width)] + [ANY] * 25,
            out_specs=[ANY, ANY, full(tokens, width), full(tokens, width)]
            + [full(tokens, n) for n in lanes]
            + [full(1, width)],
            scratch_shapes=weight_scratch(o[0], gate[0])
            + [pltpu.VMEM((tokens, width), bf16), pltpu.VMEM((tokens, width), f32)]
            + [pltpu.VMEM((tokens, wide), bf16)] * 4
            + weight_sems()
            + [dma((3, 2)), dma((2,))],
        ),
        out_shape=[like((tokens, wide), bf16)] * 2
        + [like((tokens, width), f32), like((tokens, width), bf16)]
        + [like((tokens, n), bf16) for n in lanes]
        + [like((1, width), f32)],
        compiler_params=params(52),
        cost_estimate=cost(4e10, 1e6),
        name="feed_back",
    )(f, g, gain, after, gate_act, up_act, *o, *gate, *up, *down)


def project_back_kernel(f_ref, *refs):
    grad_q, kept, came = refs[:PARTS], refs[PARTS : 2 * PARTS], refs[2 * PARTS : 3 * PARTS]
    cos_ref, sin_ref, h, gain, grad_after, own, near, far, last = refs[3 * PARTS : 3 * PARTS + 9]
    grads, grad_in, turned, gain_grad, w, sems = refs[3 * PARTS + 9 :]
    copies = row_copies(f_ref[0], (own, near, far, last), w, sems)
    start(copies)
    cos, sin = cos_ref[...], sin_ref[...]
    lane = lane_index(cos.shape)
    cos, sin = jnp.where(lane < HEAD, cos, 1.0), jnp.where(lane < HEAD, sin, 0.0)
    at = KV_HEADS * LANES
    for k in ORDER:
        first, heads_here = GROUPS[k]
        for i in range(heads_here):
            g = first + i
            tile = kept[k][i].astype(f32) + came[k][i].astype(f32)
            tile = tile * cos - swap_halves(tile) * sin
            grads[:, g * LANES : (g + 1) * LANES] = tile.astype(bf16)
        lanes = grad_q[k].shape[1]
        grads[:, at : at + lanes] = grad_q[k][...]
        at += lanes
    wait(copies)
    grad_normed = nt(grads[...], w[...])
    back, gain_part = norm_back(grad_normed, h[...].astype(f32), gain[...])
    gain_grad[...] = gain_part
    back = back + grad_after[...]
    grad_in[...] = back.astype(grad_in.dtype)
    turned[...] = back.astype(bf16).T


def project_back(f, grad_q, kept, came, cos, sin, hidden, gain, grad_after, pieces, result_type):
    tokens, width = hidden.shape
    rows, columns = pieces[0].shape
    full = lambda *shape: pl.BlockSpec(shape, lambda i, f: (0,) * len(shape))
    like = jax.ShapeDtypeStruct
    arrays = (*grad_q, *kept, *came, cos, sin, hidden, gain, grad_after)
    return pl.pallas_call(
        project_back_kernel,
        grid_spec=pltpu.PrefetchScalarGridSpec(
            num_scalar_prefetch=1,
            grid=(1,),
            in_specs=[full(*a.shape) for a in arrays] + [ANY] * 4,
            out_specs=[full(tokens, columns), full(tokens, width), full(width, tokens), full(1, width)],
            scratch_shapes=[pltpu.VMEM((4 * rows, columns), bf16), pltpu.SemaphoreType.DMA((4,))],
        ),
        out_shape=[
            like((tokens, columns), bf16),
            like((tokens, width), result_type),
            like((width, tokens), bf16),
            like((1, width), f32),
        ],
        compiler_params=params(20),
        cost_estimate=cost(4e10, 1e6),
        name="project_back",
    )(f, *arrays, *pieces)


def joined(left_first, left_second, right_first, right_second):
    left = jnp.concatenate([left_first, left_second], axis=1)
    return nn(left, jnp.concatenate([right_first, right_second], axis=0))


def outer_tiles_kernel(f_ref, left_first, left_second, right_first, right_second, *refs, rows):
    outs, acc = refs[:4], refs[4]
    acc[...] = joined(left_first[...], left_second[...], right_first[...], right_second[...])
    half = acc.shape[1] // 2
    for m in range(4):
        from_row = pl.multiple_of((f_ref[0] ^ m) * rows, 16)
        for c in (0, 1):
            outs[m][c] = acc[pl.ds(from_row, rows), c * half : (c + 1) * half].astype(bf16)


def outer_tiles(f, lefts, rights, rows, name):
    width, tokens = lefts[0].shape
    wide = rights[0].shape[1] // 2
    left = pl.BlockSpec((width, tokens), lambda i, f: (0, 0))
    right = pl.BlockSpec((tokens, wide), lambda i, f: (0, i))
    out = pl.BlockSpec((2, rows, wide // 2), lambda i, f: (i, 0, 0))
    return pl.pallas_call(
        functools.partial(outer_tiles_kernel, rows=rows),
        grid_spec=pltpu.PrefetchScalarGridSpec(
            num_scalar_prefetch=1,
            grid=(2,),
            in_specs=[left, left, right, right],
            out_specs=[out] * 4,
            scratch_shapes=[pltpu.VMEM((width, wide), f32)],
        ),
        out_shape=[jax.ShapeDtypeStruct((4, rows, wide // 2), bf16)] * 4,
        compiler_params=params(28),
        cost_estimate=cost(4e10, 1e6),
        name=name,
    )(f, *lefts, *rights)


def outer_down_kernel(f_ref, left_first, left_second, right_first, right_second, own, near):
    value = joined(left_first[...], left_second[...], right_first[...], right_second[...])
    half = value.shape[1] // 2
    first = (f_ref[0] & 1) == 0
    lower, upper = value[:, :half], value[:, half:]
    own[0] = jnp.where(first, lower, upper).astype(bf16)
    near[0] = jnp.where(first, upper, lower).astype(bf16)


def outer_down(f, lefts, rights, chip, name):
    width, tokens = lefts[0].shape
    wide = rights[0].shape[1] // 2
    left = pl.BlockSpec((width, tokens), lambda i, f: (0, 0))
    right = pl.BlockSpec((tokens, wide), lambda i, f: (0, (f[0] >> 1) ^ chip))
    out = pl.BlockSpec((1, width, wide // 2), lambda i, f: (0, 0, 0))
    return pl.pallas_call(
        outer_down_kernel,
        grid_spec=pltpu.PrefetchScalarGridSpec(
            num_scalar_prefetch=1,
            grid=(1,),
            in_specs=[left, left, right, right],
            out_specs=[out, out],
        ),
        out_shape=[jax.ShapeDtypeStruct((1, width, wide // 2), bf16)] * 2,
        compiler_params=params(28),
        cost_estimate=cost(4e10, 1e6),
        name=name,
    )(f, *lefts, *rights)


def outer_kernel(f_ref, left_first, left_second, right_first, right_second, extra, *refs, rows):
    outs, acc = refs[:4], refs[4]
    acc[...] = joined(left_first[...], left_second[...], right_first[...], right_second[...])
    columns = acc.shape[1]
    for m in range(4):
        device = f_ref[0] ^ m
        out = outs[m]
        if columns < out.shape[2]:
            out[0, :, columns:] = jnp.zeros((out.shape[1], out.shape[2] - columns), bf16)
        out[0, :rows, :columns] = acc[pl.ds(pl.multiple_of(device * rows, 16), rows), :].astype(bf16)
        out[0, rows:, :columns] = jnp.zeros((out.shape[1] - rows, columns), bf16)
        out[0, rows:, : extra.shape[2]] = extra[device]


def outer(f, lefts, rights, extra, rows, name):
    width, tokens = lefts[0].shape
    height, columns = 4 * rows, rights[0].shape[1]
    shape = (1, rows + extra.shape[1], -(-columns // LANES) * LANES)
    full = lambda *shape: pl.BlockSpec(shape, lambda i, f: (0,) * len(shape))
    return pl.pallas_call(
        functools.partial(outer_kernel, rows=rows),
        grid_spec=pltpu.PrefetchScalarGridSpec(
            num_scalar_prefetch=1,
            grid=(1,),
            in_specs=[full(height, tokens)] * 2 + [full(tokens, columns)] * 2 + [full(*extra.shape)],
            out_specs=[full(*shape)] * 4,
            scratch_shapes=[pltpu.VMEM((height, columns), f32)],
        ),
        out_shape=[jax.ShapeDtypeStruct(shape, bf16)] * 4,
        compiler_params=params(28),
        cost_estimate=cost(4e10, 1e6),
        name=name,
    )(f, *lefts, *rights, extra)


def unpack_kernel(total, key_t, value_t, query):
    rows = query.shape[0]
    width = 2 * KV_HEADS * HEAD
    turned = total[:rows, :width].astype(f32).T
    for g in range(KV_HEADS):
        key_t[g * HEAD : (g + 1) * HEAD, :] = turned[2 * g * HEAD : (2 * g + 1) * HEAD, :]
        value_t[g * HEAD : (g + 1) * HEAD, :] = turned[(2 * g + 1) * HEAD : (2 * g + 2) * HEAD, :]
    query[...] = total[:rows, width : width + HEADS * HEAD].astype(f32)


def unpack(total, rows):
    full = lambda *shape: pl.BlockSpec(shape, lambda i: (0, 0))
    like = jax.ShapeDtypeStruct
    side = (KV_HEADS * HEAD, rows)
    key_t, value_t, query = pl.pallas_call(
        unpack_kernel,
        grid=(1,),
        in_specs=[full(*total.shape)],
        out_specs=[full(*side), full(*side), full(rows, HEADS * HEAD)],
        out_shape=[like(side, f32), like(side, f32), like((rows, HEADS * HEAD), f32)],
        compiler_params=params(16),
        cost_estimate=cost(4e10, 1e6),
        name="unpack",
    )(total)
    return key_t.T, value_t.T, query


def flip(array, axis, bit):
    size = lax.axis_size(axis)
    return lax.ppermute(array, axis, [(i, i ^ bit) for i in range(size)])


def add(left, right):
    return left.astype(f32) + right.astype(f32)


def levels_of(size):
    return [(bit, 2) for bit in range(size.bit_length() - 1)]


def cut(array, count):
    blocks, rows, columns = array.shape
    outer = next(n for n in (4, 2, 1) if n <= count and blocks % n == 0)
    inner = count // outer
    array = array.reshape(outer, blocks // outer, inner, rows // inner, columns)
    return [array[i // inner, :, i % inner] for i in range(count)]


def glue(parts, shape):
    count = len(parts)
    outer = next(n for n in (4, 2, 1) if n <= count and shape[0] % n == 0)
    inner = count // outer
    rows = [jnp.concatenate(parts[i * inner : (i + 1) * inner], axis=1) for i in range(outer)]
    return jnp.concatenate(rows, axis=0).reshape(shape)


def pick(parts, index):
    while len(parts) > 1:
        odd = index % 2 == 1
        parts = [jnp.where(odd, parts[i + 1], parts[i]) for i in range(0, len(parts), 2)]
        index = index // 2
    return parts[0]


def reduction(own, near, far, last, halves):
    shape = own.shape
    if last is None:
        beside, first = yield [(near, "fsdp", 1), (far, "fsdp", 2)]
        crossed = [first]
    else:
        came, beside = yield [(last, "fsdp", 1), (near, "fsdp", 1)]
        crossed = []
        for ours, theirs in zip(cut(far, halves), cut(came, halves)):
            crossed += yield [(add(ours, theirs).astype(bf16), "fsdp", 2)]
    crossed = glue(crossed, shape) if halves > 1 else crossed[0]
    part = add(own, beside) + crossed.astype(f32)
    index = lax.axis_index("dp")
    shapes = []
    for bit, count in levels_of(lax.axis_size("dp")):
        shapes.append(part.shape)
        parts = cut(part, count)
        mine = (index >> bit) % count
        came = yield [(pick(parts, mine ^ j).astype(bf16), "dp", j << bit) for j in range(1, count)]
        part = pick(parts, mine).astype(f32)
        for other in came:
            part = part + other.astype(f32)
    part = part.astype(bf16)
    for (bit, count), wide in zip(reversed(levels_of(lax.axis_size("dp"))), reversed(shapes)):
        came = yield [(part, "dp", j << bit) for j in range(1, count)]
        mine = (index >> bit) % count
        held = [part] + came
        part = glue([pick(held, mine ^ p) for p in range(count)], wide)
    return part


class Unit:
    def __init__(self, own, near, far, last, halves=1):
        self.steps = reduction(own, near, far, last, halves)
        self.asks = next(self.steps)
        self.total = None

    def take(self, came):
        try:
            self.asks = self.steps.send(came)
        except StopIteration as end:
            self.asks, self.total = [], end.value


class Clock:
    def __init__(self, f):
        self.f = f
        self.before = []

    def phase(self, moves=(), work=None, units=(), extra=()):
        asks = list(moves)
        for unit in units:
            asks += unit.asks
        gated = lax.optimization_barrier((self.f, *(a[0] for a in asks), *extra, *self.before))
        came = [flip(g, axis, bit) for g, (_, axis, bit) in zip(gated[1:], asks)]
        done = None if work is None else work(gated[0])
        self.before = list(came) + ([] if done is None else [jax.tree.leaves(done)[0]])
        at = len(moves)
        for unit in units:
            count = len(unit.asks)
            unit.take(came[at : at + count])
            at += count
        return came[: len(moves)], done


def half_for(shard, low_first, dim):
    width = shard.shape[dim] // 2
    low = lax.slice_in_dim(shard, 0, width, axis=dim)
    high = lax.slice_in_dim(shard, width, 2 * width, axis=dim)
    return jnp.where(low_first, low, high)


def per_device(
    tokens, seq_cuts, w_query, w_key, w_value, w_output, w_gate, w_up, w_down, gain_attn, gain_ffn, cotangent
):
    rows, width = tokens.shape[1], tokens.shape[2]
    half = rows // 2
    index = lax.axis_index("fsdp")
    replica = lax.axis_index("dp")
    f = jnp.stack([index, replica % 2, replica // 2 % 2]).astype(jnp.int32)
    count = rows * lax.axis_size("fsdp")
    shard_rows = w_key.shape[0]
    core, y = ("fsdp", 1), ("fsdp", 2)
    side = (("dp", 1), ("dp", 2))

    bounds = seq_cuts[0]
    within = jnp.arange(half, dtype=jnp.int32)
    local = jnp.concatenate([2 * index * half + within, (7 - 2 * index) * half + within]).astype(jnp.int32)
    every = jnp.arange(count, dtype=jnp.int32)
    passed = local[:, None] >= bounds[None, :]
    docs = jnp.sum(passed.astype(jnp.int32), axis=1)
    positions = local - jnp.max(jnp.where(passed, bounds[None, :], 0), axis=1)
    key_docs = jnp.sum((every[:, None] >= bounds[None, :]).astype(jnp.int32), axis=1)
    lane = jnp.arange(LANES, dtype=jnp.int32)[None, :]
    one = ((lane == key_docs[:, None]) & (lane < 4)) | ((lane >= 8) & (lane < 11))
    key_marks = one.astype(bf16)
    q_marks = jnp.where((lane < 4) & (lane != docs[:, None]), NEGATIVE, 0.0).astype(bf16)
    frequency = jnp.power(10000.0, -2.0 * jnp.arange(HEAD // 2, dtype=f32) / HEAD)
    angle = positions.astype(f32)[:, None] * frequency[None, :]
    cosine, sine = jnp.cos(angle), jnp.sin(angle)
    cos = jnp.concatenate([cosine] * 4, axis=1)
    sin = jnp.concatenate([-sine, sine] * 2, axis=1)
    gain_a, gain_f = gain_attn[None, :], gain_ffn[None, :]

    clock = Clock(f)
    tokens_t, cotangent_t, down_t = tokens[0].T, cotangent[0].T, w_down.T
    shards = {"gate": w_gate, "up": w_up, "down": down_t}
    bit_of, dim_of = {"gate": 0, "up": 1, "down": 0}, {"gate": 1, "up": 1, "down": 0}
    across = lambda name: (half_for(shards[name], f[1 + bit_of[name]] == 0, dim_of[name]), *y)

    w_own = pack(w_key, w_value, w_query)
    (w_far, w_near, other_tokens), _ = clock.phase([(w_own, *y), (w_own, *core), (tokens_t[:, half:], "fsdp", 3)])
    (w_last, gate_far), (h0, _) = clock.phase(
        [(w_far, *core), across("gate")], lambda turn: join(tokens_t, other_tokens), extra=(key_marks, q_marks, cos, sin)
    )
    w_in = (w_own, w_near, w_far, w_last)

    def attend_phases(hidden, first, moves):
        came = []
        got, (normed_t, q, *parts) = clock.phase(first, lambda turn: project(turn, hidden, gain_a, cos, sin, w_in))
        came.append(got)
        a, b, c = parts
        got, _ = clock.phase([(a, *y), (a, *core), (b, *core)] + moves[0](came))
        a_far, a_near, b_near = got[:3]
        came.append(got[3:])
        got, _ = clock.phase([(a_far, *core), (b, *y), (c, *core)] + moves[1](came))
        a_last, b_far, c_near = got[:3]
        came.append(got[3:])
        gathered = [(a, a_near, a_far, a_last)]
        attended, marks = [], []

        def call(k):
            return lambda turn: attend(turn, q, q_marks, key_marks, gathered[k], GROUPS[k])

        got, (x, m) = clock.phase([(b_far, *core), (c, *y)] + moves[2](came), call(0))
        attended.append(x), marks.append(m)
        b_last, c_far = got[:2]
        came.append(got[2:])
        gathered.append((b, b_near, b_far, b_last))
        got, (x, m) = clock.phase([(c_far, *core)] + moves[3](came), call(1))
        attended.append(x), marks.append(m)
        came.append(got[1:])
        gathered.append((c, c_near, c_far, got[0]))
        got, (x, m) = clock.phase(moves[4](came), call(2))
        attended.append(x), marks.append(m)
        came.append(got)
        return (normed_t, q, gathered, attended, marks), came

    def feed_phase(hidden, weights, run, result_type, moves=()):
        normed_t, q, gathered, attended, marks = run
        got, (after, attended_t, normed_ffn_t, gate_act, up_act, hidden_act, result) = clock.phase(
            moves, lambda turn: feed(turn, hidden, attended, gain_f, *weights, result_type)
        )
        return result, got, (
            hidden, normed_t, q, gathered, attended, marks, after, attended_t, normed_ffn_t, gate_act, up_act, hidden_act,
        )

    none = lambda came: []
    run, came = attend_phases(
        h0,
        [across("up"), (gate_far, *side[0])],
        (
            lambda came: [(w_output, *core), (w_gate, *core)],
            lambda came: [across("down"), (came[0][0], *side[1])],
            lambda came: [(w_output, *y), (came[2][0], *side[0]), (w_up, *core)],
            lambda came: [(gate_far, *core), (came[0][1], *core), (came[0][0], *core), (came[2][1], *core)],
            lambda came: [(came[2][0], *core), (came[3][1], *core), (down_t, *core), (came[3][0], *core)],
        ),
    )
    up_far, gate_other = came[0]
    down_far, up_other = came[2]
    o_near, gate_near = came[1]
    o_far, down_other, up_near = came[3]
    gate_last, gate_other_last, up_last, up_other_last = came[4]
    down_last, down_other_last, down_near, o_last = came[5]
    weights = (
        (w_output, o_near, o_far, o_last),
        (w_gate, gate_near, gate_far, gate_other, gate_last, gate_other_last),
        (w_up, up_near, up_far, up_other, up_last, up_other_last),
        (down_t, down_near, down_far, down_other, down_last, down_other_last),
    )
    h1, (other_cotangent,), first = feed_phase(h0, weights, run, f32, [(cotangent_t[:, half:], "fsdp", 3)])
    run, _ = attend_phases(h1, [], (none,) * 5)
    h2, _, second = feed_phase(h1, weights, run, bf16)
    _, (cot, cot_turned) = clock.phase((), lambda turn: join(cotangent_t, other_cotangent))

    def feed_back_work(g, stored):
        return lambda turn: feed_back(turn, g, stored[6], gain_f, stored[9], stored[10], *weights)

    BACK = (1, 2, 0)

    def back_phases(grad_attended, stored, beside):
        q, gathered, attended, marks = stored[2], stored[3], stored[4], stored[5]
        grad_q, kept, far = [None] * PARTS, [None] * PARTS, [None] * PARTS
        extra = []

        def call(k):
            return lambda turn: attend_back(
                turn, q, marks[k], key_marks, gathered[k], grad_attended[k], attended[k], cos, sin, GROUPS[k]
            )

        def sums(k, keep, near):
            kept[k] = add(keep[0], near[0]).astype(bf16)
            return add(keep[1], near[1]).astype(bf16)

        b, c, a = BACK
        moves, units = beside(0)
        got, (grad_q[b], b_keep, b_send) = clock.phase(moves, call(b), units)
        extra += got
        moves, units = beside(1)
        got, (grad_q[c], c_keep, c_send) = clock.phase([(b_send, *core)] + moves, call(c), units)
        extra += got[1:]
        b_sum = sums(b, b_keep, got[0])
        moves, units = beside(2)
        got, (grad_q[a], a_keep, a_send) = clock.phase([(b_sum, *y), (c_send, *core)] + moves, call(a), units)
        far[b] = got[0]
        extra += got[2:]
        c_sum = sums(c, c_keep, got[1])
        moves, units = beside(3)
        got, _ = clock.phase([(c_sum, *y), (a_send, *core)] + moves, None, units)
        far[c] = got[0]
        extra += got[2:]
        a_sum = sums(a, a_keep, got[1])
        moves, units = beside(4)
        got, _ = clock.phase([(a_sum, *y)] + moves, None, units)
        far[a] = got[0]
        extra += got[1:]
        return (grad_q, kept, far), extra

    def project_back_work(parts, stored, grad_after, result_type):
        return lambda turn: project_back(
            turn, *parts, cos, sin, stored[0], gain_a, grad_after, w_in, result_type
        )

    _, fed2 = clock.phase((), feed_back_work(cot, second))
    out_first, out_second = part(f, h2)
    parts, extra = back_phases(
        fed2[4 : 4 + PARTS], second, lambda k: ([(out_second, "fsdp", 3)] if k == 0 else [], ())
    )
    output = jnp.concatenate([out_first, extra[0]], axis=1).T
    _, (grads2, middle, middle_turned, gain_a2) = clock.phase((), project_back_work(parts, second, fed2[2], f32))

    def down_work(chip, name):
        return lambda turn: outer_down(turn, (middle_turned, cot_turned), (first[11], second[11]), chip, name)

    _, far_pair = clock.phase((), down_work(1, "outer_down_far"))
    (far_beside,), own_pair = clock.phase([(far_pair[1], *core)], down_work(0, "outer_down_own"))
    down = Unit(*own_pair, add(far_pair[0], far_beside).astype(bf16), None)
    _, fed1 = clock.phase((), feed_back_work(middle, first), (down,))

    def outer_work(i, name):
        return lambda turn: outer_tiles(turn, (first[8], second[8]), (fed1[i], fed2[i]), shard_rows, name)

    nothing = jnp.zeros((4, 16, LANES), bf16)
    _, gate_parts = clock.phase((), outer_work(0, "outer_gate"))
    gate = Unit(*gate_parts, 2)
    _, (up_parts, o_parts) = clock.phase(
        (),
        lambda turn: (
            outer_work(1, "outer_up")(turn),
            outer(turn, (first[7], second[7]), (fed1[3], fed2[3]), nothing, shard_rows, "outer_o"),
        ),
        (down, gate),
    )
    up, out = Unit(*up_parts, 2), Unit(*o_parts)
    plan = ((gate, up, down, out), (gate, down), (up, gate, down), (gate,), ())
    parts, _ = back_phases(fed1[4 : 4 + PARTS], first, lambda k: ([], plan[k]))
    _, (grads1, grad_tokens, _, gain_a1) = clock.phase(
        (), project_back_work(parts, first, fed1[2], bf16), (up, gate, down)
    )
    gains = jnp.concatenate([gain_a1 + gain_a2, fed1[4 + PARTS] + fed2[4 + PARTS]], axis=0)
    gains = gains.reshape(2, 4, width // 4).transpose(1, 0, 2).astype(bf16)
    gains = jnp.pad(gains, ((0, 0), (0, 14), (0, 256 - width // 4)))
    _, in_parts = clock.phase(
        (),
        lambda turn: outer(turn, (first[1], second[1]), (grads1, grads2), gains, shard_rows, "outer_in"),
        (out, up, gate),
    )
    into = Unit(*in_parts)
    clock.phase((), None, (into, up, out))
    _, (back_half, back_send) = clock.phase((), lambda turn: part(turn, grad_tokens), (into, up, gate, down, out))
    clock.phase((), None, (into, up, out))
    clock.phase((), None, (into, up, gate, out))
    (other_tokens,), _ = clock.phase([(back_send, "fsdp", 3)], None, (into, up, out))
    grad_tokens = jnp.concatenate([back_half, other_tokens], axis=1).T
    units = (into, up, out, gate, down)
    while any(unit.asks for unit in units):
        clock.phase((), None, [unit for unit in units if unit.asks])

    grad_down = down.total[0].T.astype(f32)
    wide = lambda unit: jnp.concatenate([unit.total[i] for i in range(4)], axis=1).astype(f32)
    grad_gate, grad_up = wide(gate), wide(up)
    grad_o = out.total[0, :shard_rows, :width].astype(f32)
    total = into.total[0]
    grad_key, grad_value, grad_query = unpack(total, shard_rows)
    gains = total[shard_rows : shard_rows + 2, : width // 4].astype(f32)
    return (
        output[None], grad_tokens[None], grad_query, grad_key, grad_value, grad_o, grad_gate, grad_up,
        grad_down, gains[0], gains[1],
    )


def solution(mesh):
    split, whole = P("fsdp", None), P("dp", "fsdp", None)
    return jax.shard_map(
        per_device,
        mesh=mesh,
        in_specs=(whole, P("dp", None)) + (split,) * 7 + (P(), P(), whole),
        out_specs=(whole, whole) + (split,) * 7 + (P("fsdp"), P("fsdp")),
        check_vma=False,
    )
```

```python
import functools
import jax
import jax.numpy as jnp
from jax import lax
from jax.experimental import pallas as pl
from jax.experimental.pallas import tpu as pltpu
from jax.sharding import PartitionSpec as P

HEADS = 15
KV_HEADS = 5
HEAD = 64
GROUP = HEADS // KV_HEADS
LANES = 128
NEGATIVE = -1e30
LOG2E = 1.4426950408889634
LN2 = 0.6931471805599453
MIB = 1 << 20
f32 = jnp.float32
bf16 = jnp.bfloat16


def nn(left, right):
    return lax.dot_general(left, right, (((1,), (0,)), ((), ())), preferred_element_type=f32)


def nt(left, right):
    return lax.dot_general(left, right, (((1,), (1,)), ((), ())), preferred_element_type=f32)


def lane_index(shape):
    return lax.broadcasted_iota(jnp.int32, shape, len(shape) - 1)


def swap_halves(tile):
    low = lane_index(tile.shape) % HEAD < HEAD // 2
    return jnp.where(low, pltpu.roll(tile, LANES - HEAD // 2, 1), pltpu.roll(tile, HEAD // 2, 1))


def three_terms(column, lane):
    high = column.astype(bf16).astype(f32)
    rest = column - high
    middle = rest.astype(bf16).astype(f32)
    low = rest - middle
    return jnp.where(lane == 8, high, jnp.where(lane == 9, middle, jnp.where(lane == 10, low, 0.0)))


def gather_keys(f, fresh, pieces, key_marks, kvf):
    block = kvf.shape[1]
    half = block // 2
    for m, piece in enumerate(pieces):
        device = f ^ m
        kvf[device, :half, :LANES] = piece[0, :half, :]
        kvf[3 - device, half:, :LANES] = piece[0, half:, :]

    @pl.when(fresh)
    def _():
        for j in range(kvf.shape[0]):
            kvf[j, :, LANES:] = key_marks[j * block : (j + 1) * block, :]


def causal(shape):
    row = lax.broadcasted_iota(jnp.int32, shape, 0)
    return lane_index(shape) <= row + (shape[1] - shape[0])


def score_parts(f):
    parts = [(0, f, 1, True), (1, 3 - f, 2, True)]
    for i in range(3):
        second = i >= f
        parts.append((second.astype(jnp.int32), jnp.where(second, i - f, i), 2, False))
    return parts


def attend_kernel(f_ref, q, q_marks, key_marks, own, near, far, last, attended, marks_out, kvf, qf, scores, best, top, acc):
    g = pl.program_id(0)
    f = f_ref[0]
    half = kvf.shape[1] // 2
    gather_keys(f, g == 0, (own, near, far, last), key_marks, kvf)
    parts = score_parts(f)

    @pl.when(g == 0)
    def _():
        for b in (0, 1):
            for i in range(GROUP):
                qf[b, i * half : (i + 1) * half, LANES:] = q_marks[b * half : (b + 1) * half, :]

    for b in (0, 1):
        for i in range(GROUP):
            qf[b, i * half : (i + 1) * half, :LANES] = q[i, b * half : (b + 1) * half, :]

    for n, (b, k, size, diagonal) in enumerate(parts):
        keys = kvf[k, : size * half, :]
        for i in range(GROUP):
            rows = slice(i * half, (i + 1) * half)
            s = nt(qf[b, rows, :], keys)
            if diagonal:
                s = jnp.where(causal(s.shape), s, NEGATIVE)
            scores[n, rows, : size * half] = s
            peak = s[:, :LANES]
            for t in range(1, size * half // LANES):
                peak = jnp.maximum(peak, s[:, t * LANES : (t + 1) * LANES])
            best[n, rows, :] = peak

    for b in (0, 1):
        for i in range(GROUP):
            rows = slice(i * half, (i + 1) * half)
            peak = best[b, rows, :]
            for n in (2, 3, 4):
                peak = jnp.maximum(peak, jnp.where(parts[n][0] == b, best[n, rows, :], NEGATIVE))
            top[b, rows, :] = jnp.broadcast_to(jnp.max(peak, axis=1, keepdims=True), peak.shape)

    for n, (b, k, size, _) in enumerate(parts):
        keys = kvf[k, : size * half, :]
        for i in range(GROUP):
            rows = slice(i * half, (i + 1) * half)
            high = jnp.concatenate([top[b, rows, :]] * (size * half // LANES), axis=1)
            p = jnp.exp2(scores[n, rows, : size * half] - high).astype(bf16)
            mixed = nn(p, keys)
            if n < 2:
                acc[b, rows, :] = mixed
            else:
                acc[b, rows, :] += mixed

    lane = lane_index((half, LANES))
    for b in (0, 1):
        outer = slice(b * half, (b + 1) * half)
        for i in range(GROUP):
            rows = slice(i * half, (i + 1) * half)
            total = acc[b, rows, LANES + 8 : LANES + 9]
            out = acc[b, rows, :LANES] * (1.0 / total)
            log_total = top[b, rows, :] + jnp.log2(total)
            new_marks = q_marks[outer, :].astype(f32) + three_terms(-log_total, lane)
            marks_out[i, outer, :] = new_marks.astype(bf16)
            h = GROUP * g + i
            pair = pl.multiple_of((h // 2) * LANES, LANES)
            odd = h % 2 == 1
            turned = pltpu.roll(out, HEAD, 1)
            old = attended[outer, pl.ds(pair, LANES)].astype(f32)
            new = jnp.where(odd, jnp.where(lane >= HEAD, out, old), jnp.where(lane < HEAD, turned, 0.0))
            attended[outer, pl.ds(pair, LANES)] = new.astype(bf16)


def pair_lanes(heads_here):
    return -(-GROUP * heads_here // 2) * LANES


def attend(f, q, q_marks, key_marks, pieces, group):
    first, heads_here = group
    tokens = q.shape[1]
    blocks = key_marks.shape[0] // tokens
    rows = GROUP * tokens // 2
    piece = pl.BlockSpec((1, tokens, LANES), lambda g, f: (g, 0, 0))
    width = pair_lanes(heads_here)
    return pl.pallas_call(
        attend_kernel,
        grid_spec=pltpu.PrefetchScalarGridSpec(
            num_scalar_prefetch=1,
            grid=(heads_here,),
            in_specs=[
                pl.BlockSpec((GROUP, tokens, LANES), lambda g, f: (first + g, 0, 0)),
                pl.BlockSpec((tokens, LANES), lambda g, f: (0, 0)),
                pl.BlockSpec(key_marks.shape, lambda g, f: (0, 0)),
                piece,
                piece,
                piece,
                piece,
            ],
            out_specs=[
                pl.BlockSpec((tokens, width), lambda g, f: (0, 0)),
                pl.BlockSpec((GROUP, tokens, LANES), lambda g, f: (g, 0, 0)),
            ],
            scratch_shapes=[
                pltpu.VMEM((blocks, tokens, 2 * LANES), bf16),
                pltpu.VMEM((2, rows, 2 * LANES), bf16),
                pltpu.VMEM((5, rows, tokens), f32),
                pltpu.VMEM((5, rows, LANES), f32),
                pltpu.VMEM((2, rows, LANES), f32),
                pltpu.VMEM((2, rows, 2 * LANES), f32),
            ],
        ),
        out_shape=[
            jax.ShapeDtypeStruct((tokens, width), bf16),
            jax.ShapeDtypeStruct((GROUP * heads_here, tokens, LANES), bf16),
        ],
        compiler_params=params(26),
        cost_estimate=cost(4e10, 1e6),
        name="attend",
    )(f, q, q_marks, key_marks, *pieces)


def attend_back_kernel(
    f_ref, q, marks, key_marks, own, near, far, last, grad, attended, cos_ref, sin_ref,
    grad_q, keep, send, kvf, kv_sum, qf, df, turned, acc, ds_all, p_all,
):
    g = pl.program_id(0)
    f = f_ref[0]
    half = kvf.shape[1] // 2
    gather_keys(f, g == 0, (own, near, far, last), key_marks, kvf)
    kv_sum[...] = jnp.zeros(kv_sum.shape, f32)
    lane = lane_index((half, LANES))
    for b in (0, 1):
        outer = slice(b * half, (b + 1) * half)
        for i in range(GROUP):
            rows = slice(i * half, (i + 1) * half)
            qf[b, rows, :LANES] = q[i, outer, :]
            qf[b, rows, LANES:] = marks[i, outer, :]
            h = GROUP * g + i
            pair = pl.multiple_of((h // 2) * LANES, LANES)
            odd = h % 2 == 1
            d_tile = grad[outer, pl.ds(pair, LANES)].astype(f32)
            o_tile = attended[outer, pl.ds(pair, LANES)].astype(f32)
            mine = (lane >= HEAD) == odd
            inner = jnp.sum(jnp.where(mine, d_tile * o_tile, 0.0), axis=1, keepdims=True)
            moved = jnp.where(odd, d_tile, pltpu.roll(d_tile, HEAD, 1))
            moved = jnp.where(lane >= HEAD, moved, 0.0)
            df[b, rows, :LANES] = moved.astype(bf16)
            df[b, rows, LANES:] = three_terms(-inner, lane).astype(bf16)
            joined = moved + q[i, outer, :].astype(f32)
            turned[b, :, rows] = joined.T.astype(bf16)

    for n, (b, k, size, diagonal) in enumerate(score_parts(f)):
        wide = size * half
        keys = kvf[k, :wide, :]
        for i in range(GROUP):
            rows = slice(i * half, (i + 1) * half)
            p = jnp.exp2(nt(qf[b, rows, :], keys))
            if diagonal:
                p = jnp.where(causal(p.shape), p, 0.0)
            ds_all[rows, :wide] = (p * nt(df[b, rows, :], keys)).astype(bf16)
            p_all[rows, :wide] = p.astype(bf16)
        part = nn(ds_all[:, :wide], keys[:, :LANES])
        if n < 2:
            acc[b] = part
        else:
            acc[b] += part
        kv_sum[k, :HEAD, :wide] += nn(turned[b, :HEAD, :], ds_all[:, :wide])
        kv_sum[k, HEAD:, :wide] += nn(turned[b, HEAD:, :], p_all[:, :wide])

    scale = HEAD ** (-0.5)
    for b in (0, 1):
        outer = slice(b * half, (b + 1) * half)
        for i in range(GROUP):
            rows = slice(i * half, (i + 1) * half)
            h = GROUP * g + i
            pair = pl.multiple_of((h // 2) * LANES, LANES)
            odd = h % 2 == 1
            tile = acc[b, rows, :] * scale
            tile = tile * cos_ref[outer, :] - swap_halves(tile) * sin_ref[outer, :]
            other = pltpu.roll(tile, HEAD, 1)
            old = grad_q[outer, pl.ds(pair, LANES)].astype(f32)
            new = jnp.where(odd, jnp.where(lane >= HEAD, other, old), jnp.where(lane < HEAD, tile, 0.0))
            grad_q[outer, pl.ds(pair, LANES)] = new.astype(bf16)

    factor = jnp.where(lane < HEAD, LN2, 1.0)
    for m in range(4):
        device = f ^ m
        ref = send if m % 2 else keep
        ref[m // 2, 0, :half, :] = (kv_sum[device, :, :half].T * factor).astype(bf16)
        ref[m // 2, 0, half:, :] = (kv_sum[3 - device, :, half:].T * factor).astype(bf16)


def attend_back(f, q, marks, key_marks, pieces, grad, attended, cos, sin, group):
    first, heads_here = group
    tokens = q.shape[1]
    blocks = key_marks.shape[0] // tokens
    rows = GROUP * tokens // 2
    piece = pl.BlockSpec((1, tokens, LANES), lambda g, f: (g, 0, 0))
    width = pair_lanes(heads_here)
    whole = pl.BlockSpec((tokens, width), lambda g, f: (0, 0))
    table = pl.BlockSpec((tokens, LANES), lambda g, f: (0, 0))
    pair = pl.BlockSpec((2, 1, tokens, LANES), lambda g, f: (0, g, 0, 0))
    return pl.pallas_call(
        attend_back_kernel,
        grid_spec=pltpu.PrefetchScalarGridSpec(
            num_scalar_prefetch=1,
            grid=(heads_here,),
            in_specs=[
                pl.BlockSpec((GROUP, tokens, LANES), lambda g, f: (first + g, 0, 0)),
                pl.BlockSpec((GROUP, tokens, LANES), lambda g, f: (g, 0, 0)),
                pl.BlockSpec(key_marks.shape, lambda g, f: (0, 0)),
                piece,
                piece,
                piece,
                piece,
                whole,
                whole,
                table,
                table,
            ],
            out_specs=[whole, pair, pair],
            scratch_shapes=[
                pltpu.VMEM((blocks, tokens, 2 * LANES), bf16),
                pltpu.VMEM((blocks, LANES, tokens), f32),
                pltpu.VMEM((2, rows, 2 * LANES), bf16),
                pltpu.VMEM((2, rows, 2 * LANES), bf16),
                pltpu.VMEM((2, LANES, rows), bf16),
                pltpu.VMEM((2, rows, LANES), f32),
                pltpu.VMEM((rows, tokens), bf16),
                pltpu.VMEM((rows, tokens), bf16),
            ],
        ),
        out_shape=[
            jax.ShapeDtypeStruct((tokens, width), bf16),
            jax.ShapeDtypeStruct((2, heads_here, tokens, LANES), bf16),
            jax.ShapeDtypeStruct((2, heads_here, tokens, LANES), bf16),
        ],
        compiler_params=params(22),
        cost_estimate=cost(4e10, 1e6),
        name="attend_back",
    )(f, q, marks, key_marks, *pieces, grad, attended, cos, sin)


EPS = 1e-05
ANY = pl.BlockSpec(memory_space=pl.ANY)


def params(mib):
    return pltpu.CompilerParams(vmem_limit_bytes=mib * MIB)


def cost(flops, moved):
    return pl.CostEstimate(flops=int(flops), bytes_accessed=int(moved), transcendentals=0)


def row_copies(f, pieces, target, sems):
    rows = pieces[0].shape[0]
    return [
        pltpu.make_async_copy(
            piece, target.at[pl.ds(pl.multiple_of((f ^ m) * rows, 16), rows), :], sems.at[m]
        )
        for m, piece in enumerate(pieces)
    ]


def side_copies(info, bit, pieces, target, sems):
    f = info[0]
    rows = pieces[0].shape[0]
    copies = []
    for k, (m, which) in enumerate(((0, None), (1, None), (2, 0), (2, 1), (3, 0), (3, 1))):
        at = pl.ds(pl.multiple_of((f ^ m) * rows, 16), rows)
        if which is None:
            place = target.at[at, :]
        else:
            width = pieces[k].shape[1]
            place = target.at[at, pl.ds(pl.multiple_of((info[bit] ^ which) * width, width), width)]
        copies.append(pltpu.make_async_copy(pieces[k], place, sems.at[k]))
    return copies


def down_copies(info, bit, pieces, target, sems):
    f = info[0]
    width = pieces[0].shape[1]
    copies = []
    for k, (m, which) in enumerate(((0, None), (1, None), (2, 0), (2, 1), (3, 0), (3, 1))):
        at = pl.ds(pl.multiple_of((f ^ m) * width, width), width)
        if which is None:
            place = target.at[:, at]
        else:
            rows = pieces[k].shape[0]
            place = target.at[pl.ds(pl.multiple_of((info[bit] ^ which) * rows, 16), rows), at]
        copies.append(pltpu.make_async_copy(pieces[k], place, sems.at[k]))
    return copies


def start(copies):
    for copy in copies:
        copy.start()


def wait(copies):
    for copy in copies:
        copy.wait()


def inverse_of(values):
    return lax.rsqrt(jnp.mean(values * values, axis=-1, keepdims=True) + EPS)


def norm_back(upstream, values, gain):
    inverse = inverse_of(values)
    scaled = upstream * gain
    gain_grad = jnp.sum(upstream * (values * inverse), axis=0, keepdims=True)
    middle = jnp.mean(scaled * values, axis=-1, keepdims=True)
    return inverse * scaled - (inverse * inverse * inverse * middle) * values, gain_grad


def join_kernel(first, second, out, turned):
    half = out.shape[0] // 2
    turned[:, :half] = first[...]
    turned[:, half:] = second[...]
    out[:half, :] = first[...].T
    out[half:, :] = second[...].T


def join(turned, came):
    width, half = came.shape
    spec = pl.BlockSpec((width, half), lambda i: (0, 0))
    return pl.pallas_call(
        join_kernel,
        grid=(1,),
        in_specs=[spec, spec],
        out_specs=[
            pl.BlockSpec((2 * half, width), lambda i: (0, 0)),
            pl.BlockSpec((width, 2 * half), lambda i: (0, 0)),
        ],
        out_shape=[
            jax.ShapeDtypeStruct((2 * half, width), bf16),
            jax.ShapeDtypeStruct((width, 2 * half), bf16),
        ],
        compiler_params=params(16),
        cost_estimate=cost(4e10, 1e6),
        name="join",
    )(turned, came)


def part_kernel(f_ref, rows, first, second):
    half = rows.shape[0] // 2
    first[...] = rows[:half, :].T
    second[...] = rows[half:, :].T


def part(f, rows):
    tokens, width = rows.shape
    half = tokens // 2
    spec = pl.BlockSpec((width, half), lambda i, f: (0, 0))
    return pl.pallas_call(
        part_kernel,
        grid_spec=pltpu.PrefetchScalarGridSpec(
            num_scalar_prefetch=1,
            grid=(1,),
            in_specs=[pl.BlockSpec((tokens, width), lambda i, f: (0, 0))],
            out_specs=[spec, spec],
        ),
        out_shape=[jax.ShapeDtypeStruct((width, half), bf16)] * 2,
        compiler_params=params(16),
        cost_estimate=cost(4e9, 1e6),
        name="part",
    )(f, rows)


def pack_kernel(key_t, value_t, query, out):
    rows = []
    for g in range(KV_HEADS):
        rows += [key_t[g * HEAD : (g + 1) * HEAD, :], value_t[g * HEAD : (g + 1) * HEAD, :]]
    width = 2 * KV_HEADS * HEAD
    out[:, :width] = jnp.concatenate(rows, axis=0).T
    out[:, width : width + HEADS * HEAD] = query[...]
    out[:, width + HEADS * HEAD :] = jnp.zeros((out.shape[0], HEAD), bf16)


def pack(key, value, query):
    rows = key.shape[0]
    width = (2 * KV_HEADS + HEADS + 1) * HEAD
    full = lambda *shape: pl.BlockSpec(shape, lambda i: (0, 0))
    return pl.pallas_call(
        pack_kernel,
        grid=(1,),
        in_specs=[full(KV_HEADS * HEAD, rows)] * 2 + [full(*query.shape)],
        out_specs=full(rows, width),
        out_shape=jax.ShapeDtypeStruct((rows, width), bf16),
        compiler_params=params(16),
        cost_estimate=cost(4e10, 1e6),
        name="pack",
    )(key.T, value.T, query)


GROUPS = ((4, 1), (0, 2), (2, 2))
ORDER = (1, 2, 0)


def project_kernel(f_ref, h, gain, cos_ref, sin_ref, own, near, far, last, normed_t, q_out, *refs):
    kv_out, (w, sems) = refs[: len(GROUPS)], refs[len(GROUPS) :]
    copies = row_copies(f_ref[0], (own, near, far, last), w, sems)
    start(copies)
    hidden = h[...].astype(f32)
    normed = (hidden * inverse_of(hidden) * gain[...]).astype(bf16)
    normed_t[...] = normed.T
    cos, sin = cos_ref[...], sin_ref[...]
    lane = lane_index(cos.shape)
    kv_cos, kv_sin = jnp.where(lane < HEAD, cos, 1.0), jnp.where(lane < HEAD, sin, 0.0)
    wait(copies)
    first = KV_HEADS * LANES
    both = nn(normed, w[:, :first])
    for (start_head, heads_here), out in zip(GROUPS, kv_out):
        for i in range(heads_here):
            g = start_head + i
            tile = both[:, g * LANES : (g + 1) * LANES]
            out[i] = (tile * kv_cos + swap_halves(tile) * kv_sin).astype(bf16)
    query = nn(normed, w[:, first:])
    for p in range((HEADS + 1) // 2):
        tile = query[:, p * LANES : (p + 1) * LANES]
        tile = (tile * cos + swap_halves(tile) * sin) * (HEAD ** (-0.5) * LOG2E)
        q_out[2 * p] = jnp.where(lane < HEAD, tile, 0.0).astype(bf16)
        if 2 * p + 1 < HEADS:
            q_out[2 * p + 1] = jnp.where(lane < HEAD, pltpu.roll(tile, HEAD, 1), 0.0).astype(bf16)


def project(f, hidden, gain, cos, sin, pieces):
    tokens, width = hidden.shape
    rows, columns = pieces[0].shape
    full = lambda *shape: pl.BlockSpec(shape, lambda i, f: (0,) * len(shape))
    like = jax.ShapeDtypeStruct
    return pl.pallas_call(
        project_kernel,
        grid_spec=pltpu.PrefetchScalarGridSpec(
            num_scalar_prefetch=1,
            grid=(1,),
            in_specs=[full(tokens, width), full(1, width), full(*cos.shape), full(*sin.shape)] + [ANY] * 4,
            out_specs=[full(width, tokens), full(HEADS, tokens, LANES)]
            + [full(heads_here, tokens, LANES) for _, heads_here in GROUPS],
            scratch_shapes=[pltpu.VMEM((4 * rows, columns), bf16), pltpu.SemaphoreType.DMA((4,))],
        ),
        out_shape=[like((width, tokens), bf16), like((HEADS, tokens, LANES), bf16)]
        + [like((heads_here, tokens, LANES), bf16) for _, heads_here in GROUPS],
        compiler_params=params(20),
        cost_estimate=cost(4e10, 1e6),
        name="project",
    )(f, hidden, gain, cos, sin, *pieces)


PARTS = len(GROUPS)


def split_pieces(refs):
    return refs[:4], refs[4:10], refs[10:16], refs[16:22], refs[22:]


CHUNK = 256


def feed_kernel(f_ref, h, *refs):
    attended, gain = refs[:PARTS], refs[PARTS]
    o, gate, up, down, refs = split_pieces(refs[PARTS + 1 :])
    outs, result = refs[:6], refs[6]
    w_o, w_gate, w_up, w_down, n16, *refs = refs[7:]
    after, attended_t, normed_t, gate_out, up_out, hidden_out = refs[:6]
    o_sem, gate_sem, up_sem, down_sem, out_sem = refs[6:]
    depth, wide = 4 * o[0].shape[0], w_gate.shape[1]
    o_copies = row_copies(f_ref[0], o, w_o, o_sem)
    gate_copies = side_copies(f_ref, 1, gate, w_gate, gate_sem)
    up_copies = side_copies(f_ref, 2, up, w_up, up_sem)
    d_copies = down_copies(f_ref, 1, down, w_down, down_sem)
    half = wide // 2

    def leave(k, part=None):
        if part is None:
            return pltpu.make_async_copy(refs[k], outs[k], out_sem.at[k, 0])
        columns = slice(part * half, (part + 1) * half)
        return pltpu.make_async_copy(refs[k].at[:, columns], outs[k].at[:, columns], out_sem.at[k, part])

    leaving = [leave(k) for k in range(3)] + [leave(k, part) for part in (0, 1) for k in (3, 4, 5)]
    for copies in (o_copies, gate_copies, up_copies, d_copies):
        start(copies)
    att = jnp.concatenate([attended[i][...] for i in ORDER], axis=1)
    attended_t[...] = att.T
    w_o[depth:, :] = jnp.zeros((w_o.shape[0] - depth, w_o.shape[1]), bf16)
    wait(o_copies)
    value = h[...].astype(f32) + nn(att, w_o[...])
    after[...] = value
    normed = (value * inverse_of(value) * gain[...]).astype(bf16)
    n16[...] = normed
    normed_t[...] = normed.T
    wait(gate_copies)
    wait(up_copies)
    for at in range(0, wide, CHUNK):
        columns = slice(at, at + CHUNK)
        gate_act = nn(n16[...], w_gate[:, columns])
        up_act = nn(n16[...], w_up[:, columns])
        hidden = gate_act * jax.nn.sigmoid(gate_act) * up_act
        gate_out[:, columns] = gate_act.astype(bf16)
        up_out[:, columns] = up_act.astype(bf16)
        hidden_out[:, columns] = hidden.astype(bf16)
        if at + CHUNK == half:
            start(leaving[:6])
    start(leaving[6:])
    wait(d_copies)
    result[...] = (after[...] + nt(hidden_out[...], w_down[...])).astype(result.dtype)
    wait(leaving)


def weight_scratch(o, gate):
    rows, width = o.shape
    columns = gate.shape[1]
    return [
        pltpu.VMEM((4 * rows + HEAD, width), bf16),
        pltpu.VMEM((4 * rows, columns), bf16),
        pltpu.VMEM((4 * rows, columns), bf16),
        pltpu.VMEM((width, columns), bf16),
    ]


def weight_sems():
    dma = pltpu.SemaphoreType.DMA
    return [dma((4,)), dma((6,)), dma((6,)), dma((6,))]


def feed(f, hidden, attended, gain, o, gate, up, down, result_type):
    tokens, width = hidden.shape
    wide = gate[0].shape[1]
    lanes = (HEADS + 1) * HEAD
    full = lambda *shape: pl.BlockSpec(shape, lambda i, f: (0,) * len(shape))
    like = jax.ShapeDtypeStruct
    kept = [((tokens, width), f32), ((lanes, tokens), bf16), ((width, tokens), bf16)] + [((tokens, wide), bf16)] * 3
    return pl.pallas_call(
        feed_kernel,
        grid_spec=pltpu.PrefetchScalarGridSpec(
            num_scalar_prefetch=1,
            grid=(1,),
            in_specs=[full(tokens, width)] + [full(*a.shape) for a in attended] + [full(1, width)] + [ANY] * 22,
            out_specs=[ANY] * 6 + [full(tokens, width)],
            scratch_shapes=weight_scratch(o[0], gate[0])
            + [pltpu.VMEM((tokens, width), bf16)]
            + [pltpu.VMEM(*k) for k in kept]
            + weight_sems()
            + [pltpu.SemaphoreType.DMA((6, 2))],
        ),
        out_shape=[like(*k) for k in kept] + [like((tokens, width), result_type)],
        compiler_params=params(48),
        cost_estimate=cost(4e10, 1e6),
        name="feed",
    )(f, hidden, *attended, gain, *o, *gate, *up, *down)


def feed_back_kernel(f_ref, g, gain, *refs):
    held = refs[:3]
    o, gate, up, down, refs = split_pieces(refs[3:])
    outs, grad_after, branch_out = refs[:2], refs[2], refs[3]
    grad_attended, gain_grad = refs[4 : 4 + PARTS], refs[4 + PARTS]
    w_o, w_gate, w_up, w_down, g16, *refs = refs[5 + PARTS :]
    after, gate_act, up_act, grad_gate, grad_up, o_sem, gate_sem, up_sem, down_sem, in_sem, out_sem = refs
    depth, wide = 4 * o[0].shape[0], w_gate.shape[1]
    half = wide // 2
    o_copies = row_copies(f_ref[0], o, w_o, o_sem)
    gate_copies = side_copies(f_ref, 1, gate, w_gate, gate_sem)
    up_copies = side_copies(f_ref, 2, up, w_up, up_sem)
    d_copies = down_copies(f_ref, 1, down, w_down, down_sem)

    def act_copies(part):
        columns = slice(part * half, (part + 1) * half)
        return [
            pltpu.make_async_copy(held[k].at[:, columns], refs[k].at[:, columns], in_sem.at[k, part]) for k in (1, 2)
        ]

    after_copy = pltpu.make_async_copy(held[0], after, in_sem.at[0, 0])
    leave = [pltpu.make_async_copy(refs[3 + k], outs[k], out_sem.at[k]) for k in (0, 1)]
    first, second = act_copies(0), act_copies(1)
    for copies in (d_copies, first, second, gate_copies, up_copies, [after_copy], o_copies):
        start(copies)
    g16[...] = g[...].astype(bf16)
    w_o[depth:, :] = jnp.zeros((w_o.shape[0] - depth, w_o.shape[1]), bf16)
    wait(d_copies)
    for part, copies in enumerate((first, second)):
        wait(copies)
        for at in range(part * half, (part + 1) * half, CHUNK):
            columns = slice(at, at + CHUNK)
            grad_hidden = nn(g16[...], w_down[:, columns])
            value = gate_act[:, columns].astype(f32)
            logistic = jax.nn.sigmoid(value)
            steep = logistic * (1.0 + value * (1.0 - logistic))
            grad_gate[:, columns] = (grad_hidden * up_act[:, columns].astype(f32) * steep).astype(bf16)
            grad_up[:, columns] = (grad_hidden * (value * logistic)).astype(bf16)
    wait(gate_copies)
    wait(up_copies)
    start(leave)
    grad_normed = nt(grad_gate[...], w_gate[...]) + nt(grad_up[...], w_up[...])
    wait([after_copy])
    wait(o_copies)
    back, gain_part = norm_back(grad_normed, after[...], gain[...])
    back = back + g[...].astype(f32)
    gain_grad[...] = gain_part
    grad_after[...] = back
    branch = back.astype(bf16)
    branch_out[...] = branch
    whole = nt(branch, w_o[...]).astype(bf16)
    at = 0
    for i in ORDER:
        lanes = grad_attended[i].shape[1]
        grad_attended[i][...] = whole[:, at : at + lanes]
        at += lanes
    wait(leave)


def feed_back(f, g, after, gain, gate_act, up_act, o, gate, up, down):
    tokens, width = after.shape
    wide = gate[0].shape[1]
    full = lambda *shape: pl.BlockSpec(shape, lambda i, f: (0,) * len(shape))
    like = jax.ShapeDtypeStruct
    lanes = [pair_lanes(heads_here) for _, heads_here in GROUPS]
    dma = pltpu.SemaphoreType.DMA
    return pl.pallas_call(
        feed_back_kernel,
        grid_spec=pltpu.PrefetchScalarGridSpec(
            num_scalar_prefetch=1,
            grid=(1,),
            in_specs=[full(tokens, width), full(1, width)] + [ANY] * 25,
            out_specs=[ANY, ANY, full(tokens, width), full(tokens, width)]
            + [full(tokens, n) for n in lanes]
            + [full(1, width)],
            scratch_shapes=weight_scratch(o[0], gate[0])
            + [pltpu.VMEM((tokens, width), bf16), pltpu.VMEM((tokens, width), f32)]
            + [pltpu.VMEM((tokens, wide), bf16)] * 4
            + weight_sems()
            + [dma((3, 2)), dma((2,))],
        ),
        out_shape=[like((tokens, wide), bf16)] * 2
        + [like((tokens, width), f32), like((tokens, width), bf16)]
        + [like((tokens, n), bf16) for n in lanes]
        + [like((1, width), f32)],
        compiler_params=params(52),
        cost_estimate=cost(4e10, 1e6),
        name="feed_back",
    )(f, g, gain, after, gate_act, up_act, *o, *gate, *up, *down)


def feed_turn_kernel(f_ref, h, g, *refs):
    attended, gain = refs[:PARTS], refs[PARTS]
    o, gate, up, down, refs = split_pieces(refs[PARTS + 1 :])
    outs, result, grad_after, branch_out = refs[:5], refs[5], refs[6], refs[7]
    grad_attended, gain_grad = refs[8 : 8 + PARTS], refs[8 + PARTS]
    w_o, w_gate, w_up, w_down, n16, after, gate_out, up_out, *refs = refs[9 + PARTS :]
    attended_t, normed_t, hidden_out, grad_gate, grad_up = refs[:5]
    o_sem, gate_sem, up_sem, down_sem, out_sem = refs[5:]
    depth, wide = 4 * o[0].shape[0], w_gate.shape[1]
    o_copies = row_copies(f_ref[0], o, w_o, o_sem)
    gate_copies = side_copies(f_ref, 1, gate, w_gate, gate_sem)
    up_copies = side_copies(f_ref, 2, up, w_up, up_sem)
    d_copies = down_copies(f_ref, 1, down, w_down, down_sem)
    leaving = [pltpu.make_async_copy(refs[k], outs[k], out_sem.at[k]) for k in range(5)]
    for copies in (o_copies, gate_copies, up_copies, d_copies):
        start(copies)
    att = jnp.concatenate([attended[i][...] for i in ORDER], axis=1)
    attended_t[...] = att.T
    w_o[depth:, :] = jnp.zeros((w_o.shape[0] - depth, w_o.shape[1]), bf16)
    wait(o_copies)
    value = h[...].astype(f32) + nn(att, w_o[...])
    after[...] = value
    normed = (value * inverse_of(value) * gain[...]).astype(bf16)
    n16[...] = normed
    normed_t[...] = normed.T
    wait(gate_copies)
    wait(up_copies)
    for at in range(0, wide, CHUNK):
        columns = slice(at, at + CHUNK)
        gate_act = nn(n16[...], w_gate[:, columns])
        up_act = nn(n16[...], w_up[:, columns])
        gate_out[:, columns] = gate_act.astype(bf16)
        up_out[:, columns] = up_act.astype(bf16)
        hidden_out[:, columns] = (gate_act * jax.nn.sigmoid(gate_act) * up_act).astype(bf16)
    start(leaving[:3])
    wait(d_copies)
    result[...] = (after[...] + nt(hidden_out[...], w_down[...])).astype(result.dtype)
    for at in range(0, wide, CHUNK):
        columns = slice(at, at + CHUNK)
        grad_hidden = nn(g[...], w_down[:, columns])
        value = gate_out[:, columns].astype(f32)
        logistic = jax.nn.sigmoid(value)
        steep = logistic * (1.0 + value * (1.0 - logistic))
        grad_gate[:, columns] = (grad_hidden * up_out[:, columns].astype(f32) * steep).astype(bf16)
        grad_up[:, columns] = (grad_hidden * (value * logistic)).astype(bf16)
    start(leaving[3:])
    grad_normed = nt(grad_gate[...], w_gate[...]) + nt(grad_up[...], w_up[...])
    back, gain_part = norm_back(grad_normed, after[...], gain[...])
    back = back + g[...].astype(f32)
    gain_grad[...] = gain_part
    grad_after[...] = back
    branch = back.astype(bf16)
    branch_out[...] = branch
    whole = nt(branch, w_o[...]).astype(bf16)
    at = 0
    for i in ORDER:
        lanes = grad_attended[i].shape[1]
        grad_attended[i][...] = whole[:, at : at + lanes]
        at += lanes
    wait(leaving)


def feed_turn(f, hidden, g, attended, gain, o, gate, up, down):
    tokens, width = hidden.shape
    wide = gate[0].shape[1]
    full = lambda *shape: pl.BlockSpec(shape, lambda i, f: (0,) * len(shape))
    like = jax.ShapeDtypeStruct
    lanes = [pair_lanes(heads_here) for _, heads_here in GROUPS]
    kept = [(((HEADS + 1) * HEAD, tokens), bf16), ((width, tokens), bf16)] + [((tokens, wide), bf16)] * 3
    return pl.pallas_call(
        feed_turn_kernel,
        grid_spec=pltpu.PrefetchScalarGridSpec(
            num_scalar_prefetch=1,
            grid=(1,),
            in_specs=[full(tokens, width)] * 2 + [full(*a.shape) for a in attended] + [full(1, width)] + [ANY] * 22,
            out_specs=[ANY] * 5
            + [full(tokens, width)] * 3
            + [full(tokens, n) for n in lanes]
            + [full(1, width)],
            scratch_shapes=weight_scratch(o[0], gate[0])
            + [pltpu.VMEM((tokens, width), bf16), pltpu.VMEM((tokens, width), f32)]
            + [pltpu.VMEM((tokens, wide), bf16)] * 2
            + [pltpu.VMEM(*k) for k in kept]
            + weight_sems()
            + [pltpu.SemaphoreType.DMA((5,))],
        ),
        out_shape=[like(*k) for k in kept]
        + [like((tokens, width), bf16), like((tokens, width), f32), like((tokens, width), bf16)]
        + [like((tokens, n), bf16) for n in lanes]
        + [like((1, width), f32)],
        compiler_params=params(60),
        cost_estimate=cost(4e10, 1e6),
        name="feed_turn",
    )(f, hidden, g, *attended, gain, *o, *gate, *up, *down)


def project_back_kernel(f_ref, *refs):
    grad_q, kept, came = refs[:PARTS], refs[PARTS : 2 * PARTS], refs[2 * PARTS : 3 * PARTS]
    cos_ref, sin_ref, h, gain, grad_after, own, near, far, last = refs[3 * PARTS : 3 * PARTS + 9]
    grads, grad_in, turned, gain_grad, w, sems = refs[3 * PARTS + 9 :]
    copies = row_copies(f_ref[0], (own, near, far, last), w, sems)
    start(copies)
    cos, sin = cos_ref[...], sin_ref[...]
    lane = lane_index(cos.shape)
    cos, sin = jnp.where(lane < HEAD, cos, 1.0), jnp.where(lane < HEAD, sin, 0.0)
    at = KV_HEADS * LANES
    for k in ORDER:
        first, heads_here = GROUPS[k]
        for i in range(heads_here):
            g = first + i
            tile = kept[k][i].astype(f32) + came[k][i].astype(f32)
            tile = tile * cos - swap_halves(tile) * sin
            grads[:, g * LANES : (g + 1) * LANES] = tile.astype(bf16)
        lanes = grad_q[k].shape[1]
        grads[:, at : at + lanes] = grad_q[k][...]
        at += lanes
    wait(copies)
    grad_normed = nt(grads[...], w[...])
    back, gain_part = norm_back(grad_normed, h[...].astype(f32), gain[...])
    gain_grad[...] = gain_part
    back = back + grad_after[...]
    grad_in[...] = back.astype(grad_in.dtype)
    turned[...] = back.astype(bf16).T


def project_back(f, grad_q, kept, came, cos, sin, hidden, gain, grad_after, pieces, result_type):
    tokens, width = hidden.shape
    rows, columns = pieces[0].shape
    full = lambda *shape: pl.BlockSpec(shape, lambda i, f: (0,) * len(shape))
    like = jax.ShapeDtypeStruct
    arrays = (*grad_q, *kept, *came, cos, sin, hidden, gain, grad_after)
    return pl.pallas_call(
        project_back_kernel,
        grid_spec=pltpu.PrefetchScalarGridSpec(
            num_scalar_prefetch=1,
            grid=(1,),
            in_specs=[full(*a.shape) for a in arrays] + [ANY] * 4,
            out_specs=[full(tokens, columns), full(tokens, width), full(width, tokens), full(1, width)],
            scratch_shapes=[pltpu.VMEM((4 * rows, columns), bf16), pltpu.SemaphoreType.DMA((4,))],
        ),
        out_shape=[
            like((tokens, columns), bf16),
            like((tokens, width), result_type),
            like((width, tokens), bf16),
            like((1, width), f32),
        ],
        compiler_params=params(20),
        cost_estimate=cost(4e10, 1e6),
        name="project_back",
    )(f, *arrays, *pieces)


def joined(left_first, left_second, right_first, right_second):
    left = jnp.concatenate([left_first, left_second], axis=1)
    return nn(left, jnp.concatenate([right_first, right_second], axis=0))


def outer_tiles_kernel(f_ref, left_first, left_second, right_first, right_second, *refs, rows):
    outs, acc = refs[:4], refs[4]
    acc[...] = joined(left_first[...], left_second[...], right_first[...], right_second[...])
    half = acc.shape[1] // 2
    for m in range(4):
        from_row = pl.multiple_of((f_ref[0] ^ m) * rows, 16)
        for c in (0, 1):
            outs[m][c] = acc[pl.ds(from_row, rows), c * half : (c + 1) * half].astype(bf16)


def outer_tiles(f, lefts, rights, rows, name):
    width, tokens = lefts[0].shape
    wide = rights[0].shape[1] // 2
    left = pl.BlockSpec((width, tokens), lambda i, f: (0, 0))
    right = pl.BlockSpec((tokens, wide), lambda i, f: (0, i))
    out = pl.BlockSpec((2, rows, wide // 2), lambda i, f: (i, 0, 0))
    return pl.pallas_call(
        functools.partial(outer_tiles_kernel, rows=rows),
        grid_spec=pltpu.PrefetchScalarGridSpec(
            num_scalar_prefetch=1,
            grid=(2,),
            in_specs=[left, left, right, right],
            out_specs=[out] * 4,
            scratch_shapes=[pltpu.VMEM((width, wide), f32)],
        ),
        out_shape=[jax.ShapeDtypeStruct((4, rows, wide // 2), bf16)] * 4,
        compiler_params=params(28),
        cost_estimate=cost(4e10, 1e6),
        name=name,
    )(f, *lefts, *rights)


def outer_down_kernel(f_ref, left_first, left_second, right_first, right_second, own, near):
    value = joined(left_first[...], left_second[...], right_first[...], right_second[...])
    half = value.shape[1] // 2
    first = (f_ref[0] & 1) == 0
    lower, upper = value[:, :half], value[:, half:]
    own[0] = jnp.where(first, lower, upper).astype(bf16)
    near[0] = jnp.where(first, upper, lower).astype(bf16)


def outer_down(f, lefts, rights, chip, name):
    width, tokens = lefts[0].shape
    wide = rights[0].shape[1] // 2
    left = pl.BlockSpec((width, tokens), lambda i, f: (0, 0))
    right = pl.BlockSpec((tokens, wide), lambda i, f: (0, (f[0] >> 1) ^ chip))
    out = pl.BlockSpec((1, width, wide // 2), lambda i, f: (0, 0, 0))
    return pl.pallas_call(
        outer_down_kernel,
        grid_spec=pltpu.PrefetchScalarGridSpec(
            num_scalar_prefetch=1,
            grid=(1,),
            in_specs=[left, left, right, right],
            out_specs=[out, out],
        ),
        out_shape=[jax.ShapeDtypeStruct((1, width, wide // 2), bf16)] * 2,
        compiler_params=params(28),
        cost_estimate=cost(4e10, 1e6),
        name=name,
    )(f, *lefts, *rights)


def outer_kernel(f_ref, left_first, left_second, right_first, right_second, extra, *refs, rows):
    outs, acc = refs[:4], refs[4]
    acc[...] = joined(left_first[...], left_second[...], right_first[...], right_second[...])
    columns = acc.shape[1]
    for m in range(4):
        device = f_ref[0] ^ m
        out = outs[m]
        if columns < out.shape[2]:
            out[0, :, columns:] = jnp.zeros((out.shape[1], out.shape[2] - columns), bf16)
        out[0, :rows, :columns] = acc[pl.ds(pl.multiple_of(device * rows, 16), rows), :].astype(bf16)
        out[0, rows:, :columns] = jnp.zeros((out.shape[1] - rows, columns), bf16)
        out[0, rows:, : extra.shape[2]] = extra[device]


def outer(f, lefts, rights, extra, rows, name):
    width, tokens = lefts[0].shape
    height, columns = 4 * rows, rights[0].shape[1]
    shape = (1, rows + extra.shape[1], -(-columns // LANES) * LANES)
    full = lambda *shape: pl.BlockSpec(shape, lambda i, f: (0,) * len(shape))
    return pl.pallas_call(
        functools.partial(outer_kernel, rows=rows),
        grid_spec=pltpu.PrefetchScalarGridSpec(
            num_scalar_prefetch=1,
            grid=(1,),
            in_specs=[full(height, tokens)] * 2 + [full(tokens, columns)] * 2 + [full(*extra.shape)],
            out_specs=[full(*shape)] * 4,
            scratch_shapes=[pltpu.VMEM((height, columns), f32)],
        ),
        out_shape=[jax.ShapeDtypeStruct(shape, bf16)] * 4,
        compiler_params=params(28),
        cost_estimate=cost(4e10, 1e6),
        name=name,
    )(f, *lefts, *rights, extra)


def unpack_kernel(total, key_t, value_t, query):
    rows = query.shape[0]
    width = 2 * KV_HEADS * HEAD
    turned = total[:rows, :width].astype(f32).T
    for g in range(KV_HEADS):
        key_t[g * HEAD : (g + 1) * HEAD, :] = turned[2 * g * HEAD : (2 * g + 1) * HEAD, :]
        value_t[g * HEAD : (g + 1) * HEAD, :] = turned[(2 * g + 1) * HEAD : (2 * g + 2) * HEAD, :]
    query[...] = total[:rows, width : width + HEADS * HEAD].astype(f32)


def unpack(total, rows):
    full = lambda *shape: pl.BlockSpec(shape, lambda i: (0, 0))
    like = jax.ShapeDtypeStruct
    side = (KV_HEADS * HEAD, rows)
    key_t, value_t, query = pl.pallas_call(
        unpack_kernel,
        grid=(1,),
        in_specs=[full(*total.shape)],
        out_specs=[full(*side), full(*side), full(rows, HEADS * HEAD)],
        out_shape=[like(side, f32), like(side, f32), like((rows, HEADS * HEAD), f32)],
        compiler_params=params(16),
        cost_estimate=cost(4e10, 1e6),
        name="unpack",
    )(total)
    return key_t.T, value_t.T, query


def flip(array, axis, bit):
    size = lax.axis_size(axis)
    return lax.ppermute(array, axis, [(i, i ^ bit) for i in range(size)])


def add(left, right):
    return left.astype(f32) + right.astype(f32)


def levels_of(size):
    return [(bit, 2) for bit in range(size.bit_length() - 1)]


def cut(array, count):
    blocks, rows, columns = array.shape
    outer = next(n for n in (4, 2, 1) if n <= count and blocks % n == 0)
    inner = count // outer
    array = array.reshape(outer, blocks // outer, inner, rows // inner, columns)
    return [array[i // inner, :, i % inner] for i in range(count)]


def glue(parts, shape):
    count = len(parts)
    outer = next(n for n in (4, 2, 1) if n <= count and shape[0] % n == 0)
    inner = count // outer
    rows = [jnp.concatenate(parts[i * inner : (i + 1) * inner], axis=1) for i in range(outer)]
    return jnp.concatenate(rows, axis=0).reshape(shape)


def pick(parts, index):
    while len(parts) > 1:
        odd = index % 2 == 1
        parts = [jnp.where(odd, parts[i + 1], parts[i]) for i in range(0, len(parts), 2)]
        index = index // 2
    return parts[0]


def reduction(own, near, far, last, halves):
    shape = own.shape
    if last is None:
        beside, first = yield [(near, "fsdp", 1), (far, "fsdp", 2)]
        crossed = [first]
    else:
        came, beside = yield [(last, "fsdp", 1), (near, "fsdp", 1)]
        crossed = []
        for ours, theirs in zip(cut(far, halves), cut(came, halves)):
            crossed += yield [(add(ours, theirs).astype(bf16), "fsdp", 2)]
    crossed = glue(crossed, shape) if halves > 1 else crossed[0]
    part = add(own, beside) + crossed.astype(f32)
    index = lax.axis_index("dp")
    shapes = []
    for bit, count in levels_of(lax.axis_size("dp")):
        shapes.append(part.shape)
        parts = cut(part, count)
        mine = (index >> bit) % count
        came = yield [(pick(parts, mine ^ j).astype(bf16), "dp", j << bit) for j in range(1, count)]
        part = pick(parts, mine).astype(f32)
        for other in came:
            part = part + other.astype(f32)
    part = part.astype(bf16)
    for (bit, count), wide in zip(reversed(levels_of(lax.axis_size("dp"))), reversed(shapes)):
        came = yield [(part, "dp", j << bit) for j in range(1, count)]
        mine = (index >> bit) % count
        held = [part] + came
        part = glue([pick(held, mine ^ p) for p in range(count)], wide)
    return part


class Unit:
    def __init__(self, own, near, far, last, halves=1):
        self.steps = reduction(own, near, far, last, halves)
        self.asks = next(self.steps)
        self.total = None

    def take(self, came):
        try:
            self.asks = self.steps.send(came)
        except StopIteration as end:
            self.asks, self.total = [], end.value


class Clock:
    def __init__(self, f):
        self.f = f
        self.before = []

    def phase(self, moves=(), work=None, units=(), extra=()):
        asks = list(moves)
        for unit in units:
            asks += unit.asks
        gated = lax.optimization_barrier((self.f, *(a[0] for a in asks), *extra, *self.before))
        came = [flip(g, axis, bit) for g, (_, axis, bit) in zip(gated[1:], asks)]
        done = None if work is None else work(gated[0])
        self.before = list(came) + ([] if done is None else [jax.tree.leaves(done)[0]])
        at = len(moves)
        for unit in units:
            count = len(unit.asks)
            unit.take(came[at : at + count])
            at += count
        return came[: len(moves)], done


def half_for(shard, low_first, dim):
    width = shard.shape[dim] // 2
    low = lax.slice_in_dim(shard, 0, width, axis=dim)
    high = lax.slice_in_dim(shard, width, 2 * width, axis=dim)
    return jnp.where(low_first, low, high)


def per_device(
    tokens, seq_cuts, w_query, w_key, w_value, w_output, w_gate, w_up, w_down, gain_attn, gain_ffn, cotangent
):
    rows, width = tokens.shape[1], tokens.shape[2]
    half = rows // 2
    index = lax.axis_index("fsdp")
    replica = lax.axis_index("dp")
    f = jnp.stack([index, replica % 2, replica // 2 % 2]).astype(jnp.int32)
    count = rows * lax.axis_size("fsdp")
    shard_rows = w_key.shape[0]
    core, y = ("fsdp", 1), ("fsdp", 2)
    side = (("dp", 1), ("dp", 2))

    bounds = seq_cuts[0]
    within = jnp.arange(half, dtype=jnp.int32)
    local = jnp.concatenate([2 * index * half + within, (7 - 2 * index) * half + within]).astype(jnp.int32)
    every = jnp.arange(count, dtype=jnp.int32)
    passed = local[:, None] >= bounds[None, :]
    docs = jnp.sum(passed.astype(jnp.int32), axis=1)
    positions = local - jnp.max(jnp.where(passed, bounds[None, :], 0), axis=1)
    key_docs = jnp.sum((every[:, None] >= bounds[None, :]).astype(jnp.int32), axis=1)
    lane = jnp.arange(LANES, dtype=jnp.int32)[None, :]
    one = ((lane == key_docs[:, None]) & (lane < 4)) | ((lane >= 8) & (lane < 11))
    key_marks = one.astype(bf16)
    q_marks = jnp.where((lane < 4) & (lane != docs[:, None]), NEGATIVE, 0.0).astype(bf16)
    frequency = jnp.power(10000.0, -2.0 * jnp.arange(HEAD // 2, dtype=f32) / HEAD)
    angle = positions.astype(f32)[:, None] * frequency[None, :]
    cosine, sine = jnp.cos(angle), jnp.sin(angle)
    cos = jnp.concatenate([cosine] * 4, axis=1)
    sin = jnp.concatenate([-sine, sine] * 2, axis=1)
    gain_a, gain_f = gain_attn[None, :], gain_ffn[None, :]

    clock = Clock(f)
    tokens_t, cotangent_t, down_t = tokens[0].T, cotangent[0].T, w_down.T
    shards = {"gate": w_gate, "up": w_up, "down": down_t}
    bit_of, dim_of = {"gate": 0, "up": 1, "down": 0}, {"gate": 1, "up": 1, "down": 0}
    across = lambda name: (half_for(shards[name], f[1 + bit_of[name]] == 0, dim_of[name]), *y)

    w_own = pack(w_key, w_value, w_query)
    (w_far, w_near, other_tokens), _ = clock.phase([(w_own, *y), (w_own, *core), (tokens_t[:, half:], "fsdp", 3)])
    (w_last, gate_far), (h0, _) = clock.phase(
        [(w_far, *core), across("gate")], lambda turn: join(tokens_t, other_tokens), extra=(key_marks, q_marks, cos, sin)
    )
    w_in = (w_own, w_near, w_far, w_last)

    def attend_phases(hidden, first, moves):
        came = []
        got, (normed_t, q, *parts) = clock.phase(first, lambda turn: project(turn, hidden, gain_a, cos, sin, w_in))
        came.append(got)
        a, b, c = parts
        got, _ = clock.phase([(a, *y), (a, *core), (b, *core)] + moves[0](came))
        a_far, a_near, b_near = got[:3]
        came.append(got[3:])
        got, _ = clock.phase([(a_far, *core), (b, *y), (c, *core)] + moves[1](came))
        a_last, b_far, c_near = got[:3]
        came.append(got[3:])
        gathered = [(a, a_near, a_far, a_last)]
        attended, marks = [], []

        def call(k):
            return lambda turn: attend(turn, q, q_marks, key_marks, gathered[k], GROUPS[k])

        got, (x, m) = clock.phase([(b_far, *core), (c, *y)] + moves[2](came), call(0))
        attended.append(x), marks.append(m)
        b_last, c_far = got[:2]
        came.append(got[2:])
        gathered.append((b, b_near, b_far, b_last))
        got, (x, m) = clock.phase([(c_far, *core)] + moves[3](came), call(1))
        attended.append(x), marks.append(m)
        came.append(got[1:])
        gathered.append((c, c_near, c_far, got[0]))
        got, (x, m) = clock.phase(moves[4](came), call(2))
        attended.append(x), marks.append(m)
        came.append(got)
        return (normed_t, q, gathered, attended, marks), came

    def feed_phase(hidden, weights, run, result_type, moves=()):
        normed_t, q, gathered, attended, marks = run
        got, (after, attended_t, normed_ffn_t, gate_act, up_act, hidden_act, result) = clock.phase(
            moves, lambda turn: feed(turn, hidden, attended, gain_f, *weights, result_type)
        )
        return result, got, (
            hidden, normed_t, q, gathered, attended, marks, after, attended_t, normed_ffn_t, gate_act, up_act, hidden_act,
        )

    none = lambda came: []
    run, came = attend_phases(
        h0,
        [across("up"), (gate_far, *side[0])],
        (
            lambda came: [(w_output, *core), (w_gate, *core)],
            lambda came: [across("down"), (came[0][0], *side[1])],
            lambda came: [(w_output, *y), (came[2][0], *side[0]), (w_up, *core)],
            lambda came: [(gate_far, *core), (came[0][1], *core), (came[0][0], *core), (came[2][1], *core)],
            lambda came: [(came[2][0], *core), (came[3][1], *core), (down_t, *core), (came[3][0], *core)],
        ),
    )
    up_far, gate_other = came[0]
    down_far, up_other = came[2]
    o_near, gate_near = came[1]
    o_far, down_other, up_near = came[3]
    gate_last, gate_other_last, up_last, up_other_last = came[4]
    down_last, down_other_last, down_near, o_last = came[5]
    weights = (
        (w_output, o_near, o_far, o_last),
        (w_gate, gate_near, gate_far, gate_other, gate_last, gate_other_last),
        (w_up, up_near, up_far, up_other, up_last, up_other_last),
        (down_t, down_near, down_far, down_other, down_last, down_other_last),
    )
    h1, (other_cotangent,), first = feed_phase(h0, weights, run, f32, [(cotangent_t[:, half:], "fsdp", 3)])
    run, _ = attend_phases(h1, [], (none,) * 5)
    cot, cot_turned = join(cotangent_t, other_cotangent)
    _, turn_out = clock.phase((), lambda turn: feed_turn(turn, h1, cot, run[3], gain_f, *weights))
    attended_t, normed_ffn_t, hidden_act, grad_gate, grad_up, h2, *rest = turn_out
    second = (h1, run[0], run[1], run[2], run[3], run[4], None, attended_t, normed_ffn_t, None, None, hidden_act)
    fed2 = (grad_gate, grad_up, *rest)

    def feed_back_work(g, stored):
        return lambda turn: feed_back(turn, g, stored[6], gain_f, stored[9], stored[10], *weights)

    BACK = (1, 2, 0)

    def back_phases(grad_attended, stored, beside):
        q, gathered, attended, marks = stored[2], stored[3], stored[4], stored[5]
        grad_q, kept, far = [None] * PARTS, [None] * PARTS, [None] * PARTS
        extra = []

        def call(k):
            return lambda turn: attend_back(
                turn, q, marks[k], key_marks, gathered[k], grad_attended[k], attended[k], cos, sin, GROUPS[k]
            )

        def sums(k, keep, near):
            kept[k] = add(keep[0], near[0]).astype(bf16)
            return add(keep[1], near[1]).astype(bf16)

        b, c, a = BACK
        moves, units = beside(0)
        got, (grad_q[b], b_keep, b_send) = clock.phase(moves, call(b), units)
        extra += got
        moves, units = beside(1)
        got, (grad_q[c], c_keep, c_send) = clock.phase([(b_send, *core)] + moves, call(c), units)
        extra += got[1:]
        b_sum = sums(b, b_keep, got[0])
        moves, units = beside(2)
        got, (grad_q[a], a_keep, a_send) = clock.phase([(b_sum, *y), (c_send, *core)] + moves, call(a), units)
        far[b] = got[0]
        extra += got[2:]
        c_sum = sums(c, c_keep, got[1])
        moves, units = beside(3)
        got, _ = clock.phase([(c_sum, *y), (a_send, *core)] + moves, None, units)
        far[c] = got[0]
        extra += got[2:]
        a_sum = sums(a, a_keep, got[1])
        moves, units = beside(4)
        got, _ = clock.phase([(a_sum, *y)] + moves, None, units)
        far[a] = got[0]
        extra += got[1:]
        return (grad_q, kept, far), extra

    def project_back_work(parts, stored, grad_after, result_type):
        return lambda turn: project_back(
            turn, *parts, cos, sin, stored[0], gain_a, grad_after, w_in, result_type
        )

    out_first, out_second = part(f, h2)
    parts, extra = back_phases(
        fed2[4 : 4 + PARTS], second, lambda k: ([(out_second, "fsdp", 3)] if k == 0 else [], ())
    )
    output = jnp.concatenate([out_first, extra[0]], axis=1).T
    _, (grads2, middle, middle_turned, gain_a2) = clock.phase((), project_back_work(parts, second, fed2[2], f32))

    def down_work(chip, name):
        return lambda turn: outer_down(turn, (middle_turned, cot_turned), (first[11], second[11]), chip, name)

    _, far_pair = clock.phase((), down_work(1, "outer_down_far"))
    (far_beside,), own_pair = clock.phase([(far_pair[1], *core)], down_work(0, "outer_down_own"))
    down = Unit(*own_pair, add(far_pair[0], far_beside).astype(bf16), None)
    _, fed1 = clock.phase((), feed_back_work(middle, first), (down,))

    def outer_work(i, name):
        return lambda turn: outer_tiles(turn, (first[8], second[8]), (fed1[i], fed2[i]), shard_rows, name)

    nothing = jnp.zeros((4, 16, LANES), bf16)
    _, gate_parts = clock.phase((), outer_work(0, "outer_gate"))
    gate = Unit(*gate_parts, 2)
    _, (up_parts, o_parts) = clock.phase(
        (),
        lambda turn: (
            outer_work(1, "outer_up")(turn),
            outer(turn, (first[7], second[7]), (fed1[3], fed2[3]), nothing, shard_rows, "outer_o"),
        ),
        (down, gate),
    )
    up, out = Unit(*up_parts, 2), Unit(*o_parts)
    plan = ((gate, up, down, out), (gate, down), (up, gate, down), (gate,), ())
    parts, _ = back_phases(fed1[4 : 4 + PARTS], first, lambda k: ([], plan[k]))
    _, (grads1, grad_tokens, _, gain_a1) = clock.phase(
        (), project_back_work(parts, first, fed1[2], bf16), (up, gate, down)
    )
    gains = jnp.concatenate([gain_a1 + gain_a2, fed1[4 + PARTS] + fed2[4 + PARTS]], axis=0)
    gains = gains.reshape(2, 4, width // 4).transpose(1, 0, 2).astype(bf16)
    gains = jnp.pad(gains, ((0, 0), (0, 14), (0, 256 - width // 4)))
    _, in_parts = clock.phase(
        (),
        lambda turn: outer(turn, (first[1], second[1]), (grads1, grads2), gains, shard_rows, "outer_in"),
        (out, up, gate),
    )
    into = Unit(*in_parts)
    clock.phase((), None, (into, up, out))
    _, (back_half, back_send) = clock.phase((), lambda turn: part(turn, grad_tokens), (into, up, gate, down, out))
    clock.phase((), None, (into, up, out))
    clock.phase((), None, (into, up, gate, out))
    (other_tokens,), _ = clock.phase([(back_send, "fsdp", 3)], None, (into, up, out))
    grad_tokens = jnp.concatenate([back_half, other_tokens], axis=1).T
    units = (into, up, out, gate, down)
    while any(unit.asks for unit in units):
        clock.phase((), None, [unit for unit in units if unit.asks])

    grad_down = down.total[0].T.astype(f32)
    wide = lambda unit: jnp.concatenate([unit.total[i] for i in range(4)], axis=1).astype(f32)
    grad_gate, grad_up = wide(gate), wide(up)
    grad_o = out.total[0, :shard_rows, :width].astype(f32)
    total = into.total[0]
    grad_key, grad_value, grad_query = unpack(total, shard_rows)
    gains = total[shard_rows : shard_rows + 2, : width // 4].astype(f32)
    return (
        output[None], grad_tokens[None], grad_query, grad_key, grad_value, grad_o, grad_gate, grad_up,
        grad_down, gains[0], gains[1],
    )


def solution(mesh):
    split, whole = P("fsdp", None), P("dp", "fsdp", None)
    return jax.shard_map(
        per_device,
        mesh=mesh,
        in_specs=(whole, P("dp", None)) + (split,) * 7 + (P(), P(), whole),
        out_specs=(whole, whole) + (split,) * 7 + (P("fsdp"), P("fsdp")),
        check_vma=False,
    )
```

```python
import functools
import jax
import jax.numpy as jnp
from jax import lax
from jax.experimental import pallas as pl
from jax.experimental.pallas import tpu as pltpu
from jax.sharding import PartitionSpec as P

HEADS = 15
KV_HEADS = 5
HEAD = 64
GROUP = HEADS // KV_HEADS
LANES = 128
NEGATIVE = -1e30
LOG2E = 1.4426950408889634
LN2 = 0.6931471805599453
MIB = 1 << 20
f32 = jnp.float32
bf16 = jnp.bfloat16


def nn(left, right):
    return lax.dot_general(left, right, (((1,), (0,)), ((), ())), preferred_element_type=f32)


def nt(left, right):
    return lax.dot_general(left, right, (((1,), (1,)), ((), ())), preferred_element_type=f32)


def lane_index(shape):
    return lax.broadcasted_iota(jnp.int32, shape, len(shape) - 1)


def swap_halves(tile):
    low = lane_index(tile.shape) % HEAD < HEAD // 2
    return jnp.where(low, pltpu.roll(tile, LANES - HEAD // 2, 1), pltpu.roll(tile, HEAD // 2, 1))


def three_terms(column, lane):
    high = column.astype(bf16).astype(f32)
    rest = column - high
    middle = rest.astype(bf16).astype(f32)
    low = rest - middle
    return jnp.where(lane == 8, high, jnp.where(lane == 9, middle, jnp.where(lane == 10, low, 0.0)))


def gather_keys(f, fresh, pieces, key_marks, kvf):
    block = kvf.shape[1]
    half = block // 2
    for m, piece in enumerate(pieces):
        device = f ^ m
        kvf[device, :half, :LANES] = piece[0, :half, :]
        kvf[3 - device, half:, :LANES] = piece[0, half:, :]

    @pl.when(fresh)
    def _():
        for j in range(kvf.shape[0]):
            kvf[j, :, LANES:] = key_marks[j * block : (j + 1) * block, :]


def causal(shape):
    row = lax.broadcasted_iota(jnp.int32, shape, 0)
    return lane_index(shape) <= row + (shape[1] - shape[0])


def score_parts(f):
    parts = [(0, f, 1, True), (1, 3 - f, 2, True)]
    for i in range(3):
        second = i >= f
        parts.append((second.astype(jnp.int32), jnp.where(second, i - f, i), 2, False))
    return parts


def attend_kernel(f_ref, q, q_marks, key_marks, own, near, far, last, attended, marks_out, kvf, qf, scores, best, top, acc):
    g = pl.program_id(0)
    f = f_ref[0]
    half = kvf.shape[1] // 2
    gather_keys(f, g == 0, (own, near, far, last), key_marks, kvf)
    parts = score_parts(f)

    @pl.when(g == 0)
    def _():
        for b in (0, 1):
            for i in range(GROUP):
                qf[b, i * half : (i + 1) * half, LANES:] = q_marks[b * half : (b + 1) * half, :]

    for b in (0, 1):
        for i in range(GROUP):
            qf[b, i * half : (i + 1) * half, :LANES] = q[i, b * half : (b + 1) * half, :]

    for n, (b, k, size, diagonal) in enumerate(parts):
        keys = kvf[k, : size * half, :]
        for i in range(GROUP):
            rows = slice(i * half, (i + 1) * half)
            s = nt(qf[b, rows, :], keys)
            if diagonal:
                s = jnp.where(causal(s.shape), s, NEGATIVE)
            scores[n, rows, : size * half] = s
            peak = s[:, :LANES]
            for t in range(1, size * half // LANES):
                peak = jnp.maximum(peak, s[:, t * LANES : (t + 1) * LANES])
            best[n, rows, :] = peak

    for b in (0, 1):
        for i in range(GROUP):
            rows = slice(i * half, (i + 1) * half)
            peak = best[b, rows, :]
            for n in (2, 3, 4):
                peak = jnp.maximum(peak, jnp.where(parts[n][0] == b, best[n, rows, :], NEGATIVE))
            top[b, rows, :] = jnp.broadcast_to(jnp.max(peak, axis=1, keepdims=True), peak.shape)

    for n, (b, k, size, _) in enumerate(parts):
        keys = kvf[k, : size * half, :]
        for i in range(GROUP):
            rows = slice(i * half, (i + 1) * half)
            high = jnp.concatenate([top[b, rows, :]] * (size * half // LANES), axis=1)
            p = jnp.exp2(scores[n, rows, : size * half] - high).astype(bf16)
            mixed = nn(p, keys)
            if n < 2:
                acc[b, rows, :] = mixed
            else:
                acc[b, rows, :] += mixed

    lane = lane_index((half, LANES))
    for b in (0, 1):
        outer = slice(b * half, (b + 1) * half)
        for i in range(GROUP):
            rows = slice(i * half, (i + 1) * half)
            total = acc[b, rows, LANES + 8 : LANES + 9]
            out = acc[b, rows, :LANES] * (1.0 / total)
            log_total = top[b, rows, :] + jnp.log2(total)
            new_marks = q_marks[outer, :].astype(f32) + three_terms(-log_total, lane)
            marks_out[i, outer, :] = new_marks.astype(bf16)
            h = GROUP * g + i
            pair = pl.multiple_of((h // 2) * LANES, LANES)
            odd = h % 2 == 1
            turned = pltpu.roll(out, HEAD, 1)
            old = attended[outer, pl.ds(pair, LANES)].astype(f32)
            new = jnp.where(odd, jnp.where(lane >= HEAD, out, old), jnp.where(lane < HEAD, turned, 0.0))
            attended[outer, pl.ds(pair, LANES)] = new.astype(bf16)


def pair_lanes(heads_here):
    return -(-GROUP * heads_here // 2) * LANES


def attend(f, q, q_marks, key_marks, pieces, group):
    first, heads_here = group
    tokens = q.shape[1]
    blocks = key_marks.shape[0] // tokens
    rows = GROUP * tokens // 2
    piece = pl.BlockSpec((1, tokens, LANES), lambda g, f: (g, 0, 0))
    width = pair_lanes(heads_here)
    return pl.pallas_call(
        attend_kernel,
        grid_spec=pltpu.PrefetchScalarGridSpec(
            num_scalar_prefetch=1,
            grid=(heads_here,),
            in_specs=[
                pl.BlockSpec((GROUP, tokens, LANES), lambda g, f: (first + g, 0, 0)),
                pl.BlockSpec((tokens, LANES), lambda g, f: (0, 0)),
                pl.BlockSpec(key_marks.shape, lambda g, f: (0, 0)),
                piece,
                piece,
                piece,
                piece,
            ],
            out_specs=[
                pl.BlockSpec((tokens, width), lambda g, f: (0, 0)),
                pl.BlockSpec((GROUP, tokens, LANES), lambda g, f: (g, 0, 0)),
            ],
            scratch_shapes=[
                pltpu.VMEM((blocks, tokens, 2 * LANES), bf16),
                pltpu.VMEM((2, rows, 2 * LANES), bf16),
                pltpu.VMEM((5, rows, tokens), f32),
                pltpu.VMEM((5, rows, LANES), f32),
                pltpu.VMEM((2, rows, LANES), f32),
                pltpu.VMEM((2, rows, 2 * LANES), f32),
            ],
        ),
        out_shape=[
            jax.ShapeDtypeStruct((tokens, width), bf16),
            jax.ShapeDtypeStruct((GROUP * heads_here, tokens, LANES), bf16),
        ],
        compiler_params=params(20),
        cost_estimate=cost(4e10, 1e6),
        name="attend",
    )(f, q, q_marks, key_marks, *pieces)


def attend_back_kernel(
    f_ref, q, marks, key_marks, own, near, far, last, grad, attended, cos_ref, sin_ref,
    grad_q, keep, send, kvf, kv_sum, qf, df, turned, acc, ds_all, p_all,
):
    g = pl.program_id(0)
    f = f_ref[0]
    half = kvf.shape[1] // 2
    gather_keys(f, g == 0, (own, near, far, last), key_marks, kvf)
    kv_sum[...] = jnp.zeros(kv_sum.shape, f32)
    lane = lane_index((half, LANES))
    for b in (0, 1):
        outer = slice(b * half, (b + 1) * half)
        for i in range(GROUP):
            rows = slice(i * half, (i + 1) * half)
            qf[b, rows, :LANES] = q[i, outer, :]
            qf[b, rows, LANES:] = marks[i, outer, :]
            h = GROUP * g + i
            pair = pl.multiple_of((h // 2) * LANES, LANES)
            odd = h % 2 == 1
            d_tile = grad[outer, pl.ds(pair, LANES)].astype(f32)
            o_tile = attended[outer, pl.ds(pair, LANES)].astype(f32)
            mine = (lane >= HEAD) == odd
            inner = jnp.sum(jnp.where(mine, d_tile * o_tile, 0.0), axis=1, keepdims=True)
            moved = jnp.where(odd, d_tile, pltpu.roll(d_tile, HEAD, 1))
            moved = jnp.where(lane >= HEAD, moved, 0.0)
            df[b, rows, :LANES] = moved.astype(bf16)
            df[b, rows, LANES:] = three_terms(-inner, lane).astype(bf16)
            joined = moved + q[i, outer, :].astype(f32)
            turned[b, :, rows] = joined.T.astype(bf16)

    for n, (b, k, size, diagonal) in enumerate(score_parts(f)):
        wide = size * half
        keys = kvf[k, :wide, :]
        for i in range(GROUP):
            rows = slice(i * half, (i + 1) * half)
            p = jnp.exp2(nt(qf[b, rows, :], keys))
            if diagonal:
                p = jnp.where(causal(p.shape), p, 0.0)
            ds_all[rows, :wide] = (p * nt(df[b, rows, :], keys)).astype(bf16)
            p_all[rows, :wide] = p.astype(bf16)
        part = nn(ds_all[:, :wide], keys[:, :LANES])
        if n < 2:
            acc[b] = part
        else:
            acc[b] += part
        kv_sum[k, :HEAD, :wide] += nn(turned[b, :HEAD, :], ds_all[:, :wide])
        kv_sum[k, HEAD:, :wide] += nn(turned[b, HEAD:, :], p_all[:, :wide])

    scale = HEAD ** (-0.5)
    for b in (0, 1):
        outer = slice(b * half, (b + 1) * half)
        for i in range(GROUP):
            rows = slice(i * half, (i + 1) * half)
            h = GROUP * g + i
            pair = pl.multiple_of((h // 2) * LANES, LANES)
            odd = h % 2 == 1
            tile = acc[b, rows, :] * scale
            tile = tile * cos_ref[outer, :] - swap_halves(tile) * sin_ref[outer, :]
            other = pltpu.roll(tile, HEAD, 1)
            old = grad_q[outer, pl.ds(pair, LANES)].astype(f32)
            new = jnp.where(odd, jnp.where(lane >= HEAD, other, old), jnp.where(lane < HEAD, tile, 0.0))
            grad_q[outer, pl.ds(pair, LANES)] = new.astype(bf16)

    factor = jnp.where(lane < HEAD, LN2, 1.0)
    for m in range(4):
        device = f ^ m
        ref = send if m % 2 else keep
        ref[m // 2, 0, :half, :] = (kv_sum[device, :, :half].T * factor).astype(bf16)
        ref[m // 2, 0, half:, :] = (kv_sum[3 - device, :, half:].T * factor).astype(bf16)


def attend_back(f, q, marks, key_marks, pieces, grad, attended, cos, sin, group):
    first, heads_here = group
    tokens = q.shape[1]
    blocks = key_marks.shape[0] // tokens
    rows = GROUP * tokens // 2
    piece = pl.BlockSpec((1, tokens, LANES), lambda g, f: (g, 0, 0))
    width = pair_lanes(heads_here)
    whole = pl.BlockSpec((tokens, width), lambda g, f: (0, 0))
    table = pl.BlockSpec((tokens, LANES), lambda g, f: (0, 0))
    pair = pl.BlockSpec((2, 1, tokens, LANES), lambda g, f: (0, g, 0, 0))
    return pl.pallas_call(
        attend_back_kernel,
        grid_spec=pltpu.PrefetchScalarGridSpec(
            num_scalar_prefetch=1,
            grid=(heads_here,),
            in_specs=[
                pl.BlockSpec((GROUP, tokens, LANES), lambda g, f: (first + g, 0, 0)),
                pl.BlockSpec((GROUP, tokens, LANES), lambda g, f: (g, 0, 0)),
                pl.BlockSpec(key_marks.shape, lambda g, f: (0, 0)),
                piece,
                piece,
                piece,
                piece,
                whole,
                whole,
                table,
                table,
            ],
            out_specs=[whole, pair, pair],
            scratch_shapes=[
                pltpu.VMEM((blocks, tokens, 2 * LANES), bf16),
                pltpu.VMEM((blocks, LANES, tokens), f32),
                pltpu.VMEM((2, rows, 2 * LANES), bf16),
                pltpu.VMEM((2, rows, 2 * LANES), bf16),
                pltpu.VMEM((2, LANES, rows), bf16),
                pltpu.VMEM((2, rows, LANES), f32),
                pltpu.VMEM((rows, tokens), bf16),
                pltpu.VMEM((rows, tokens), bf16),
            ],
        ),
        out_shape=[
            jax.ShapeDtypeStruct((tokens, width), bf16),
            jax.ShapeDtypeStruct((2, heads_here, tokens, LANES), bf16),
            jax.ShapeDtypeStruct((2, heads_here, tokens, LANES), bf16),
        ],
        compiler_params=params(20),
        cost_estimate=cost(4e10, 1e6),
        name="attend_back",
    )(f, q, marks, key_marks, *pieces, grad, attended, cos, sin)


EPS = 1e-05
ANY = pl.BlockSpec(memory_space=pl.ANY)


def params(mib):
    return pltpu.CompilerParams(vmem_limit_bytes=mib * MIB)


def cost(flops, moved):
    return pl.CostEstimate(flops=int(flops), bytes_accessed=int(moved), transcendentals=0)


def row_copies(f, pieces, target, sems):
    rows = pieces[0].shape[0]
    return [
        pltpu.make_async_copy(
            piece, target.at[pl.ds(pl.multiple_of((f ^ m) * rows, 16), rows), :], sems.at[m]
        )
        for m, piece in enumerate(pieces)
    ]


def side_copies(info, bit, pieces, target, sems):
    f = info[0]
    rows = pieces[0].shape[0]
    copies = []
    for k, (m, which) in enumerate(((0, None), (1, None), (2, 0), (2, 1), (3, 0), (3, 1))):
        at = pl.ds(pl.multiple_of((f ^ m) * rows, 16), rows)
        if which is None:
            place = target.at[at, :]
        else:
            width = pieces[k].shape[1]
            place = target.at[at, pl.ds(pl.multiple_of((info[bit] ^ which) * width, width), width)]
        copies.append(pltpu.make_async_copy(pieces[k], place, sems.at[k]))
    return copies


def down_copies(info, bit, pieces, target, sems):
    f = info[0]
    width = pieces[0].shape[1]
    copies = []
    for k, (m, which) in enumerate(((0, None), (1, None), (2, 0), (2, 1), (3, 0), (3, 1))):
        at = pl.ds(pl.multiple_of((f ^ m) * width, width), width)
        if which is None:
            place = target.at[:, at]
        else:
            rows = pieces[k].shape[0]
            place = target.at[pl.ds(pl.multiple_of((info[bit] ^ which) * rows, 16), rows), at]
        copies.append(pltpu.make_async_copy(pieces[k], place, sems.at[k]))
    return copies


def start(copies):
    for copy in copies:
        copy.start()


def wait(copies):
    for copy in copies:
        copy.wait()


def inverse_of(values):
    return lax.rsqrt(jnp.mean(values * values, axis=-1, keepdims=True) + EPS)


def norm_back(upstream, values, gain):
    inverse = inverse_of(values)
    scaled = upstream * gain
    gain_grad = jnp.sum(upstream * (values * inverse), axis=0, keepdims=True)
    middle = jnp.mean(scaled * values, axis=-1, keepdims=True)
    return inverse * scaled - (inverse * inverse * inverse * middle) * values, gain_grad


def join_kernel(first, second, out, turned):
    half = out.shape[0] // 2
    turned[:, :half] = first[...]
    turned[:, half:] = second[...]
    out[:half, :] = first[...].T
    out[half:, :] = second[...].T


def join(turned, came):
    width, half = came.shape
    spec = pl.BlockSpec((width, half), lambda i: (0, 0))
    return pl.pallas_call(
        join_kernel,
        grid=(1,),
        in_specs=[spec, spec],
        out_specs=[
            pl.BlockSpec((2 * half, width), lambda i: (0, 0)),
            pl.BlockSpec((width, 2 * half), lambda i: (0, 0)),
        ],
        out_shape=[
            jax.ShapeDtypeStruct((2 * half, width), bf16),
            jax.ShapeDtypeStruct((width, 2 * half), bf16),
        ],
        compiler_params=params(16),
        cost_estimate=cost(4e10, 1e6),
        name="join",
    )(turned, came)


def part_kernel(f_ref, rows, first, second):
    half = rows.shape[0] // 2
    first[...] = rows[:half, :].T
    second[...] = rows[half:, :].T


def part(f, rows):
    tokens, width = rows.shape
    half = tokens // 2
    spec = pl.BlockSpec((width, half), lambda i, f: (0, 0))
    return pl.pallas_call(
        part_kernel,
        grid_spec=pltpu.PrefetchScalarGridSpec(
            num_scalar_prefetch=1,
            grid=(1,),
            in_specs=[pl.BlockSpec((tokens, width), lambda i, f: (0, 0))],
            out_specs=[spec, spec],
        ),
        out_shape=[jax.ShapeDtypeStruct((width, half), bf16)] * 2,
        compiler_params=params(16),
        cost_estimate=cost(4e9, 1e6),
        name="part",
    )(f, rows)


def pack_kernel(key_t, value_t, query, out):
    rows = []
    for g in range(KV_HEADS):
        rows += [key_t[g * HEAD : (g + 1) * HEAD, :], value_t[g * HEAD : (g + 1) * HEAD, :]]
    width = 2 * KV_HEADS * HEAD
    out[:, :width] = jnp.concatenate(rows, axis=0).T
    out[:, width : width + HEADS * HEAD] = query[...]
    out[:, width + HEADS * HEAD :] = jnp.zeros((out.shape[0], HEAD), bf16)


def pack(key, value, query):
    rows = key.shape[0]
    width = (2 * KV_HEADS + HEADS + 1) * HEAD
    full = lambda *shape: pl.BlockSpec(shape, lambda i: (0, 0))
    return pl.pallas_call(
        pack_kernel,
        grid=(1,),
        in_specs=[full(KV_HEADS * HEAD, rows)] * 2 + [full(*query.shape)],
        out_specs=full(rows, width),
        out_shape=jax.ShapeDtypeStruct((rows, width), bf16),
        compiler_params=params(16),
        cost_estimate=cost(4e10, 1e6),
        name="pack",
    )(key.T, value.T, query)


GROUPS = ((4, 1), (0, 2), (2, 2))
ORDER = (1, 2, 0)


def project_kernel(f_ref, h, gain, cos_ref, sin_ref, own, near, far, last, normed_t, q_out, *refs):
    kv_out, (w, sems) = refs[: len(GROUPS)], refs[len(GROUPS) :]
    copies = row_copies(f_ref[0], (own, near, far, last), w, sems)
    start(copies)
    hidden = h[...].astype(f32)
    normed = (hidden * inverse_of(hidden) * gain[...]).astype(bf16)
    normed_t[...] = normed.T
    cos, sin = cos_ref[...], sin_ref[...]
    lane = lane_index(cos.shape)
    kv_cos, kv_sin = jnp.where(lane < HEAD, cos, 1.0), jnp.where(lane < HEAD, sin, 0.0)
    wait(copies)
    first = KV_HEADS * LANES
    both = nn(normed, w[:, :first])
    for (start_head, heads_here), out in zip(GROUPS, kv_out):
        for i in range(heads_here):
            g = start_head + i
            tile = both[:, g * LANES : (g + 1) * LANES]
            out[i] = (tile * kv_cos + swap_halves(tile) * kv_sin).astype(bf16)
    query = nn(normed, w[:, first:])
    for p in range((HEADS + 1) // 2):
        tile = query[:, p * LANES : (p + 1) * LANES]
        tile = (tile * cos + swap_halves(tile) * sin) * (HEAD ** (-0.5) * LOG2E)
        q_out[2 * p] = jnp.where(lane < HEAD, tile, 0.0).astype(bf16)
        if 2 * p + 1 < HEADS:
            q_out[2 * p + 1] = jnp.where(lane < HEAD, pltpu.roll(tile, HEAD, 1), 0.0).astype(bf16)


def project(f, hidden, gain, cos, sin, pieces):
    tokens, width = hidden.shape
    rows, columns = pieces[0].shape
    full = lambda *shape: pl.BlockSpec(shape, lambda i, f: (0,) * len(shape))
    like = jax.ShapeDtypeStruct
    return pl.pallas_call(
        project_kernel,
        grid_spec=pltpu.PrefetchScalarGridSpec(
            num_scalar_prefetch=1,
            grid=(1,),
            in_specs=[full(tokens, width), full(1, width), full(*cos.shape), full(*sin.shape)] + [ANY] * 4,
            out_specs=[full(width, tokens), full(HEADS, tokens, LANES)]
            + [full(heads_here, tokens, LANES) for _, heads_here in GROUPS],
            scratch_shapes=[pltpu.VMEM((4 * rows, columns), bf16), pltpu.SemaphoreType.DMA((4,))],
        ),
        out_shape=[like((width, tokens), bf16), like((HEADS, tokens, LANES), bf16)]
        + [like((heads_here, tokens, LANES), bf16) for _, heads_here in GROUPS],
        compiler_params=params(20),
        cost_estimate=cost(4e10, 1e6),
        name="project",
    )(f, hidden, gain, cos, sin, *pieces)


PARTS = len(GROUPS)


def split_pieces(refs):
    return refs[:4], refs[4:10], refs[10:16], refs[16:22], refs[22:]


CHUNK = 256


def feed_kernel(f_ref, h, *refs):
    attended, gain = refs[:PARTS], refs[PARTS]
    o, gate, up, down, refs = split_pieces(refs[PARTS + 1 :])
    outs, result = refs[:6], refs[6]
    w_o, w_gate, w_up, w_down, n16, *refs = refs[7:]
    after, attended_t, normed_t, gate_out, up_out, hidden_out = refs[:6]
    o_sem, gate_sem, up_sem, down_sem, out_sem = refs[6:]
    depth, wide = 4 * o[0].shape[0], w_gate.shape[1]
    o_copies = row_copies(f_ref[0], o, w_o, o_sem)
    gate_copies = side_copies(f_ref, 1, gate, w_gate, gate_sem)
    up_copies = side_copies(f_ref, 2, up, w_up, up_sem)
    d_copies = down_copies(f_ref, 1, down, w_down, down_sem)
    half = wide // 2

    def leave(k, part=None):
        if part is None:
            return pltpu.make_async_copy(refs[k], outs[k], out_sem.at[k, 0])
        columns = slice(part * half, (part + 1) * half)
        return pltpu.make_async_copy(refs[k].at[:, columns], outs[k].at[:, columns], out_sem.at[k, part])

    leaving = [leave(k) for k in range(3)] + [leave(k, part) for part in (0, 1) for k in (3, 4, 5)]
    for copies in (o_copies, gate_copies, up_copies, d_copies):
        start(copies)
    att = jnp.concatenate([attended[i][...] for i in ORDER], axis=1)
    attended_t[...] = att.T
    w_o[depth:, :] = jnp.zeros((w_o.shape[0] - depth, w_o.shape[1]), bf16)
    wait(o_copies)
    value = h[...].astype(f32) + nn(att, w_o[...])
    after[...] = value
    normed = (value * inverse_of(value) * gain[...]).astype(bf16)
    n16[...] = normed
    normed_t[...] = normed.T
    wait(gate_copies)
    wait(up_copies)
    for at in range(0, wide, CHUNK):
        columns = slice(at, at + CHUNK)
        gate_act = nn(n16[...], w_gate[:, columns])
        up_act = nn(n16[...], w_up[:, columns])
        hidden = gate_act * jax.nn.sigmoid(gate_act) * up_act
        gate_out[:, columns] = gate_act.astype(bf16)
        up_out[:, columns] = up_act.astype(bf16)
        hidden_out[:, columns] = hidden.astype(bf16)
        if at + CHUNK == half:
            start(leaving[:6])
    start(leaving[6:])
    wait(d_copies)
    result[...] = (after[...] + nt(hidden_out[...], w_down[...])).astype(result.dtype)
    wait(leaving)


def weight_scratch(o, gate):
    rows, width = o.shape
    columns = gate.shape[1]
    return [
        pltpu.VMEM((4 * rows + HEAD, width), bf16),
        pltpu.VMEM((4 * rows, columns), bf16),
        pltpu.VMEM((4 * rows, columns), bf16),
        pltpu.VMEM((width, columns), bf16),
    ]


def weight_sems():
    dma = pltpu.SemaphoreType.DMA
    return [dma((4,)), dma((6,)), dma((6,)), dma((6,))]


def feed(f, hidden, attended, gain, o, gate, up, down, result_type):
    tokens, width = hidden.shape
    wide = gate[0].shape[1]
    lanes = (HEADS + 1) * HEAD
    full = lambda *shape: pl.BlockSpec(shape, lambda i, f: (0,) * len(shape))
    like = jax.ShapeDtypeStruct
    kept = [((tokens, width), f32), ((lanes, tokens), bf16), ((width, tokens), bf16)] + [((tokens, wide), bf16)] * 3
    return pl.pallas_call(
        feed_kernel,
        grid_spec=pltpu.PrefetchScalarGridSpec(
            num_scalar_prefetch=1,
            grid=(1,),
            in_specs=[full(tokens, width)] + [full(*a.shape) for a in attended] + [full(1, width)] + [ANY] * 22,
            out_specs=[ANY] * 6 + [full(tokens, width)],
            scratch_shapes=weight_scratch(o[0], gate[0])
            + [pltpu.VMEM((tokens, width), bf16)]
            + [pltpu.VMEM(*k) for k in kept]
            + weight_sems()
            + [pltpu.SemaphoreType.DMA((6, 2))],
        ),
        out_shape=[like(*k) for k in kept] + [like((tokens, width), result_type)],
        compiler_params=params(42),
        cost_estimate=cost(4e10, 1e6),
        name="feed",
    )(f, hidden, *attended, gain, *o, *gate, *up, *down)


def feed_back_kernel(f_ref, g, gain, *refs):
    held = refs[:3]
    o, gate, up, down, refs = split_pieces(refs[3:])
    outs, grad_after, branch_out = refs[:2], refs[2], refs[3]
    grad_attended, gain_grad = refs[4 : 4 + PARTS], refs[4 + PARTS]
    w_o, w_gate, w_up, w_down, g16, *refs = refs[5 + PARTS :]
    after, gate_act, up_act, grad_gate, grad_up, o_sem, gate_sem, up_sem, down_sem, in_sem, out_sem = refs
    depth, wide = 4 * o[0].shape[0], w_gate.shape[1]
    half = wide // 2
    o_copies = row_copies(f_ref[0], o, w_o, o_sem)
    gate_copies = side_copies(f_ref, 1, gate, w_gate, gate_sem)
    up_copies = side_copies(f_ref, 2, up, w_up, up_sem)
    d_copies = down_copies(f_ref, 1, down, w_down, down_sem)

    def act_copies(part):
        columns = slice(part * half, (part + 1) * half)
        return [
            pltpu.make_async_copy(held[k].at[:, columns], refs[k].at[:, columns], in_sem.at[k, part]) for k in (1, 2)
        ]

    after_copy = pltpu.make_async_copy(held[0], after, in_sem.at[0, 0])
    leave = [pltpu.make_async_copy(refs[3 + k], outs[k], out_sem.at[k]) for k in (0, 1)]
    first, second = act_copies(0), act_copies(1)
    for copies in (d_copies, first, second, gate_copies, up_copies, [after_copy], o_copies):
        start(copies)
    g16[...] = g[...].astype(bf16)
    w_o[depth:, :] = jnp.zeros((w_o.shape[0] - depth, w_o.shape[1]), bf16)
    wait(d_copies)
    for part, copies in enumerate((first, second)):
        wait(copies)
        for at in range(part * half, (part + 1) * half, CHUNK):
            columns = slice(at, at + CHUNK)
            grad_hidden = nn(g16[...], w_down[:, columns])
            value = gate_act[:, columns].astype(f32)
            logistic = jax.nn.sigmoid(value)
            steep = logistic * (1.0 + value * (1.0 - logistic))
            grad_gate[:, columns] = (grad_hidden * up_act[:, columns].astype(f32) * steep).astype(bf16)
            grad_up[:, columns] = (grad_hidden * (value * logistic)).astype(bf16)
    wait(gate_copies)
    wait(up_copies)
    start(leave)
    grad_normed = nt(grad_gate[...], w_gate[...]) + nt(grad_up[...], w_up[...])
    wait([after_copy])
    wait(o_copies)
    back, gain_part = norm_back(grad_normed, after[...], gain[...])
    back = back + g[...].astype(f32)
    gain_grad[...] = gain_part
    grad_after[...] = back
    branch = back.astype(bf16)
    branch_out[...] = branch
    whole = nt(branch, w_o[...]).astype(bf16)
    at = 0
    for i in ORDER:
        lanes = grad_attended[i].shape[1]
        grad_attended[i][...] = whole[:, at : at + lanes]
        at += lanes
    wait(leave)


def feed_back(f, g, after, gain, gate_act, up_act, o, gate, up, down):
    tokens, width = after.shape
    wide = gate[0].shape[1]
    full = lambda *shape: pl.BlockSpec(shape, lambda i, f: (0,) * len(shape))
    like = jax.ShapeDtypeStruct
    lanes = [pair_lanes(heads_here) for _, heads_here in GROUPS]
    dma = pltpu.SemaphoreType.DMA
    return pl.pallas_call(
        feed_back_kernel,
        grid_spec=pltpu.PrefetchScalarGridSpec(
            num_scalar_prefetch=1,
            grid=(1,),
            in_specs=[full(tokens, width), full(1, width)] + [ANY] * 25,
            out_specs=[ANY, ANY, full(tokens, width), full(tokens, width)]
            + [full(tokens, n) for n in lanes]
            + [full(1, width)],
            scratch_shapes=weight_scratch(o[0], gate[0])
            + [pltpu.VMEM((tokens, width), bf16), pltpu.VMEM((tokens, width), f32)]
            + [pltpu.VMEM((tokens, wide), bf16)] * 4
            + weight_sems()
            + [dma((3, 2)), dma((2,))],
        ),
        out_shape=[like((tokens, wide), bf16)] * 2
        + [like((tokens, width), f32), like((tokens, width), bf16)]
        + [like((tokens, n), bf16) for n in lanes]
        + [like((1, width), f32)],
        compiler_params=params(46),
        cost_estimate=cost(4e10, 1e6),
        name="feed_back",
    )(f, g, gain, after, gate_act, up_act, *o, *gate, *up, *down)


def feed_turn_kernel(f_ref, h, g, *refs):
    attended, gain = refs[:PARTS], refs[PARTS]
    o, gate, up, down, refs = split_pieces(refs[PARTS + 1 :])
    outs, result, grad_after, branch_out = refs[:5], refs[5], refs[6], refs[7]
    grad_attended, gain_grad = refs[8 : 8 + PARTS], refs[8 + PARTS]
    w_o, w_gate, w_up, w_down, n16, after, gate_out, up_out, *refs = refs[9 + PARTS :]
    attended_t, normed_t, hidden_out, grad_gate, grad_up = refs[:5]
    o_sem, gate_sem, up_sem, down_sem, out_sem = refs[5:]
    depth, wide = 4 * o[0].shape[0], w_gate.shape[1]
    o_copies = row_copies(f_ref[0], o, w_o, o_sem)
    gate_copies = side_copies(f_ref, 1, gate, w_gate, gate_sem)
    up_copies = side_copies(f_ref, 2, up, w_up, up_sem)
    d_copies = down_copies(f_ref, 1, down, w_down, down_sem)
    leaving = [pltpu.make_async_copy(refs[k], outs[k], out_sem.at[k]) for k in range(5)]
    for copies in (o_copies, gate_copies, up_copies, d_copies):
        start(copies)
    att = jnp.concatenate([attended[i][...] for i in ORDER], axis=1)
    attended_t[...] = att.T
    w_o[depth:, :] = jnp.zeros((w_o.shape[0] - depth, w_o.shape[1]), bf16)
    wait(o_copies)
    value = h[...].astype(f32) + nn(att, w_o[...])
    after[...] = value
    normed = (value * inverse_of(value) * gain[...]).astype(bf16)
    n16[...] = normed
    normed_t[...] = normed.T
    wait(gate_copies)
    wait(up_copies)
    for at in range(0, wide, CHUNK):
        columns = slice(at, at + CHUNK)
        gate_act = nn(n16[...], w_gate[:, columns])
        up_act = nn(n16[...], w_up[:, columns])
        gate_out[:, columns] = gate_act.astype(bf16)
        up_out[:, columns] = up_act.astype(bf16)
        hidden_out[:, columns] = (gate_act * jax.nn.sigmoid(gate_act) * up_act).astype(bf16)
    start(leaving[:3])
    wait(d_copies)
    result[...] = (after[...] + nt(hidden_out[...], w_down[...])).astype(result.dtype)
    for at in range(0, wide, CHUNK):
        columns = slice(at, at + CHUNK)
        grad_hidden = nn(g[...], w_down[:, columns])
        value = gate_out[:, columns].astype(f32)
        logistic = jax.nn.sigmoid(value)
        steep = logistic * (1.0 + value * (1.0 - logistic))
        grad_gate[:, columns] = (grad_hidden * up_out[:, columns].astype(f32) * steep).astype(bf16)
        grad_up[:, columns] = (grad_hidden * (value * logistic)).astype(bf16)
    start(leaving[3:])
    grad_normed = nt(grad_gate[...], w_gate[...]) + nt(grad_up[...], w_up[...])
    back, gain_part = norm_back(grad_normed, after[...], gain[...])
    back = back + g[...].astype(f32)
    gain_grad[...] = gain_part
    grad_after[...] = back
    branch = back.astype(bf16)
    branch_out[...] = branch
    whole = nt(branch, w_o[...]).astype(bf16)
    at = 0
    for i in ORDER:
        lanes = grad_attended[i].shape[1]
        grad_attended[i][...] = whole[:, at : at + lanes]
        at += lanes
    wait(leaving)


def feed_turn(f, hidden, g, attended, gain, o, gate, up, down):
    tokens, width = hidden.shape
    wide = gate[0].shape[1]
    full = lambda *shape: pl.BlockSpec(shape, lambda i, f: (0,) * len(shape))
    like = jax.ShapeDtypeStruct
    lanes = [pair_lanes(heads_here) for _, heads_here in GROUPS]
    kept = [(((HEADS + 1) * HEAD, tokens), bf16), ((width, tokens), bf16)] + [((tokens, wide), bf16)] * 3
    return pl.pallas_call(
        feed_turn_kernel,
        grid_spec=pltpu.PrefetchScalarGridSpec(
            num_scalar_prefetch=1,
            grid=(1,),
            in_specs=[full(tokens, width)] * 2 + [full(*a.shape) for a in attended] + [full(1, width)] + [ANY] * 22,
            out_specs=[ANY] * 5
            + [full(tokens, width)] * 3
            + [full(tokens, n) for n in lanes]
            + [full(1, width)],
            scratch_shapes=weight_scratch(o[0], gate[0])
            + [pltpu.VMEM((tokens, width), bf16), pltpu.VMEM((tokens, width), f32)]
            + [pltpu.VMEM((tokens, wide), bf16)] * 2
            + [pltpu.VMEM(*k) for k in kept]
            + weight_sems()
            + [pltpu.SemaphoreType.DMA((5,))],
        ),
        out_shape=[like(*k) for k in kept]
        + [like((tokens, width), bf16), like((tokens, width), f32), like((tokens, width), bf16)]
        + [like((tokens, n), bf16) for n in lanes]
        + [like((1, width), f32)],
        compiler_params=params(54),
        cost_estimate=cost(4e10, 1e6),
        name="feed_turn",
    )(f, hidden, g, *attended, gain, *o, *gate, *up, *down)


def project_back_kernel(f_ref, *refs):
    grad_q, kept, came = refs[:PARTS], refs[PARTS : 2 * PARTS], refs[2 * PARTS : 3 * PARTS]
    cos_ref, sin_ref, h, gain, grad_after, own, near, far, last = refs[3 * PARTS : 3 * PARTS + 9]
    grads, grad_in, turned, gain_grad, w, sems = refs[3 * PARTS + 9 :]
    copies = row_copies(f_ref[0], (own, near, far, last), w, sems)
    start(copies)
    cos, sin = cos_ref[...], sin_ref[...]
    lane = lane_index(cos.shape)
    cos, sin = jnp.where(lane < HEAD, cos, 1.0), jnp.where(lane < HEAD, sin, 0.0)
    at = KV_HEADS * LANES
    for k in ORDER:
        first, heads_here = GROUPS[k]
        for i in range(heads_here):
            g = first + i
            tile = kept[k][i].astype(f32) + came[k][i].astype(f32)
            tile = tile * cos - swap_halves(tile) * sin
            grads[:, g * LANES : (g + 1) * LANES] = tile.astype(bf16)
        lanes = grad_q[k].shape[1]
        grads[:, at : at + lanes] = grad_q[k][...]
        at += lanes
    wait(copies)
    grad_normed = nt(grads[...], w[...])
    back, gain_part = norm_back(grad_normed, h[...].astype(f32), gain[...])
    gain_grad[...] = gain_part
    back = back + grad_after[...]
    grad_in[...] = back.astype(grad_in.dtype)
    turned[...] = back.astype(bf16).T


def project_back(f, grad_q, kept, came, cos, sin, hidden, gain, grad_after, pieces, result_type):
    tokens, width = hidden.shape
    rows, columns = pieces[0].shape
    full = lambda *shape: pl.BlockSpec(shape, lambda i, f: (0,) * len(shape))
    like = jax.ShapeDtypeStruct
    arrays = (*grad_q, *kept, *came, cos, sin, hidden, gain, grad_after)
    return pl.pallas_call(
        project_back_kernel,
        grid_spec=pltpu.PrefetchScalarGridSpec(
            num_scalar_prefetch=1,
            grid=(1,),
            in_specs=[full(*a.shape) for a in arrays] + [ANY] * 4,
            out_specs=[full(tokens, columns), full(tokens, width), full(width, tokens), full(1, width)],
            scratch_shapes=[pltpu.VMEM((4 * rows, columns), bf16), pltpu.SemaphoreType.DMA((4,))],
        ),
        out_shape=[
            like((tokens, columns), bf16),
            like((tokens, width), result_type),
            like((width, tokens), bf16),
            like((1, width), f32),
        ],
        compiler_params=params(20),
        cost_estimate=cost(4e10, 1e6),
        name="project_back",
    )(f, *arrays, *pieces)


def joined(left_first, left_second, right_first, right_second):
    left = jnp.concatenate([left_first, left_second], axis=1)
    return nn(left, jnp.concatenate([right_first, right_second], axis=0))


def outer_tiles_kernel(f_ref, left_first, left_second, right_first, right_second, *refs, rows):
    outs, acc = refs[:4], refs[4]
    acc[...] = joined(left_first[...], left_second[...], right_first[...], right_second[...])
    half = acc.shape[1] // 2
    for m in range(4):
        from_row = pl.multiple_of((f_ref[0] ^ m) * rows, 16)
        for c in (0, 1):
            outs[m][c] = acc[pl.ds(from_row, rows), c * half : (c + 1) * half].astype(bf16)


def outer_tiles(f, lefts, rights, rows, name):
    width, tokens = lefts[0].shape
    wide = rights[0].shape[1] // 2
    left = pl.BlockSpec((width, tokens), lambda i, f: (0, 0))
    right = pl.BlockSpec((tokens, wide), lambda i, f: (0, i))
    out = pl.BlockSpec((2, rows, wide // 2), lambda i, f: (i, 0, 0))
    return pl.pallas_call(
        functools.partial(outer_tiles_kernel, rows=rows),
        grid_spec=pltpu.PrefetchScalarGridSpec(
            num_scalar_prefetch=1,
            grid=(2,),
            in_specs=[left, left, right, right],
            out_specs=[out] * 4,
            scratch_shapes=[pltpu.VMEM((width, wide), f32)],
        ),
        out_shape=[jax.ShapeDtypeStruct((4, rows, wide // 2), bf16)] * 4,
        compiler_params=params(28),
        cost_estimate=cost(4e10, 1e6),
        name=name,
    )(f, *lefts, *rights)


def outer_down_kernel(f_ref, left_first, left_second, right_first, right_second, own, near):
    value = joined(left_first[...], left_second[...], right_first[...], right_second[...])
    half = value.shape[1] // 2
    first = (f_ref[0] & 1) == 0
    lower, upper = value[:, :half], value[:, half:]
    own[0] = jnp.where(first, lower, upper).astype(bf16)
    near[0] = jnp.where(first, upper, lower).astype(bf16)


def outer_down(f, lefts, rights, chip, name):
    width, tokens = lefts[0].shape
    wide = rights[0].shape[1] // 2
    left = pl.BlockSpec((width, tokens), lambda i, f: (0, 0))
    right = pl.BlockSpec((tokens, wide), lambda i, f: (0, (f[0] >> 1) ^ chip))
    out = pl.BlockSpec((1, width, wide // 2), lambda i, f: (0, 0, 0))
    return pl.pallas_call(
        outer_down_kernel,
        grid_spec=pltpu.PrefetchScalarGridSpec(
            num_scalar_prefetch=1,
            grid=(1,),
            in_specs=[left, left, right, right],
            out_specs=[out, out],
        ),
        out_shape=[jax.ShapeDtypeStruct((1, width, wide // 2), bf16)] * 2,
        compiler_params=params(28),
        cost_estimate=cost(4e10, 1e6),
        name=name,
    )(f, *lefts, *rights)


def outer_kernel(f_ref, left_first, left_second, right_first, right_second, extra, *refs, rows):
    outs, acc = refs[:4], refs[4]
    acc[...] = joined(left_first[...], left_second[...], right_first[...], right_second[...])
    columns = acc.shape[1]
    for m in range(4):
        device = f_ref[0] ^ m
        out = outs[m]
        if columns < out.shape[2]:
            out[0, :, columns:] = jnp.zeros((out.shape[1], out.shape[2] - columns), bf16)
        out[0, :rows, :columns] = acc[pl.ds(pl.multiple_of(device * rows, 16), rows), :].astype(bf16)
        out[0, rows:, :columns] = jnp.zeros((out.shape[1] - rows, columns), bf16)
        out[0, rows:, : extra.shape[2]] = extra[device]


def outer(f, lefts, rights, extra, rows, name):
    width, tokens = lefts[0].shape
    height, columns = 4 * rows, rights[0].shape[1]
    shape = (1, rows + extra.shape[1], -(-columns // LANES) * LANES)
    full = lambda *shape: pl.BlockSpec(shape, lambda i, f: (0,) * len(shape))
    return pl.pallas_call(
        functools.partial(outer_kernel, rows=rows),
        grid_spec=pltpu.PrefetchScalarGridSpec(
            num_scalar_prefetch=1,
            grid=(1,),
            in_specs=[full(height, tokens)] * 2 + [full(tokens, columns)] * 2 + [full(*extra.shape)],
            out_specs=[full(*shape)] * 4,
            scratch_shapes=[pltpu.VMEM((height, columns), f32)],
        ),
        out_shape=[jax.ShapeDtypeStruct(shape, bf16)] * 4,
        compiler_params=params(28),
        cost_estimate=cost(4e10, 1e6),
        name=name,
    )(f, *lefts, *rights, extra)


def unpack_kernel(total, key_t, value_t, query):
    rows = query.shape[0]
    width = 2 * KV_HEADS * HEAD
    turned = total[:rows, :width].astype(f32).T
    for g in range(KV_HEADS):
        key_t[g * HEAD : (g + 1) * HEAD, :] = turned[2 * g * HEAD : (2 * g + 1) * HEAD, :]
        value_t[g * HEAD : (g + 1) * HEAD, :] = turned[(2 * g + 1) * HEAD : (2 * g + 2) * HEAD, :]
    query[...] = total[:rows, width : width + HEADS * HEAD].astype(f32)


def unpack(total, rows):
    full = lambda *shape: pl.BlockSpec(shape, lambda i: (0, 0))
    like = jax.ShapeDtypeStruct
    side = (KV_HEADS * HEAD, rows)
    key_t, value_t, query = pl.pallas_call(
        unpack_kernel,
        grid=(1,),
        in_specs=[full(*total.shape)],
        out_specs=[full(*side), full(*side), full(rows, HEADS * HEAD)],
        out_shape=[like(side, f32), like(side, f32), like((rows, HEADS * HEAD), f32)],
        compiler_params=params(16),
        cost_estimate=cost(4e10, 1e6),
        name="unpack",
    )(total)
    return key_t.T, value_t.T, query


def flip(array, axis, bit):
    size = lax.axis_size(axis)
    return lax.ppermute(array, axis, [(i, i ^ bit) for i in range(size)])


def add(left, right):
    return left.astype(f32) + right.astype(f32)


def levels_of(size):
    return [(bit, 2) for bit in range(size.bit_length() - 1)]


def cut(array, count):
    blocks, rows, columns = array.shape
    outer = next(n for n in (4, 2, 1) if n <= count and blocks % n == 0)
    inner = count // outer
    array = array.reshape(outer, blocks // outer, inner, rows // inner, columns)
    return [array[i // inner, :, i % inner] for i in range(count)]


def glue(parts, shape):
    count = len(parts)
    outer = next(n for n in (4, 2, 1) if n <= count and shape[0] % n == 0)
    inner = count // outer
    rows = [jnp.concatenate(parts[i * inner : (i + 1) * inner], axis=1) for i in range(outer)]
    return jnp.concatenate(rows, axis=0).reshape(shape)


def pick(parts, index):
    while len(parts) > 1:
        odd = index % 2 == 1
        parts = [jnp.where(odd, parts[i + 1], parts[i]) for i in range(0, len(parts), 2)]
        index = index // 2
    return parts[0]


def reduction(own, near, far, last, halves):
    shape = own.shape
    if last is None:
        beside, first = yield [(near, "fsdp", 1), (far, "fsdp", 2)]
        crossed = [first]
    else:
        came, beside = yield [(last, "fsdp", 1), (near, "fsdp", 1)]
        crossed = []
        for ours, theirs in zip(cut(far, halves), cut(came, halves)):
            crossed += yield [(add(ours, theirs).astype(bf16), "fsdp", 2)]
    crossed = glue(crossed, shape) if halves > 1 else crossed[0]
    part = add(own, beside) + crossed.astype(f32)
    index = lax.axis_index("dp")
    shapes = []
    for bit, count in levels_of(lax.axis_size("dp")):
        shapes.append(part.shape)
        parts = cut(part, count)
        mine = (index >> bit) % count
        came = yield [(pick(parts, mine ^ j).astype(bf16), "dp", j << bit) for j in range(1, count)]
        part = pick(parts, mine).astype(f32)
        for other in came:
            part = part + other.astype(f32)
    part = part.astype(bf16)
    for (bit, count), wide in zip(reversed(levels_of(lax.axis_size("dp"))), reversed(shapes)):
        came = yield [(part, "dp", j << bit) for j in range(1, count)]
        mine = (index >> bit) % count
        held = [part] + came
        part = glue([pick(held, mine ^ p) for p in range(count)], wide)
    return part


class Unit:
    def __init__(self, own, near, far, last, halves=1):
        self.steps = reduction(own, near, far, last, halves)
        self.asks = next(self.steps)
        self.total = None

    def take(self, came):
        try:
            self.asks = self.steps.send(came)
        except StopIteration as end:
            self.asks, self.total = [], end.value


class Clock:
    def __init__(self, f):
        self.f = f
        self.before = []

    def phase(self, moves=(), work=None, units=(), extra=()):
        asks = list(moves)
        for unit in units:
            asks += unit.asks
        gated = lax.optimization_barrier((self.f, *(a[0] for a in asks), *extra, *self.before))
        came = [flip(g, axis, bit) for g, (_, axis, bit) in zip(gated[1:], asks)]
        done = None if work is None else work(gated[0])
        self.before = list(came) + ([] if done is None else [jax.tree.leaves(done)[0]])
        at = len(moves)
        for unit in units:
            count = len(unit.asks)
            unit.take(came[at : at + count])
            at += count
        return came[: len(moves)], done


def half_for(shard, low_first, dim):
    width = shard.shape[dim] // 2
    low = lax.slice_in_dim(shard, 0, width, axis=dim)
    high = lax.slice_in_dim(shard, width, 2 * width, axis=dim)
    return jnp.where(low_first, low, high)


def per_device(
    tokens, seq_cuts, w_query, w_key, w_value, w_output, w_gate, w_up, w_down, gain_attn, gain_ffn, cotangent
):
    rows, width = tokens.shape[1], tokens.shape[2]
    half = rows // 2
    index = lax.axis_index("fsdp")
    replica = lax.axis_index("dp")
    f = jnp.stack([index, replica % 2, replica // 2 % 2]).astype(jnp.int32)
    count = rows * lax.axis_size("fsdp")
    shard_rows = w_key.shape[0]
    core, y = ("fsdp", 1), ("fsdp", 2)
    side = (("dp", 1), ("dp", 2))

    bounds = seq_cuts[0]
    within = jnp.arange(half, dtype=jnp.int32)
    local = jnp.concatenate([2 * index * half + within, (7 - 2 * index) * half + within]).astype(jnp.int32)
    every = jnp.arange(count, dtype=jnp.int32)
    passed = local[:, None] >= bounds[None, :]
    docs = jnp.sum(passed.astype(jnp.int32), axis=1)
    positions = local - jnp.max(jnp.where(passed, bounds[None, :], 0), axis=1)
    key_docs = jnp.sum((every[:, None] >= bounds[None, :]).astype(jnp.int32), axis=1)
    lane = jnp.arange(LANES, dtype=jnp.int32)[None, :]
    one = ((lane == key_docs[:, None]) & (lane < 4)) | ((lane >= 8) & (lane < 11))
    key_marks = one.astype(bf16)
    q_marks = jnp.where((lane < 4) & (lane != docs[:, None]), NEGATIVE, 0.0).astype(bf16)
    frequency = jnp.power(10000.0, -2.0 * jnp.arange(HEAD // 2, dtype=f32) / HEAD)
    angle = positions.astype(f32)[:, None] * frequency[None, :]
    cosine, sine = jnp.cos(angle), jnp.sin(angle)
    cos = jnp.concatenate([cosine] * 4, axis=1)
    sin = jnp.concatenate([-sine, sine] * 2, axis=1)
    gain_a, gain_f = gain_attn[None, :], gain_ffn[None, :]

    clock = Clock(f)
    tokens_t, cotangent_t, down_t = tokens[0].T, cotangent[0].T, w_down.T
    shards = {"gate": w_gate, "up": w_up, "down": down_t}
    bit_of, dim_of = {"gate": 0, "up": 1, "down": 0}, {"gate": 1, "up": 1, "down": 0}
    across = lambda name: (half_for(shards[name], f[1 + bit_of[name]] == 0, dim_of[name]), *y)

    w_own = pack(w_key, w_value, w_query)
    (w_far, w_near, other_tokens), _ = clock.phase([(w_own, *y), (w_own, *core), (tokens_t[:, half:], "fsdp", 3)])
    (w_last, gate_far), (h0, _) = clock.phase(
        [(w_far, *core), across("gate")], lambda turn: join(tokens_t, other_tokens), extra=(key_marks, q_marks, cos, sin)
    )
    w_in = (w_own, w_near, w_far, w_last)

    def attend_phases(hidden, first, moves):
        came = []
        got, (normed_t, q, *parts) = clock.phase(first, lambda turn: project(turn, hidden, gain_a, cos, sin, w_in))
        came.append(got)
        a, b, c = parts
        got, _ = clock.phase([(a, *y), (a, *core), (b, *core)] + moves[0](came))
        a_far, a_near, b_near = got[:3]
        came.append(got[3:])
        got, _ = clock.phase([(a_far, *core), (b, *y), (c, *core)] + moves[1](came))
        a_last, b_far, c_near = got[:3]
        came.append(got[3:])
        gathered = [(a, a_near, a_far, a_last)]
        attended, marks = [], []

        def call(k):
            return lambda turn: attend(turn, q, q_marks, key_marks, gathered[k], GROUPS[k])

        got, (x, m) = clock.phase([(b_far, *core), (c, *y)] + moves[2](came), call(0))
        attended.append(x), marks.append(m)
        b_last, c_far = got[:2]
        came.append(got[2:])
        gathered.append((b, b_near, b_far, b_last))
        got, (x, m) = clock.phase([(c_far, *core)] + moves[3](came), call(1))
        attended.append(x), marks.append(m)
        came.append(got[1:])
        gathered.append((c, c_near, c_far, got[0]))
        got, (x, m) = clock.phase(moves[4](came), call(2))
        attended.append(x), marks.append(m)
        came.append(got)
        return (normed_t, q, gathered, attended, marks), came

    def feed_phase(hidden, weights, run, result_type, moves=()):
        normed_t, q, gathered, attended, marks = run
        got, (after, attended_t, normed_ffn_t, gate_act, up_act, hidden_act, result) = clock.phase(
            moves, lambda turn: feed(turn, hidden, attended, gain_f, *weights, result_type)
        )
        return result, got, (
            hidden, normed_t, q, gathered, attended, marks, after, attended_t, normed_ffn_t, gate_act, up_act, hidden_act,
        )

    none = lambda came: []
    run, came = attend_phases(
        h0,
        [across("up"), (gate_far, *side[0])],
        (
            lambda came: [(w_output, *core), (w_gate, *core)],
            lambda came: [across("down"), (came[0][0], *side[1])],
            lambda came: [(w_output, *y), (came[2][0], *side[0]), (w_up, *core)],
            lambda came: [(gate_far, *core), (came[0][1], *core), (came[0][0], *core), (came[2][1], *core)],
            lambda came: [(came[2][0], *core), (came[3][1], *core), (down_t, *core), (came[3][0], *core)],
        ),
    )
    up_far, gate_other = came[0]
    down_far, up_other = came[2]
    o_near, gate_near = came[1]
    o_far, down_other, up_near = came[3]
    gate_last, gate_other_last, up_last, up_other_last = came[4]
    down_last, down_other_last, down_near, o_last = came[5]
    weights = (
        (w_output, o_near, o_far, o_last),
        (w_gate, gate_near, gate_far, gate_other, gate_last, gate_other_last),
        (w_up, up_near, up_far, up_other, up_last, up_other_last),
        (down_t, down_near, down_far, down_other, down_last, down_other_last),
    )
    h1, (other_cotangent,), first = feed_phase(h0, weights, run, f32, [(cotangent_t[:, half:], "fsdp", 3)])
    run, _ = attend_phases(h1, [], (none,) * 5)
    cot, cot_turned = join(cotangent_t, other_cotangent)
    _, turn_out = clock.phase((), lambda turn: feed_turn(turn, h1, cot, run[3], gain_f, *weights))
    attended_t, normed_ffn_t, hidden_act, grad_gate, grad_up, h2, *rest = turn_out
    second = (h1, run[0], run[1], run[2], run[3], run[4], None, attended_t, normed_ffn_t, None, None, hidden_act)
    fed2 = (grad_gate, grad_up, *rest)

    def feed_back_work(g, stored):
        return lambda turn: feed_back(turn, g, stored[6], gain_f, stored[9], stored[10], *weights)

    BACK = (1, 2, 0)

    def back_phases(grad_attended, stored, beside):
        q, gathered, attended, marks = stored[2], stored[3], stored[4], stored[5]
        grad_q, kept, far = [None] * PARTS, [None] * PARTS, [None] * PARTS
        extra = []

        def call(k):
            return lambda turn: attend_back(
                turn, q, marks[k], key_marks, gathered[k], grad_attended[k], attended[k], cos, sin, GROUPS[k]
            )

        def sums(k, keep, near):
            kept[k] = add(keep[0], near[0]).astype(bf16)
            return add(keep[1], near[1]).astype(bf16)

        b, c, a = BACK
        moves, units = beside(0)
        got, (grad_q[b], b_keep, b_send) = clock.phase(moves, call(b), units)
        extra += got
        moves, units = beside(1)
        got, (grad_q[c], c_keep, c_send) = clock.phase([(b_send, *core)] + moves, call(c), units)
        extra += got[1:]
        b_sum = sums(b, b_keep, got[0])
        moves, units = beside(2)
        got, (grad_q[a], a_keep, a_send) = clock.phase([(b_sum, *y), (c_send, *core)] + moves, call(a), units)
        far[b] = got[0]
        extra += got[2:]
        c_sum = sums(c, c_keep, got[1])
        moves, units = beside(3)
        got, _ = clock.phase([(c_sum, *y), (a_send, *core)] + moves, None, units)
        far[c] = got[0]
        extra += got[2:]
        a_sum = sums(a, a_keep, got[1])
        moves, units = beside(4)
        got, _ = clock.phase([(a_sum, *y)] + moves, None, units)
        far[a] = got[0]
        extra += got[1:]
        return (grad_q, kept, far), extra

    def project_back_work(parts, stored, grad_after, result_type):
        return lambda turn: project_back(
            turn, *parts, cos, sin, stored[0], gain_a, grad_after, w_in, result_type
        )

    out_first, out_second = part(f, h2)
    parts, extra = back_phases(
        fed2[4 : 4 + PARTS], second, lambda k: ([(out_second, "fsdp", 3)] if k == 0 else [], ())
    )
    output = jnp.concatenate([out_first, extra[0]], axis=1).T
    _, (grads2, middle, middle_turned, gain_a2) = clock.phase((), project_back_work(parts, second, fed2[2], f32))

    def down_work(chip, name):
        return lambda turn: outer_down(turn, (middle_turned, cot_turned), (first[11], second[11]), chip, name)

    _, far_pair = clock.phase((), down_work(1, "outer_down_far"))
    (far_beside,), own_pair = clock.phase([(far_pair[1], *core)], down_work(0, "outer_down_own"))
    down = Unit(*own_pair, add(far_pair[0], far_beside).astype(bf16), None)
    _, fed1 = clock.phase((), feed_back_work(middle, first), (down,))

    def outer_work(i, name):
        return lambda turn: outer_tiles(turn, (first[8], second[8]), (fed1[i], fed2[i]), shard_rows, name)

    nothing = jnp.zeros((4, 16, LANES), bf16)
    _, gate_parts = clock.phase((), outer_work(0, "outer_gate"))
    gate = Unit(*gate_parts, 2)
    _, (up_parts, o_parts) = clock.phase(
        (),
        lambda turn: (
            outer_work(1, "outer_up")(turn),
            outer(turn, (first[7], second[7]), (fed1[3], fed2[3]), nothing, shard_rows, "outer_o"),
        ),
        (down, gate),
    )
    up, out = Unit(*up_parts, 2), Unit(*o_parts)
    plan = ((gate, up, down, out), (gate, down), (up, gate, down), (gate,), ())
    parts, _ = back_phases(fed1[4 : 4 + PARTS], first, lambda k: ([], plan[k]))
    _, (grads1, grad_tokens, _, gain_a1) = clock.phase(
        (), project_back_work(parts, first, fed1[2], bf16), (up, gate, down)
    )
    gains = jnp.concatenate([gain_a1 + gain_a2, fed1[4 + PARTS] + fed2[4 + PARTS]], axis=0)
    gains = gains.reshape(2, 4, width // 4).transpose(1, 0, 2).astype(bf16)
    gains = jnp.pad(gains, ((0, 0), (0, 14), (0, 256 - width // 4)))
    _, in_parts = clock.phase(
        (),
        lambda turn: outer(turn, (first[1], second[1]), (grads1, grads2), gains, shard_rows, "outer_in"),
        (out, up, gate),
    )
    into = Unit(*in_parts)
    clock.phase((), None, (into, up, out))
    _, (back_half, back_send) = clock.phase((), lambda turn: part(turn, grad_tokens), (into, up, gate, down, out))
    clock.phase((), None, (into, up, out))
    clock.phase((), None, (into, up, gate, out))
    (other_tokens,), _ = clock.phase([(back_send, "fsdp", 3)], None, (into, up, out))
    grad_tokens = jnp.concatenate([back_half, other_tokens], axis=1).T
    units = (into, up, out, gate, down)
    while any(unit.asks for unit in units):
        clock.phase((), None, [unit for unit in units if unit.asks])

    grad_down = down.total[0].T.astype(f32)
    wide = lambda unit: jnp.concatenate([unit.total[i] for i in range(4)], axis=1).astype(f32)
    grad_gate, grad_up = wide(gate), wide(up)
    grad_o = out.total[0, :shard_rows, :width].astype(f32)
    total = into.total[0]
    grad_key, grad_value, grad_query = unpack(total, shard_rows)
    gains = total[shard_rows : shard_rows + 2, : width // 4].astype(f32)
    return (
        output[None], grad_tokens[None], grad_query, grad_key, grad_value, grad_o, grad_gate, grad_up,
        grad_down, gains[0], gains[1],
    )


def solution(mesh):
    split, whole = P("fsdp", None), P("dp", "fsdp", None)
    return jax.shard_map(
        per_device,
        mesh=mesh,
        in_specs=(whole, P("dp", None)) + (split,) * 7 + (P(), P(), whole),
        out_specs=(whole, whole) + (split,) * 7 + (P("fsdp"), P("fsdp")),
        check_vma=False,
    )
```
